32 devices in a mesh: box: 16 (over z, y, x), samp: 2 (over core).
Axes of the slice: x: 2, y: 2, z: 4, core: 2. Of those that a mesh axis runs over, the one named last changes fastest.
Arguments:
- child_pattern: bfloat16 [2, 2, 512, 2048], P(None, 'samp', None, 'box'), may hold values from -6 to 6
- child_parent: int32 [2048], P('box'), may hold values from 0 to 511, as said below
- child_octant: int32 [2048], P('box'), may hold values from 0 to 7, as said below
- child_sources: int32 [2048, 8], P('box'), may hold values from 0 to 2047, as said below
- child_offsets: int32 [2048, 8], P('box'), may hold values from 0 to 315
- child_counts: int32 [2048], P('box'), may hold values from 1 to 8, as said below
- parent_sources: int32 [512, 8], replicated, may hold values from 0 to 511
- parent_offsets: int32 [512, 8], replicated, may hold values from 0 to 315
- parent_counts: int32 [512], replicated, may hold values from 1 to 8, as said below
- interp_weights: bfloat16 [640, 2048], replicated, may hold values from -0.25 to 0.25
- shift_phase: float32 [8, 2, 2048], P(None, 'samp'), may hold values from -3.140625 to 3.140625
- child_table: bfloat16 [2, 316, 2, 512], P(None, None, 'samp'), may hold values from -4 to 4
- parent_table: bfloat16 [2, 316, 2, 2048], P(None, None, 'samp', 'box'), may hold values from -1.25 to 1.25
Outputs:
- child_field: bfloat16 [2, 2, 512, 2048], P(None, 'samp', None, 'box')
The draws below stay inside these ranges and needn't reach their ends.
Inputs may be any that keep to these rules, and one draw needn't show every extreme that they name: `child_parent`: child boxes on one index d of box have their parents among the boxes d * 32 to d * 32 + 31; children of one parent stand next to each other, parents in rising order; every parent has 2 to 8 children, and each index has parents with 8 and with 2. `child_octant`: children of one parent have different octants. `child_sources`: an entry of a child box's list names a child box of the same index of box, one of the last 32 boxes of the index before it, or one of the first 32 boxes of the index after it. Entries of child_sources and child_offsets at positions child_counts[c] and beyond are unused; on every index of box some child list is full. Entries of parent_sources and parent_offsets at positions parent_counts[p] and beyond are unused; some parent list is full.
All inputs are finite; a program needn't handle non-finite values.
Results may differ from the reference program's by a relative error of at most 0.0061.
Values may be sent and summed in bfloat16 or wider, within the bound.
No kernel may reach another device: no remote copies, remote signals or barrier semaphores. Data moves between devices by JAX's collectives and lax.ppermute only.
A program may use at most 128 MiB of HBM per device.

```python
import jax
import jax.numpy as jnp
from jax import lax

CHILD_DEV = 128
PAR_DEV = 32
KCG = 512
KPG = 2048
RIM = 64
NOFF = 316
MC = 8
MP = 8
NEARB = 32
NG = 2
NBC = 2048
NBP = 512


def octree_links(key):
    base = jax.random.fold_in(key, 7)
    first_key, second_key = jax.random.split(base)
    devices = NBC // CHILD_DEV
    orders = jax.vmap(lambda device_key: jax.random.permutation(device_key, PAR_DEV))(jax.random.split(first_key, devices))
    pattern = jnp.array([8, 2, 4, 2], dtype=jnp.int32)[jnp.arange(PAR_DEV) % 4]
    inverse = jnp.argsort(orders, axis=1)
    family = pattern[inverse]
    ends = jnp.cumsum(family, axis=1)
    slots = jnp.arange(CHILD_DEV, dtype=jnp.int32)
    local_parent = jnp.sum((ends[:, None, :] <= slots[None, :, None]).astype(jnp.int32), axis=2)
    starts = ends - family
    ranks = slots[None, :] - jnp.take_along_axis(starts, local_parent, axis=1)
    parents = local_parent + jnp.arange(devices, dtype=jnp.int32)[:, None] * PAR_DEV
    scores = jax.random.randint(second_key, (devices * PAR_DEV, 8), 0, 1 << 20) * 8 + jnp.arange(8, dtype=jnp.int32)[None, :]
    octants = jnp.argsort(scores, axis=1).astype(jnp.int32)
    child_octants = octants[parents.reshape(-1), ranks.reshape(-1)]
    return (parents.reshape(-1).astype(jnp.int32), child_octants.astype(jnp.int32))


def draw_child_parent(key, part):
    return octree_links(key)[0]


def draw_child_octant(key, part):
    return octree_links(key)[1]


def draw_child_sources(key, part):
    devices = NBC // CHILD_DEV
    keys = jax.random.split(jax.random.fold_in(key, 13), 3)
    region = jax.random.randint(keys[0], (NBC, MC), 0, 4)
    device_of = (jnp.arange(NBC, dtype=jnp.int32) // CHILD_DEV)[:, None]
    own_box = device_of * CHILD_DEV + jax.random.randint(keys[1], (NBC, MC), 0, CHILD_DEV)
    rim_pick = jax.random.randint(keys[2], (NBC, MC), 0, NEARB)
    left_box = (device_of - 1) * CHILD_DEV + CHILD_DEV - NEARB + rim_pick
    right_box = (device_of + 1) * CHILD_DEV + rim_pick
    use_left = (region == 2) & (device_of > 0)
    use_right = (region == 3) & (device_of < devices - 1)
    chosen = jnp.where(use_left, left_box, jnp.where(use_right, right_box, own_box)).astype(jnp.int32)
    chosen = chosen.at[0, 0].set(0)
    return chosen.at[NBC - 1, 0].set(NBC - 1)


def ragged_counts(key, total, longest, groups):
    keys = jax.random.split(key, 2)
    width_each = total // groups
    counts = jax.random.randint(keys[0], (groups, width_each), 1, longest + 1)
    spot = jax.random.randint(keys[1], (groups, 1), 0, width_each)
    filled = jnp.where(jnp.arange(width_each)[None, :] == spot, longest, counts)
    return filled.reshape(-1).astype(jnp.int32)


def draw_child_counts(key, part):
    return ragged_counts(jax.random.fold_in(key, 17), NBC, MC, NBC // CHILD_DEV)


def draw_parent_counts(key, part):
    return ragged_counts(jax.random.fold_in(key, 19), NBP, MP, 1)


def with_ends(values, own_key, low, high):
    extent = values.shape
    spot = [jax.random.randint(jax.random.fold_in(own_key, axis), (), 0, extent[axis]) for axis in range(len(extent))]
    values = values.at[tuple(spot)].set(low)
    longest = extent.index(max(extent))
    spot[longest] = (spot[longest] + 1) % extent[longest]
    return values.at[tuple(spot)].set(high)


def level_of(key, dims, pieces, low, top_value):
    gain = 1.0
    for position, shards_of in pieces:
        steps = jax.random.uniform(jax.random.fold_in(jax.random.fold_in(key, 6), position), (shards_of,), jnp.float32, low / len(pieces), top_value / len(pieces))
        gain = gain * jnp.repeat(jnp.exp(steps), dims[position] // shards_of).reshape((-1,) + (1,) * (len(dims) - 1 - position))
    return gain


def bell_draw(rng, shape, scale, bound, shards=(), kind=jnp.bfloat16):
    factor_of = level_of(rng, shape, shards, -0.22, 0.18) if shards else 1.0
    values = jax.random.normal(rng, shape, jnp.float32) * scale * factor_of
    return jnp.minimum(jnp.maximum(values, -bound), bound).astype(kind)


def setup_inputs(seed: int = 0) -> dict:
    seeds = jax.random.split(jax.random.key(seed), 14)
    return {
        "child_pattern": bell_draw(seeds[0], (2, NG, KCG, NBC), 1.0, 6.0, ((1, 2), (3, 16))),
        "child_parent": draw_child_parent(jax.random.fold_in(seeds[13], 71), 0),
        "child_octant": draw_child_octant(jax.random.fold_in(seeds[13], 71), 0),
        "child_sources": draw_child_sources(jax.random.fold_in(seeds[13], 71), 0),
        "child_offsets": with_ends(jax.random.randint(seeds[4], (NBC, MC), 0, NOFF), jax.random.fold_in(seeds[4], 1), 0, NOFF - 1).astype(jnp.int32),
        "child_counts": draw_child_counts(jax.random.fold_in(seeds[13], 71), 0),
        "parent_sources": with_ends(jax.random.randint(seeds[6], (NBP, MP), 0, NBP), jax.random.fold_in(seeds[6], 1), 0, NBP - 1).astype(jnp.int32),
        "parent_offsets": with_ends(jax.random.randint(seeds[7], (NBP, MP), 0, NOFF), jax.random.fold_in(seeds[7], 1), 0, NOFF - 1).astype(jnp.int32),
        "parent_counts": draw_parent_counts(jax.random.fold_in(seeds[13], 71), 0),
        "interp_weights": bell_draw(seeds[9], (KCG + 2 * RIM, KPG), (KCG + 2 * RIM) ** -0.5, 0.25),
        "shift_phase": jnp.clip(jax.random.uniform(seeds[10], (8, NG, KPG), jnp.float32, -3.140625, 3.140625), -3.140625, 3.140625),
        "child_table": bell_draw(seeds[11], (2, NOFF, NG, KCG), 0.25, 4.0, ((2, 2),)),
        "parent_table": bell_draw(seeds[12], (2, NOFF, NG, KPG), 0.08, 1.25, ((2, 2), (3, 16))),
    }


def complex_terms(coefficient, picked):
    return jnp.stack([coefficient[0] * picked[0] - coefficient[1] * picked[1], coefficient[0] * picked[1] + coefficient[1] * picked[0]])


def list_sum(pattern, table, sources, offsets, counts, slots):
    box_total = sources.shape[0]
    sample_count = pattern.shape[1]

    def advance(step_index, summed):
        picked = pattern[:, :, sources[:, step_index]].astype(jnp.float32)
        coefficient = jnp.transpose(table[:, offsets[:, step_index], :], (0, 2, 1)).astype(jnp.float32)
        alive = (step_index < counts)[None, None, :]
        return summed + jnp.where(alive, complex_terms(coefficient, picked), 0.0)

    return lax.fori_loop(0, slots, advance, jnp.zeros((2, sample_count, box_total), jnp.float32))


def reference(child_pattern, child_parent, child_octant, child_sources, child_offsets, child_counts, parent_sources, parent_offsets, parent_counts, interp_weights, shift_phase, child_table, parent_table):
    highest = lax.Precision.HIGHEST
    weights = interp_weights.astype(jnp.float32)
    flat_pattern = child_pattern.reshape(2, NG * KCG, NBC)
    groups = jnp.arange(NG, dtype=jnp.int32)

    def phases(group):
        angles = jnp.take(shift_phase, group, axis=1)
        return jnp.cos(angles)[child_octant].T, jnp.sin(angles)[child_octant].T

    def aggregate(group):
        positions = (group * KCG - RIM + jnp.arange(KCG + 2 * RIM, dtype=jnp.int32)) % (NG * KCG)
        extended = jnp.take(flat_pattern, positions.astype(jnp.int32), axis=1).astype(jnp.float32)
        interp = jnp.einsum("jk,rjc->rkc", weights, extended, precision=highest)
        cosine, sine_part = phases(group)
        shifted = jnp.stack([interp[0] * cosine - interp[1] * sine_part, interp[0] * sine_part + interp[1] * cosine])
        summed = jax.ops.segment_sum(jnp.transpose(shifted, (2, 0, 1)), child_parent, num_segments=NBP)
        return jnp.transpose(summed, (1, 2, 0)).astype(jnp.bfloat16)

    parent_pattern = lax.map(aggregate, groups)

    def parent_translate(group):
        table = jnp.take(parent_table, group, axis=2)
        return list_sum(parent_pattern[group], table, parent_sources, parent_offsets, parent_counts, MP).astype(jnp.bfloat16)

    parent_far = lax.map(parent_translate, groups)

    def disaggregate(group):
        field = parent_far[group][:, :, child_parent].astype(jnp.float32)
        cosine, sine_part = phases(group)
        lowered = jnp.stack([field[0] * cosine + field[1] * sine_part, field[1] * cosine - field[0] * sine_part]).astype(jnp.bfloat16)
        lowered = lax.optimization_barrier(lowered).astype(jnp.float32)
        return jnp.einsum("jk,rkc->rjc", weights, lowered, precision=highest).astype(jnp.bfloat16)

    child_terms = lax.map(disaggregate, groups)

    def finish(group):
        table = jnp.take(child_table, group, axis=2)
        pattern = jnp.take(child_pattern, group, axis=1)
        nearby = list_sum(pattern, table, child_sources, child_offsets, child_counts, MC)
        own_terms = child_terms[group].astype(jnp.float32)
        before = child_terms[(group - 1) % NG].astype(jnp.float32)
        after = child_terms[(group + 1) % NG].astype(jnp.float32)
        incoming = own_terms[:, RIM:RIM + KCG]
        incoming = incoming.at[:, :RIM].add(before[:, KCG + RIM:])
        incoming = incoming.at[:, KCG - RIM:].add(after[:, :RIM])
        return (nearby + incoming).astype(jnp.bfloat16)

    result = lax.map(finish, groups)
    return jnp.transpose(result, (1, 0, 2, 3))
```

```python
import jax
import jax.numpy as jnp
from jax import lax
from jax.experimental import pallas as pl
from jax.experimental.pallas import tpu as pltpu
from jax.sharding import PartitionSpec as P

NEARB = 32
OCTANTS = 8
LANES = 128
f32, bf16, i32 = jnp.float32, jnp.bfloat16, jnp.int32
VMEM = pl.BlockSpec(memory_space=pltpu.VMEM)


def call(body, outs, name, scratch=(), flops=1 << 20, moved=1 << 20, limit=24 << 20):
    def run(*args):
        return pl.pallas_call(
            body,
            out_shape=outs,
            in_specs=[VMEM] * len(args),
            out_specs=[VMEM] * len(outs) if isinstance(outs, list) else VMEM,
            scratch_shapes=list(scratch),
            name=name,
            cost_estimate=pl.CostEstimate(flops=flops, bytes_accessed=moved, transcendentals=0),
            compiler_params=pltpu.CompilerParams(vmem_limit_bytes=limit),
        )(*args)

    return run


def nt(a, b):
    return lax.dot_general(a, b, (((1,), (1,)), ((), ())), preferred_element_type=f32)


def tn(a, b, precision=None):
    return lax.dot_general(
        a, b, (((0,), (0,)), ((), ())), preferred_element_type=f32, precision=precision
    )


def nn(a, b):
    return lax.dot_general(a, b, (((1,), (0,)), ((), ())), preferred_element_type=f32)


def sincos(x):
    h = 0.5 * x
    q = h * h
    s = -2.50521083854417e-08 + q * 1.60590438368216e-10
    s = 2.75573192239859e-06 + q * s
    s = -1.98412698412698e-04 + q * s
    s = 8.33333333333333e-03 + q * s
    s = -1.66666666666667e-01 + q * s
    s = h + h * (q * s)
    c = 2.08767569878681e-09 + q * -1.14707455977297e-11
    c = -2.75573192239859e-07 + q * c
    c = 2.48015873015873e-05 + q * c
    c = -1.38888888888889e-03 + q * c
    c = 4.16666666666667e-02 + q * c
    c = -0.5 + q * c
    c = 1.0 + q * c
    return 2.0 * (s * c), 1.0 - 2.0 * (s * s)


def iota(shape, dim):
    return lax.broadcasted_iota(i32, shape, dim)


def slot_onehot(parent_ref, octant_ref, parents):
    base = lax.axis_index("box") * parents
    slot = octant_ref[...] * parents + (parent_ref[...] - base)
    shape = (OCTANTS * parents, slot.shape[1])
    return jnp.where(iota(shape, 0) == slot, 1.0, 0.0).astype(bf16)


def weighted(y, cosine, sine, begin, width, parents):
    slots = OCTANTS * parents
    real = imag = None
    for o in range(OCTANTS):
        yr = y[o * parents : (o + 1) * parents]
        yi = y[slots + o * parents : slots + (o + 1) * parents]
        c = cosine[o : o + 1, pl.ds(begin, width)]
        s = sine[o : o + 1, pl.ds(begin, width)]
        tr, ti = yr * c - yi * s, yr * s + yi * c
        real, imag = (tr, ti) if o == 0 else (real + tr, imag + ti)
    return real, imag


def interior(own, parent, octant, phase, weights, parents):
    _, kcg, boxes = own.shape
    kpg = weights.shape[1]
    rim = (weights.shape[0] - kcg) // 2
    slots = OCTANTS * parents
    width = 256

    def body(own_ref, par_ref, oct_ref, ph_ref, w_ref, acc_ref, cos_ref, sin_ref, e_ref):
        onehot = slot_onehot(par_ref, oct_ref, parents)
        for r in range(2):
            e_ref[r * slots : (r + 1) * slots] = nt(onehot, own_ref[r]).astype(bf16)
        sin_ref[...], cos_ref[...] = sincos(ph_ref[:, 0, :])

        @pl.loop(0, kpg // width)
        def _(step):
            begin = pl.multiple_of(step * width, width)
            y = nn(e_ref[...], w_ref[rim : rim + kcg, pl.ds(begin, width)])
            real, imag = weighted(y, cos_ref, sin_ref, begin, width, parents)
            acc_ref[0, :, pl.ds(begin, width)] = real
            acc_ref[1, :, pl.ds(begin, width)] = imag

    return call(
        body,
        [
            jax.ShapeDtypeStruct((2, parents, kpg), f32),
            jax.ShapeDtypeStruct((OCTANTS, kpg), f32),
            jax.ShapeDtypeStruct((OCTANTS, kpg), f32),
        ],
        "interior",
        [pltpu.VMEM((2 * slots, kcg), bf16)],
        flops=2 * 2 * slots * kcg * kpg,
    )(own, parent, octant, phase, weights)


def with_rims(before, after, parent, octant, cosine, sine, weights, acc, parents, spans, packed):
    kpg = weights.shape[1]
    rows = weights.shape[0]
    rim = spans[0][1] - spans[0][0]
    slots = OCTANTS * parents
    width = 256
    arrays = [before] if after is None else [before, after]

    def body(*refs):
        rims = refs[: len(arrays)]
        par_ref, oct_ref, cos_ref, sin_ref, w_ref, acc_ref, out_ref, e_ref, wr_ref = refs[len(arrays) :]
        onehot = slot_onehot(par_ref, oct_ref, parents)
        for r in range(2):
            for side, (low, high) in enumerate(spans):
                picked = nt(onehot, rims[min(side, len(arrays) - 1)][r, low:high, :])
                e_ref[r * slots : (r + 1) * slots, side * rim : (side + 1) * rim] = picked.astype(bf16)
        wr_ref[:rim] = w_ref[:rim]
        wr_ref[rim:] = w_ref[rows - rim :]

        @pl.loop(0, kpg // width)
        def _(step):
            begin = pl.multiple_of(step * width, width)
            y = nn(e_ref[...], wr_ref[:, pl.ds(begin, width)])
            sums = weighted(y, cos_ref, sin_ref, begin, width, parents)
            for r in range(2):
                total = (acc_ref[r, :, pl.ds(begin, width)] + sums[r]).astype(bf16)
                if packed:
                    for part in range(width // LANES):
                        row = pl.multiple_of((step * (width // LANES) + part) * parents, parents)
                        out_ref[pl.ds(row, parents), r * LANES : (r + 1) * LANES] = total[
                            :, part * LANES : (part + 1) * LANES
                        ]
                else:
                    out_ref[r, :, pl.ds(begin, width)] = total

    shape = (kpg // LANES * parents, 2 * LANES) if packed else (2, parents, kpg)
    return call(
        body,
        jax.ShapeDtypeStruct(shape, bf16),
        "with_rims",
        [pltpu.VMEM((2 * slots, 2 * rim), bf16), pltpu.VMEM((2 * rim, kpg), bf16)],
        flops=2 * 2 * slots * 2 * rim * kpg,
    )(*arrays, parent, octant, cosine, sine, weights, acc)


CHUNK = 128


def list_tables(sources, offsets, counts, table):
    slots, boxes = sources.shape
    total = boxes
    operators, lanes = table.shape

    def body(src_ref, off_ref, cnt_ref, tab_ref, hot_ref, coef_ref):
        alive = iota((slots, boxes), 0) < cnt_ref[...]
        src = src_ref[...].T
        off = jnp.where(alive, off_ref[...], -1).T
        for chunk in range(boxes // CHUNK):
            rows = slice(chunk * CHUNK, (chunk + 1) * CHUNK)
            for m in range(slots):
                at = (chunk * slots + m) * CHUNK
                hot = src[rows, m : m + 1] == iota((CHUNK, total), 1)
                hot_ref[at : at + CHUNK] = jnp.where(hot, 1.0, 0.0).astype(bf16)
                pick = off[rows, m : m + 1] == iota((CHUNK, operators), 1)
                coef_ref[at : at + CHUNK] = nn(
                    jnp.where(pick, 1.0, 0.0).astype(bf16), tab_ref[...]
                ).astype(bf16)

    return call(
        body,
        [
            jax.ShapeDtypeStruct((slots * boxes, total), bf16),
            jax.ShapeDtypeStruct((slots * boxes, lanes), bf16),
        ],
        "list_tables",
        flops=2 * slots * boxes * operators * lanes * 4,
        moved=8 << 20,
        limit=32 << 20,
    )(sources, offsets, counts, table)


def parent_sums(pattern, hot, coef, slots):
    total, lanes = pattern.shape
    half = lanes // 2

    def body(pat_ref, hot_ref, coef_ref, out_ref):
        for chunk in range(total // CHUNK):
            at = chunk * slots * CHUNK
            picked = nn(hot_ref[at : at + slots * CHUNK], pat_ref[...])
            real = imag = 0.0
            for m in range(slots):
                rows = slice(m * CHUNK, (m + 1) * CHUNK)
                pr, pi = picked[rows, :half], picked[rows, half:]
                c = coef_ref[at + m * CHUNK : at + (m + 1) * CHUNK].astype(f32)
                cr, ci = c[:, :half], c[:, half:]
                real += cr * pr - ci * pi
                imag += cr * pi + ci * pr
            out_ref[chunk * CHUNK : (chunk + 1) * CHUNK, :half] = real.astype(bf16)
            out_ref[chunk * CHUNK : (chunk + 1) * CHUNK, half:] = imag.astype(bf16)

    return call(
        body,
        jax.ShapeDtypeStruct((total, lanes), bf16),
        "parent_sums",
        flops=2 * slots * total * total * lanes,
        moved=8 << 20,
        limit=32 << 20,
    )(pattern, hot, coef)


def child_phases(octant, cosine, sine):
    boxes = octant.shape[1]
    kpg = cosine.shape[1]

    def body(oct_ref, cos_ref, sin_ref, c_ref, s_ref):
        onehot = jnp.where(iota((OCTANTS, boxes), 0) == oct_ref[...], 1.0, 0.0)
        c_ref[...] = tn(onehot, cos_ref[...], lax.Precision.HIGHEST)
        s_ref[...] = tn(onehot, sin_ref[...], lax.Precision.HIGHEST)

    shape = jax.ShapeDtypeStruct((boxes, kpg), f32)
    return call(body, [shape, shape], "child_phases", flops=1 << 28)(octant, cosine, sine)


def lower(far, parent, cosine, sine, weights, parents, rim, packed):
    boxes, kpg = cosine.shape
    rows = weights.shape[0]
    width = LANES if packed else 256

    def body(far_ref, par_ref, cos_ref, sin_ref, w_ref, low_ref, rim_ref, acc_ref):
        base = lax.axis_index("box") * parents
        hot = jnp.where(iota((parents, boxes), 0) == par_ref[...] - base, 1.0, 0.0).astype(bf16)
        hot = hot.T
        for step in range(kpg // width):
            cols = slice(step * width, (step + 1) * width)
            if packed:
                spread = nn(hot, far_ref[step * parents : (step + 1) * parents])
                sr, si = spread[:, :LANES], spread[:, LANES:]
            else:
                sr, si = nn(hot, far_ref[0, :, cols]), nn(hot, far_ref[1, :, cols])
            c, s = cos_ref[:, cols], sin_ref[:, cols]
            low_ref[:boxes, cols] = (sr * c + si * s).astype(bf16)
            low_ref[boxes:, cols] = (si * c - sr * s).astype(bf16)
        first = nt(w_ref[:rim], low_ref[...]).astype(bf16)
        last = nt(w_ref[rows - rim :], low_ref[...]).astype(bf16)
        for side, terms in enumerate((first, last)):
            for r in range(2):
                rim_ref[side, r] = terms[:, r * boxes : (r + 1) * boxes]

    return call(
        body,
        [
            jax.ShapeDtypeStruct((2 * boxes, kpg), bf16),
            jax.ShapeDtypeStruct((2, 2, rim, boxes), bf16),
        ],
        "lower",
        [pltpu.VMEM((8, LANES), f32)],
        flops=2 * 2 * boxes * kpg * 2 * rim,
    )(far, parent, cosine, sine, weights)


def anterpolate(weights, lowered, nearby, rim):
    _, kcg, boxes = nearby.shape

    def body(w_ref, low_ref, near_ref, out_ref):
        terms = nt(w_ref[rim : rim + kcg], low_ref[...]).astype(bf16).astype(f32)
        for r in range(2):
            out_ref[r] = near_ref[r] + terms[:, r * boxes : (r + 1) * boxes]

    return call(
        body,
        jax.ShapeDtypeStruct(nearby.shape, f32),
        "anterpolate",
        flops=2 * kcg * weights.shape[1] * 2 * boxes,
    )(weights, lowered, nearby)


def finish(partial, start_terms, end_terms):
    _, kcg, boxes = partial.shape
    rim = start_terms.shape[1]

    def body(sum_ref, start_ref, end_ref, out_ref):
        out_ref[:, rim : kcg - rim] = sum_ref[:, rim : kcg - rim].astype(bf16)
        out_ref[:, :rim] = (sum_ref[:, :rim] + start_ref[...].astype(f32)).astype(bf16)
        out_ref[:, kcg - rim :] = (sum_ref[:, kcg - rim :] + end_ref[...].astype(f32)).astype(bf16)

    return call(body, jax.ShapeDtypeStruct(partial.shape, bf16), "finish")(partial, start_terms, end_terms)


def near_sums(own, before, after, sources, offsets, counts, table):
    _, kcg, boxes = own.shape
    slots = sources.shape[0]
    operators = table.shape[1]
    reach = boxes + 2 * NEARB
    depth = 2 * boxes
    pair = 2

    def body(own_ref, bef_ref, aft_ref, src_ref, off_ref, cnt_ref, tab_ref, out_ref, ext_ref, tt_ref, acc_ref):
        eye = jnp.where(iota((kcg, kcg), 0) == iota((kcg, kcg), 1), 1.0, 0.0).astype(bf16)
        for r in range(2):
            rows = slice(r * kcg, (r + 1) * kcg)
            ext_ref[rows, :boxes] = own_ref[r]
            halo = jnp.concatenate(
                [bef_ref[r], aft_ref[r], jnp.zeros((boxes - 2 * NEARB, kcg), bf16)], axis=0
            )
            ext_ref[rows, boxes:] = nt(eye, halo).astype(bf16)
            tt_ref[rows] = nt(eye, tab_ref[r]).astype(bf16)
        base = lax.axis_index("box") * boxes
        rel = src_ref[...] - base
        rel = jnp.where(rel < 0, rel + boxes + NEARB, jnp.where(rel >= boxes, rel + NEARB, rel))
        off = jnp.where(iota((slots, boxes), 0) < cnt_ref[...], off_ref[...], -1)
        for m in range(0, slots, pair):
            src = jnp.concatenate([rel[m + j : m + j + 1] for j in range(pair)], axis=1)
            ops = jnp.concatenate([off[m + j : m + j + 1] for j in range(pair)], axis=1)
            hot = jnp.where(iota((depth, pair * boxes), 0) == src, 1.0, 0.0).astype(bf16)
            pick = jnp.where(iota((operators, pair * boxes), 0) == ops, 1.0, 0.0).astype(bf16)
            picked = nn(ext_ref[...], hot)
            coef = nn(tt_ref[...], pick)
            pr, pi, cr, ci = picked[:kcg], picked[kcg:], coef[:kcg], coef[kcg:]
            real, imag = cr * pr - ci * pi, cr * pi + ci * pr
            for r, value in enumerate((real, imag)):
                value = sum(value[:, j * boxes : (j + 1) * boxes] for j in range(pair))
                out_ref[r] = value if m == 0 else out_ref[r] + value

    return call(
        body,
        jax.ShapeDtypeStruct(own.shape, f32),
        "near_sums",
        [
            pltpu.VMEM((2 * kcg, depth), bf16),
            pltpu.VMEM((2 * kcg, operators), bf16),
            pltpu.VMEM((8, LANES), f32),
        ],
        flops=2 * slots * boxes * 2 * kcg * (depth + operators),
        limit=32 << 20,
    )(own, before, after, sources, offsets, counts, table)


def plain_translate(pattern, table, sources, offsets, counts):
    coef = jnp.transpose(table, (0, 2, 1))

    def advance(m, summed):
        src = lax.dynamic_index_in_dim(sources, m, 0, keepdims=False)
        off = lax.dynamic_index_in_dim(offsets, m, 0, keepdims=False)
        p = pattern[:, :, src].astype(f32)
        c = coef[:, :, off].astype(f32) * (m < counts).astype(f32)
        return summed + jnp.stack([c[0] * p[0] - c[1] * p[1], c[0] * p[1] + c[1] * p[0]])

    return lax.fori_loop(
        0, sources.shape[0], advance, jnp.zeros(pattern.shape[:2] + (sources.shape[1],), f32)
    )


def shift(value, axis, step, wrap):
    peers = lax.axis_size(axis)
    pairs = [(i, (i + step) % peers) for i in range(peers) if wrap or 0 <= i + step < peers]
    return lax.ppermute(value, axis, pairs)


def local(
    child_pattern,
    child_parent,
    child_octant,
    child_sources,
    child_offsets,
    child_counts,
    parent_sources,
    parent_offsets,
    parent_counts,
    interp_weights,
    shift_phase,
    child_table,
    parent_table,
):
    own = child_pattern[:, 0]
    _, kcg, boxes = own.shape
    rim = (interp_weights.shape[0] - kcg) // 2
    peers, groups = lax.axis_size("box"), lax.axis_size("samp")
    total = parent_sources.shape[0]
    parents = total // peers
    kpg = interp_weights.shape[1]
    mine = kpg // peers
    packed = mine == LANES and total % CHUNK == 0
    parent, octant = child_parent[None, :], child_octant[None, :]

    if groups == 2:
        before, after = shift(own, "samp", 1, True), None
        spans = ((kcg - rim, kcg), (0, rim))
    else:
        before = shift(own[:, kcg - rim :], "samp", 1, True)
        after = shift(own[:, :rim], "samp", -1, True)
        spans = ((0, rim), (0, rim))
    acc, cosine, sine = interior(own, parent, octant, shift_phase, interp_weights, parents)
    pattern = with_rims(
        before, after, parent, octant, cosine, sine, interp_weights, acc, parents, spans, packed
    )

    edge = jnp.transpose(own, (0, 2, 1))
    near_before = shift(edge[:, boxes - NEARB :], "box", 1, False)
    near_after = shift(edge[:, :NEARB], "box", -1, False)

    table = parent_table[:, :, 0, :]
    if packed:
        regrouped = lax.all_to_all(pattern, "box", split_axis=0, concat_axis=0, tiled=True)
        flat_table = jnp.transpose(table, (1, 0, 2)).reshape(table.shape[1], 2 * mine)
        hot, coef = list_tables(parent_sources.T, parent_offsets.T, parent_counts[None, :], flat_table)
        far = parent_sums(regrouped, hot, coef, parent_sources.shape[1])
        returned = lax.all_to_all(far, "box", split_axis=0, concat_axis=0, tiled=True)
    else:
        regrouped = lax.all_to_all(pattern, "box", split_axis=2, concat_axis=1, tiled=True)
        far = plain_translate(
            jnp.transpose(regrouped, (0, 2, 1)), table, parent_sources.T, parent_offsets.T, parent_counts
        ).astype(bf16)
        far = jnp.transpose(far, (0, 2, 1))
        returned = lax.all_to_all(far, "box", split_axis=1, concat_axis=2, tiled=True)

    child_cos, child_sin = child_phases(octant, cosine, sine)
    nearby = near_sums(
        own,
        near_before,
        near_after,
        child_sources.T,
        child_offsets.T,
        child_counts[None, :],
        child_table[:, :, 0, :],
    )
    lowered, rims = lower(returned, parent, child_cos, child_sin, interp_weights, parents, rim, packed)
    if groups == 2:
        got = shift(rims, "samp", 1, True)
        start_terms, end_terms = got[1], got[0]
    else:
        start_terms = shift(rims[1], "samp", 1, True)
        end_terms = shift(rims[0], "samp", -1, True)
    partial = anterpolate(interp_weights, lowered, nearby, rim)
    return finish(partial, start_terms, end_terms)[:, None]


def solution(mesh):
    return jax.shard_map(
        local,
        mesh=mesh,
        in_specs=(
            P(None, "samp", None, "box"),
            P("box"),
            P("box"),
            P("box", None),
            P("box", None),
            P("box"),
            P(),
            P(),
            P(),
            P(),
            P(None, "samp", None),
            P(None, None, "samp", None),
            P(None, None, "samp", "box"),
        ),
        out_specs=P(None, "samp", None, "box"),
        check_vma=False,
    )
```

```python
import jax
import jax.numpy as jnp
from jax import lax
from jax.experimental import pallas as pl
from jax.experimental.pallas import tpu as pltpu
from jax.sharding import PartitionSpec as P

NEARB = 32
OCTANTS = 8
LANES = 128
CHUNK = 128
f32, bf16, i32 = jnp.float32, jnp.bfloat16, jnp.int32
V, H = pltpu.VMEM, pltpu.HBM


class Fetched:
    def __init__(self, source, room, semaphore):
        self.copy = pltpu.make_async_copy(source, room, semaphore)
        self.room, self.waited = room, False
        self.copy.start()

    def __call__(self):
        if not self.waited:
            self.copy.wait()
            self.waited = True
        return self.room


def call(body, args, places, outs, name, rooms=(), scratch=(), flops=1 << 20, moved=1 << 20, limit=16 << 20):
    rooms = dict(rooms)
    fetched = [i for i, place in enumerate(places) if place is H and rooms.get(i, 0) is not None]
    spaces = [
        pltpu.VMEM(rooms.get(i, args[i].shape), args[i].dtype) for i in fetched
    ]

    def kernel(*refs):
        ins = list(refs[: len(args)])
        results = refs[len(args) : len(args) + len(outs)]
        rest = refs[len(args) + len(outs) :]
        held, rest = rest[: len(fetched)], rest[len(fetched) :]
        if fetched:
            semaphores, rest = rest[0], rest[1:]
            for n, i in enumerate(fetched):
                ins[i] = Fetched(ins[i], held[n], semaphores.at[n])
        body(ins, results, rest)

    semaphores = [pltpu.SemaphoreType.DMA((len(fetched),))] if fetched else []
    args = [
        pltpu.with_memory_space_constraint(arg, H) if place is H else arg for arg, place in zip(args, places)
    ]
    return pl.pallas_call(
        kernel,
        out_shape=[
            jax.ShapeDtypeStruct(shape, dtype) if place is None else place(shape, dtype)
            for shape, dtype, place in outs
        ],
        in_specs=[pl.BlockSpec(memory_space=place) for place in places],
        out_specs=[pl.BlockSpec(memory_space=place or V) for _, _, place in outs],
        scratch_shapes=spaces + semaphores + list(scratch),
        name=name,
        cost_estimate=pl.CostEstimate(flops=flops, bytes_accessed=moved, transcendentals=0),
        compiler_params=pltpu.CompilerParams(vmem_limit_bytes=limit),
    )(*args)


def nt(a, b):
    return lax.dot_general(a, b, (((1,), (1,)), ((), ())), preferred_element_type=f32)


def tn(a, b):
    return lax.dot_general(a, b, (((0,), (0,)), ((), ())), preferred_element_type=f32)


def nn(a, b):
    return lax.dot_general(a, b, (((1,), (0,)), ((), ())), preferred_element_type=f32)


def iota(shape, dim):
    return lax.broadcasted_iota(i32, shape, dim)


def ones_where(mask):
    return jnp.where(mask, 1.0, 0.0).astype(bf16)


def identity(n):
    return ones_where(iota((n, n), 0) == iota((n, n), 1))


def sincos(x):
    h = 0.5 * x
    q = h * h
    s = -2.50521083854417e-08 + q * 1.60590438368216e-10
    s = 2.75573192239859e-06 + q * s
    s = -1.98412698412698e-04 + q * s
    s = 8.33333333333333e-03 + q * s
    s = -1.66666666666667e-01 + q * s
    s = h + h * (q * s)
    c = 2.08767569878681e-09 + q * -1.14707455977297e-11
    c = -2.75573192239859e-07 + q * c
    c = 2.48015873015873e-05 + q * c
    c = -1.38888888888889e-03 + q * c
    c = 4.16666666666667e-02 + q * c
    c = -0.5 + q * c
    c = 1.0 + q * c
    return 2.0 * (s * c), 1.0 - 2.0 * (s * s)


def parts(x):
    high = x.astype(bf16)
    rest = x - high.astype(f32)
    middle = rest.astype(bf16)
    return [high, middle, (rest - middle.astype(f32)).astype(bf16)]


def phase_rows(cosine, sine):
    halves = [jnp.concatenate(parts(x) + [jnp.zeros(x.shape, bf16)], axis=0) for x in (cosine, sine)]
    return jnp.concatenate(halves, axis=1)


def octant_rows(octant, boxes):
    onehot = ones_where(iota((OCTANTS, boxes), 0) == octant)
    return jnp.concatenate([onehot] * 4, axis=0)


def prepare(own, octant, parent, phase, weights, parents):
    _, kcg, boxes = own.shape
    rows, kpg = weights.shape
    rim = (rows - kcg) // 2
    width = 512

    def body(ins, outs, rest):
        own_in, oct_in, par_in, ph_in, w_hbm = ins
        cos_ref, sin_ref, y_ref, w_ref, family_ref, phase_out, lead_out, trail_out = outs
        e_ref, phase_ref, sems = rest
        pieces = [
            pltpu.make_async_copy(
                w_hbm.at[:, pl.ds(n * (kpg // 2), kpg // 2)], w_ref.at[:, pl.ds(n * (kpg // 2), kpg // 2)], sems.at[n]
            )
            for n in range(2)
        ]
        for piece in pieces:
            piece.start()
        eye = identity(boxes)
        me = lax.axis_index("box")
        family = ones_where(iota((parents, boxes), 0) == par_in()[...] - me * parents)
        family_ref[...] = jnp.concatenate([family, family], axis=1)
        onehot = octant_rows(oct_in()[...], boxes)
        sine, cosine = sincos(ph_in()[:, 0, :])
        phase_ref[...] = phase_rows(cosine, sine)
        room = own_in()
        for r in range(2):
            e_ref[r * boxes : (r + 1) * boxes] = nt(eye, room[r]).astype(bf16)
        odd = lax.rem(me, 2)
        copies = [pltpu.make_async_copy(phase_ref, phase_out, sems.at[2])]
        for n, out in enumerate((lead_out, trail_out)):
            begin = pl.multiple_of(jnp.where(odd == n, boxes - NEARB, 0), NEARB)
            for r in range(2):
                copies.append(
                    pltpu.make_async_copy(
                        e_ref.at[pl.ds(r * boxes + begin, NEARB)], out.at[r], sems.at[3 + 2 * n + r]
                    )
                )
        for copy in copies:
            copy.start()
        cos_ref[...] = tn(onehot, phase_ref[:, :kpg])
        sin_ref[...] = tn(onehot, phase_ref[:, kpg:])
        for n, piece in enumerate(pieces):
            piece.wait()
            for step in range(kpg // 2 // width):
                begin = n * (kpg // 2) + step * width
                cols = slice(begin, begin + width)
                y_ref[:, cols] = nn(e_ref[...], w_ref[rim : rim + kcg, cols])
        for copy in copies:
            copy.wait()

    wave = ((boxes, kpg), f32, V)
    edge = ((2, NEARB, kcg), bf16, H)
    phases = (4 * OCTANTS, 2 * kpg)
    return call(
        body,
        [own, octant, parent, phase, weights],
        [H] * 5,
        [
            wave,
            wave,
            ((2 * boxes, kpg), f32, V),
            (weights.shape, bf16, V),
            ((parents, 2 * boxes), bf16, V),
            (phases, bf16, H),
            edge,
            edge,
        ],
        "prepare",
        rooms={4: None},
        scratch=[pltpu.VMEM((2 * boxes, kcg), bf16), pltpu.VMEM(phases, bf16), pltpu.SemaphoreType.DMA((7,))],
        flops=2 * 2 * boxes * kcg * kpg,
    )


def rise(rims, spans, family, cosine, sine, inner, weights, parents, packed):
    boxes, kpg = cosine.shape
    rows = weights.shape[0]
    rim = spans[0][2] - spans[0][1]
    width = 256
    shape = (kpg // LANES * parents, 2 * LANES) if packed else (2, parents, kpg)

    def body(ins, outs, rest):
        sides = ins[: len(rims)]
        family_ref, cos_ref, sin_ref, y_ref, w_ref = ins[len(rims) :]
        (out_hbm,) = outs
        out_ref, e_ref, wr_ref, shift_ref, sems = rest
        eye = identity(boxes)
        wr_ref[:rim] = w_ref[:rim]
        wr_ref[rim:] = w_ref[rows - rim :]
        for r in range(2):
            for side, (n, low, high) in enumerate(spans):
                e_ref[r * boxes : (r + 1) * boxes, side * rim : (side + 1) * rim] = nt(
                    eye, sides[n][r, low:high, :]
                ).astype(bf16)
        for step in range(kpg // width):
            cols = slice(step * width, (step + 1) * width)
            y = y_ref[:, cols] + nn(e_ref[...], wr_ref[:, cols])
            yr, yi, c, s = y[:boxes], y[boxes:], cos_ref[:, cols], sin_ref[:, cols]
            for r, value in enumerate((yr * c - yi * s, yr * s + yi * c)):
                high = value.astype(bf16)
                shift_ref[r, :boxes, cols] = high
                shift_ref[r, boxes:, cols] = (value - high.astype(f32)).astype(bf16)
        for step in range(kpg // width):
            cols = slice(step * width, (step + 1) * width)
            for r in range(2):
                total = nn(family_ref[...], shift_ref[r, :, cols]).astype(bf16)
                if packed:
                    for part in range(width // LANES):
                        row = (step * (width // LANES) + part) * parents
                        out_ref[row : row + parents, r * LANES : (r + 1) * LANES] = total[
                            :, part * LANES : (part + 1) * LANES
                        ]
                else:
                    out_ref[r, :, cols] = total
        copy = pltpu.make_async_copy(out_ref, out_hbm, sems)
        copy.start()
        copy.wait()

    return call(
        body,
        [*rims, family, cosine, sine, inner, weights],
        [V] * (len(rims) + 5),
        [(shape, bf16, H)],
        "rise",
        scratch=[
            pltpu.VMEM(shape, bf16),
            pltpu.VMEM((2 * boxes, 2 * rim), bf16),
            pltpu.VMEM((2 * rim, kpg), bf16),
            pltpu.VMEM((2, 2 * boxes, kpg), bf16),
            pltpu.SemaphoreType.DMA,
        ],
        flops=2 * 2 * boxes * 2 * rim * kpg,
    )[0]


def operators_of_lists(offsets, counts, table):
    slots, boxes = offsets.shape
    operators, lanes = table.shape

    def body(ins, outs, rest):
        off_in, cnt_in, tab_in = ins
        (coef_out,) = outs
        coef_ref, sems = rest
        off = jnp.where(iota((slots, boxes), 0) < cnt_in()[...], off_in()[...], -1).T
        size = slots * CHUNK
        copies = []
        for chunk in range(boxes // CHUNK):
            rows = slice(chunk * CHUNK, (chunk + 1) * CHUNK)
            pick = jnp.concatenate(
                [ones_where(off[rows, m : m + 1] == iota((CHUNK, operators), 1)) for m in range(slots)], axis=0
            )
            coef_ref[chunk * size : (chunk + 1) * size] = nn(pick, tab_in()[...]).astype(bf16)
            part = pl.ds(chunk * size, size)
            copies.append(pltpu.make_async_copy(coef_ref.at[part], coef_out.at[part], sems.at[chunk]))
            copies[-1].start()
        for copy in copies:
            copy.wait()

    return call(
        body,
        [offsets, counts, table],
        [H, H, H],
        [((slots * boxes, lanes), bf16, H)],
        "operators_of_lists",
        scratch=[pltpu.VMEM((slots * boxes, lanes), bf16), pltpu.SemaphoreType.DMA((boxes // CHUNK,))],
        flops=2 * slots * boxes * operators * lanes,
    )[0]


def parent_sums(pattern, sources, coef):
    total, lanes = pattern.shape
    slots = sources.shape[0]
    half = lanes // 2
    size = slots * CHUNK
    chunks = total // CHUNK
    halves = 2

    def body(ins, outs, rest):
        pat_ref, src_in, coef_in = ins
        (out_hbm,) = outs
        pick_ref, out_ref, sems = rest
        src = src_in()[...].T
        for chunk in range(chunks):
            rows = slice(chunk * CHUNK, (chunk + 1) * CHUNK)
            hot = jnp.concatenate(
                [ones_where(src[rows, m : m + 1] == iota((CHUNK, total), 1)) for m in range(slots)], axis=0
            )
            pick_ref[chunk * size : (chunk + 1) * size] = nn(hot, pat_ref[...])
        coef_ref = coef_in()
        copies = []
        for chunk in range(chunks):
            real = imag = 0.0
            for m in range(slots):
                part = slice(chunk * size + m * CHUNK, chunk * size + (m + 1) * CHUNK)
                pr, pi = pick_ref[part, :half], pick_ref[part, half:]
                c = coef_ref[part].astype(f32)
                cr, ci = c[:, :half], c[:, half:]
                real += cr * pr - ci * pi
                imag += cr * pi + ci * pr
            rows = slice(chunk * CHUNK, (chunk + 1) * CHUNK)
            out_ref[rows, :half] = real.astype(bf16)
            out_ref[rows, half:] = imag.astype(bf16)
            if (chunk + 1) % (chunks // halves) == 0:
                part = pl.ds(len(copies) * (total // halves), total // halves)
                copies.append(
                    pltpu.make_async_copy(out_ref.at[part], out_hbm.at[part], sems.at[len(copies)])
                )
                copies[-1].start()
        for copy in copies:
            copy.wait()

    return call(
        body,
        [pattern, sources, coef],
        [V, H, H],
        [((total, lanes), bf16, H)],
        "parent_sums",
        scratch=[
            pltpu.VMEM((slots * total, lanes), f32),
            pltpu.VMEM((total, lanes), bf16),
            pltpu.SemaphoreType.DMA((halves,)),
        ],
        flops=2 * slots * total * total * lanes,
        limit=24 << 20,
    )[0]


def lower(far, parent, octant, phases, weights, parents, rim, packed):
    boxes = parent.shape[1]
    rows, kpg = weights.shape
    width = LANES if packed else 256

    def body(ins, outs, rest):
        far_ref, par_in, oct_in, phase_in, w_ref = ins
        low_ref, rim_ref = outs
        base = lax.axis_index("box") * parents
        hot = ones_where(iota((parents, boxes), 0) == par_in()[...] - base).T
        onehot = octant_rows(oct_in()[...], boxes).T
        phase_ref = phase_in()
        for step in range(kpg // width):
            cols = slice(step * width, (step + 1) * width)
            if packed:
                spread = nn(hot, far_ref[step * parents : (step + 1) * parents])
                sr, si = spread[:, :LANES], spread[:, LANES:]
            else:
                sr, si = nn(hot, far_ref[0, :, cols]), nn(hot, far_ref[1, :, cols])
            sine_cols = slice(kpg + step * width, kpg + (step + 1) * width)
            both = nn(onehot, jnp.concatenate([phase_ref[:, cols], phase_ref[:, sine_cols]], axis=1))
            c, s = both[:, :width], both[:, width:]
            low_ref[:boxes, cols] = (sr * c + si * s).astype(bf16)
            low_ref[boxes:, cols] = (si * c - sr * s).astype(bf16)
        first = nt(w_ref[:rim], low_ref[...]).astype(bf16)
        last = nt(w_ref[rows - rim :], low_ref[...]).astype(bf16)
        for side, terms in enumerate((first, last)):
            for r in range(2):
                rim_ref[side, r] = terms[:, r * boxes : (r + 1) * boxes]

    return call(
        body,
        [far, parent, octant, phases, weights],
        [V, H, H, H, V],
        [((2 * boxes, kpg), bf16, V), ((2, 2, rim, boxes), bf16, V)],
        "lower",
        flops=2 * 2 * boxes * kpg * 2 * rim,
    )


def anterpolate(weights, lowered, nearby, rim):
    _, kcg, boxes = nearby.shape

    def body(ins, outs, rest):
        w_ref, low_ref, near_in = ins
        (out_ref,) = outs
        terms = nt(w_ref[rim : rim + kcg], low_ref[...]).astype(bf16).astype(f32)
        for r in range(2):
            out_ref[r] = near_in()[r] + terms[:, r * boxes : (r + 1) * boxes]

    return call(
        body,
        [weights, lowered, nearby],
        [V, V, H],
        [(nearby.shape, f32, V)],
        "anterpolate",
        flops=2 * kcg * weights.shape[1] * 2 * boxes,
    )[0]


def finish(partial, start_terms, end_terms):
    _, kcg, boxes = partial.shape
    rim = start_terms[0].shape[-2]
    arrays = [start_terms[0]] if end_terms[0] is start_terms[0] else [start_terms[0], end_terms[0]]

    def body(ins, outs, rest):
        sum_ref, start_ref, end_ref = ins[0], ins[1], ins[-1]
        (out_ref,) = outs
        start = start_ref[...] if start_terms[1] is None else start_ref[start_terms[1]]
        end = end_ref[...] if end_terms[1] is None else end_ref[end_terms[1]]
        out_ref[:, rim : kcg - rim] = sum_ref[:, rim : kcg - rim].astype(bf16)
        out_ref[:, :rim] = (sum_ref[:, :rim] + start.astype(f32)).astype(bf16)
        out_ref[:, kcg - rim :] = (sum_ref[:, kcg - rim :] + end.astype(f32)).astype(bf16)

    return call(
        body, [partial, *arrays], [V] * (1 + len(arrays)), [(partial.shape, bf16, None)], "finish"
    )[0]


def near_sums(own, lead, trail, sources, offsets, counts, table):
    _, kcg, boxes = own.shape
    slots = sources.shape[0]
    operators = table.shape[1]
    depth = 2 * boxes
    pair = 2

    def body(ins, outs, rest):
        own_in, lead_in, trail_in, src_in, off_in, cnt_in, tab_in = ins
        (near_out,) = outs
        out_ref, ext_ref, tt_ref, sem = rest
        eye = identity(boxes)
        own_ref, tab_ref = own_in(), tab_in()
        for r in range(2):
            rows = slice(r * kcg, (r + 1) * kcg)
            ext_ref[rows, :boxes] = own_ref[r]
            for step in range(kcg // boxes):
                cols = slice(step * boxes, (step + 1) * boxes)
                part = slice(r * kcg + step * boxes, r * kcg + (step + 1) * boxes)
                tt_ref[part] = nt(eye, tab_ref[r, :, cols]).astype(bf16)
        lead_ref, trail_ref = lead_in(), trail_in()
        for r in range(2):
            for step in range(kcg // boxes):
                cols = slice(step * boxes, (step + 1) * boxes)
                part = slice(r * kcg + step * boxes, r * kcg + (step + 1) * boxes)
                halo = jnp.concatenate(
                    [lead_ref[r, :, cols], trail_ref[r, :, cols], jnp.zeros((boxes - 2 * NEARB, boxes), bf16)],
                    axis=0,
                )
                ext_ref[part, boxes:] = nt(eye, halo).astype(bf16)
        me = lax.axis_index("box")
        odd = lax.rem(me, 2)
        rel = src_in()[...] - me * boxes
        below = rel + (boxes + NEARB) + (1 - odd) * NEARB
        above = rel + odd * NEARB
        rel = jnp.where(rel < 0, below, jnp.where(rel >= boxes, above, rel))
        off = jnp.where(iota((slots, boxes), 0) < cnt_in()[...], off_in()[...], -1)
        for m in range(0, slots, pair):
            src = jnp.concatenate([rel[m + j : m + j + 1] for j in range(pair)], axis=1)
            ops = jnp.concatenate([off[m + j : m + j + 1] for j in range(pair)], axis=1)
            hot = ones_where(iota((depth, pair * boxes), 0) == src)
            pick = ones_where(iota((operators, pair * boxes), 0) == ops)
            picked = nn(ext_ref[...], hot)
            coef = nn(tt_ref[...], pick)
            pr, pi, cr, ci = picked[:kcg], picked[kcg:], coef[:kcg], coef[kcg:]
            real, imag = cr * pr - ci * pi, cr * pi + ci * pr
            for r, value in enumerate((real, imag)):
                value = sum(value[:, j * boxes : (j + 1) * boxes] for j in range(pair))
                out_ref[r] = value if m == 0 else out_ref[r] + value
        copy = pltpu.make_async_copy(out_ref, near_out, sem)
        copy.start()
        copy.wait()

    return call(
        body,
        [own, lead, trail, sources, offsets, counts, table],
        [H] * 7,
        [(own.shape, f32, H)],
        "near_sums",
        scratch=[
            pltpu.VMEM(own.shape, f32),
            pltpu.VMEM((2 * kcg, depth), bf16),
            pltpu.VMEM((2 * kcg, operators), bf16),
            pltpu.SemaphoreType.DMA,
        ],
        flops=2 * slots * boxes * 2 * kcg * (depth + operators),
        limit=24 << 20,
    )[0]


def plain_translate(pattern, table, sources, offsets, counts):
    coef = jnp.transpose(table, (0, 2, 1))

    def advance(m, summed):
        src = lax.dynamic_index_in_dim(sources, m, 0, keepdims=False)
        off = lax.dynamic_index_in_dim(offsets, m, 0, keepdims=False)
        p = pattern[:, :, src].astype(f32)
        c = coef[:, :, off].astype(f32) * (m < counts).astype(f32)
        return summed + jnp.stack([c[0] * p[0] - c[1] * p[1], c[0] * p[1] + c[1] * p[0]])

    return lax.fori_loop(
        0, sources.shape[0], advance, jnp.zeros(pattern.shape[:2] + (sources.shape[1],), f32)
    )


def shift(value, axis, step):
    peers = lax.axis_size(axis)
    return lax.ppermute(value, axis, [(i, (i + step) % peers) for i in range(peers)])


def exchange(value, axis, first):
    peers = lax.axis_size(axis)
    pairs = [(i, i + 1) for i in range(first, peers - 1, 2)]
    return lax.ppermute(value, axis, pairs + [(j, i) for i, j in pairs])


def local(
    child_pattern,
    child_parent,
    child_octant,
    child_sources,
    child_offsets,
    child_counts,
    parent_sources,
    parent_offsets,
    parent_counts,
    interp_weights,
    shift_phase,
    child_table,
    parent_table,
):
    own = child_pattern[:, 0]
    _, kcg, boxes = own.shape
    rim = (interp_weights.shape[0] - kcg) // 2
    peers, groups = lax.axis_size("box"), lax.axis_size("samp")
    total = parent_sources.shape[0]
    parents = total // peers
    kpg = interp_weights.shape[1]
    mine = kpg // peers
    packed = mine == LANES and total % CHUNK == 0
    parent, octant = child_parent[None, :], child_octant[None, :]

    if groups == 2:
        rims = [shift(own, "samp", 1)]
        spans = ((0, kcg - rim, kcg), (0, 0, rim))
    else:
        rims = [shift(own[:, kcg - rim :], "samp", 1), shift(own[:, :rim], "samp", -1)]
        spans = ((0, 0, rim), (1, 0, rim))
    cosine, sine, inner, weights, family, phases, lead, trail = prepare(
        own, octant, parent, shift_phase, interp_weights, parents
    )
    pattern = rise(rims, spans, family, cosine, sine, inner, weights, parents, packed)
    lead, trail = exchange(lead, "box", 0), exchange(trail, "box", 1)

    table = parent_table[:, :, 0, :]
    if packed:
        regrouped = lax.all_to_all(pattern, "box", split_axis=0, concat_axis=0, tiled=True)
        regrouped, lead, trail = lax.optimization_barrier((regrouped, lead, trail))
        flat_table = jnp.transpose(table, (1, 0, 2)).reshape(table.shape[1], 2 * mine)
        coef = operators_of_lists(parent_offsets.T, parent_counts[None, :], flat_table)
        far = parent_sums(regrouped, parent_sources.T, coef)
        returned = lax.all_to_all(far, "box", split_axis=0, concat_axis=0, tiled=True)
    else:
        regrouped = lax.all_to_all(pattern, "box", split_axis=2, concat_axis=1, tiled=True)
        far = plain_translate(
            jnp.transpose(regrouped, (0, 2, 1)), table, parent_sources.T, parent_offsets.T, parent_counts
        ).astype(bf16)
        far = jnp.transpose(far, (0, 2, 1))
        returned = lax.all_to_all(far, "box", split_axis=1, concat_axis=2, tiled=True)

    nearby = near_sums(
        own,
        lead,
        trail,
        child_sources.T,
        child_offsets.T,
        child_counts[None, :],
        child_table[:, :, 0, :],
    )
    returned, nearby = lax.optimization_barrier((returned, nearby))
    lowered, terms = lower(returned, parent, octant, phases, interp_weights, parents, rim, packed)
    if groups == 2:
        got = shift(terms, "samp", 1)
        start_terms, end_terms = (got, 1), (got, 0)
    else:
        start_terms = (shift(terms[1], "samp", 1), None)
        end_terms = (shift(terms[0], "samp", -1), None)
    partial = anterpolate(interp_weights, lowered, nearby, rim)
    return finish(partial, start_terms, end_terms)[:, None]


def solution(mesh):
    return jax.shard_map(
        local,
        mesh=mesh,
        in_specs=(
            P(None, "samp", None, "box"),
            P("box"),
            P("box"),
            P("box", None),
            P("box", None),
            P("box"),
            P(),
            P(),
            P(),
            P(),
            P(None, "samp", None),
            P(None, None, "samp", None),
            P(None, None, "samp", "box"),
        ),
        out_specs=P(None, "samp", None, "box"),
        check_vma=False,
    )
```

```python
import jax
import jax.numpy as jnp
from jax import lax
from jax.experimental import pallas as pl
from jax.experimental.pallas import tpu as pltpu
from jax.sharding import PartitionSpec as P

NEARB = 32
OCTANTS = 8
LANES = 128
CHUNK = 128
f32, bf16, i32 = jnp.float32, jnp.bfloat16, jnp.int32
V, H = pltpu.VMEM, pltpu.HBM


class Fetched:
    def __init__(self, source, room, semaphore):
        self.copy = pltpu.make_async_copy(source, room, semaphore)
        self.room, self.waited = room, False
        self.copy.start()

    def __call__(self):
        if not self.waited:
            self.copy.wait()
            self.waited = True
        return self.room


def call(body, args, places, outs, name, rooms=(), scratch=(), flops=1 << 20, moved=1 << 20, limit=16 << 20):
    rooms = dict(rooms)
    fetched = [i for i, place in enumerate(places) if place is H and rooms.get(i, 0) is not None]
    spaces = [
        pltpu.VMEM(rooms.get(i, args[i].shape), args[i].dtype) for i in fetched
    ]

    def kernel(*refs):
        ins = list(refs[: len(args)])
        results = refs[len(args) : len(args) + len(outs)]
        rest = refs[len(args) + len(outs) :]
        held, rest = rest[: len(fetched)], rest[len(fetched) :]
        if fetched:
            semaphores, rest = rest[0], rest[1:]
            for n, i in enumerate(fetched):
                ins[i] = Fetched(ins[i], held[n], semaphores.at[n])
        body(ins, results, rest)

    semaphores = [pltpu.SemaphoreType.DMA((len(fetched),))] if fetched else []
    args = [
        pltpu.with_memory_space_constraint(arg, H) if place is H else arg for arg, place in zip(args, places)
    ]
    return pl.pallas_call(
        kernel,
        out_shape=[
            jax.ShapeDtypeStruct(shape, dtype) if place is None else place(shape, dtype)
            for shape, dtype, place in outs
        ],
        in_specs=[pl.BlockSpec(memory_space=place) for place in places],
        out_specs=[pl.BlockSpec(memory_space=place or V) for _, _, place in outs],
        scratch_shapes=spaces + semaphores + list(scratch),
        name=name,
        cost_estimate=pl.CostEstimate(flops=flops, bytes_accessed=moved, transcendentals=0),
        compiler_params=pltpu.CompilerParams(vmem_limit_bytes=limit),
    )(*args)


def nt(a, b):
    return lax.dot_general(a, b, (((1,), (1,)), ((), ())), preferred_element_type=f32)


def tn(a, b):
    return lax.dot_general(a, b, (((0,), (0,)), ((), ())), preferred_element_type=f32)


def nn(a, b):
    return lax.dot_general(a, b, (((1,), (0,)), ((), ())), preferred_element_type=f32)


def iota(shape, dim):
    return lax.broadcasted_iota(i32, shape, dim)


def ones_where(mask):
    return jnp.where(mask, 1.0, 0.0).astype(bf16)


def identity(n):
    return ones_where(iota((n, n), 0) == iota((n, n), 1))


def sincos(x):
    h = 0.5 * x
    q = h * h
    s = -2.50521083854417e-08 + q * 1.60590438368216e-10
    s = 2.75573192239859e-06 + q * s
    s = -1.98412698412698e-04 + q * s
    s = 8.33333333333333e-03 + q * s
    s = -1.66666666666667e-01 + q * s
    s = h + h * (q * s)
    c = 2.08767569878681e-09 + q * -1.14707455977297e-11
    c = -2.75573192239859e-07 + q * c
    c = 2.48015873015873e-05 + q * c
    c = -1.38888888888889e-03 + q * c
    c = 4.16666666666667e-02 + q * c
    c = -0.5 + q * c
    c = 1.0 + q * c
    return 2.0 * (s * c), 1.0 - 2.0 * (s * s)


def parts(x):
    high = x.astype(bf16)
    rest = x - high.astype(f32)
    middle = rest.astype(bf16)
    return [high, middle, (rest - middle.astype(f32)).astype(bf16)]


def phase_rows(x):
    return jnp.concatenate(parts(x) + [jnp.zeros(x.shape, bf16)], axis=0)


def octant_rows(octant, boxes):
    onehot = ones_where(iota((OCTANTS, boxes), 0) == octant)
    return jnp.concatenate([onehot] * 4, axis=0)


def prepare(own, octant, parent, phase, weights, parents):
    _, kcg, boxes = own.shape
    rows, kpg = weights.shape
    rim = (rows - kcg) // 2
    width = 512

    def body(ins, outs, rest):
        own_in, oct_in, par_in, ph_in, w_hbm = ins
        cos_ref, sin_ref, y_ref, w_ref, family_ref, phase_out, lead_out, trail_out = outs
        e_ref, phase_ref, sems = rest
        pieces = [
            pltpu.make_async_copy(
                w_hbm.at[:, pl.ds(n * (kpg // 2), kpg // 2)], w_ref.at[:, pl.ds(n * (kpg // 2), kpg // 2)], sems.at[n]
            )
            for n in range(2)
        ]
        for piece in pieces:
            piece.start()
        eye = identity(boxes)
        me = lax.axis_index("box")
        family = ones_where(iota((parents, boxes), 0) == par_in()[...] - me * parents)
        family_ref[...] = jnp.concatenate([family, family], axis=1)
        onehot = octant_rows(oct_in()[...], boxes)
        sine, cosine = sincos(ph_in()[:, 0, :])
        phase_ref[:OCTANTS] = cosine
        phase_ref[OCTANTS:] = sine
        room = own_in()
        for r in range(2):
            e_ref[r * boxes : (r + 1) * boxes] = nt(eye, room[r]).astype(bf16)
        odd = lax.rem(me, 2)
        copies = [pltpu.make_async_copy(phase_ref, phase_out, sems.at[2])]
        for n, out in enumerate((lead_out, trail_out)):
            begin = pl.multiple_of(jnp.where(odd == n, boxes - NEARB, 0), NEARB)
            for r in range(2):
                copies.append(
                    pltpu.make_async_copy(
                        e_ref.at[pl.ds(r * boxes + begin, NEARB)], out.at[r], sems.at[3 + 2 * n + r]
                    )
                )
        for copy in copies:
            copy.start()
        cos_ref[...] = tn(onehot, phase_rows(cosine))
        sin_ref[...] = tn(onehot, phase_rows(sine))
        for n, piece in enumerate(pieces):
            piece.wait()
            for step in range(kpg // 2 // width):
                begin = n * (kpg // 2) + step * width
                cols = slice(begin, begin + width)
                y_ref[:, cols] = nn(e_ref[...], w_ref[rim : rim + kcg, cols])
        for copy in copies:
            copy.wait()

    wave = ((boxes, kpg), f32, V)
    edge = ((2, NEARB, kcg), bf16, H)
    phases = (2 * OCTANTS, kpg)
    return call(
        body,
        [own, octant, parent, phase, weights],
        [H] * 5,
        [
            wave,
            wave,
            ((2 * boxes, kpg), f32, V),
            (weights.shape, bf16, V),
            ((parents, 2 * boxes), bf16, V),
            (phases, f32, H),
            edge,
            edge,
        ],
        "prepare",
        rooms={4: None},
        scratch=[pltpu.VMEM((2 * boxes, kcg), bf16), pltpu.VMEM(phases, f32), pltpu.SemaphoreType.DMA((7,))],
        flops=2 * 2 * boxes * kcg * kpg,
    )


def rise(rims, spans, family, cosine, sine, inner, weights, parents, packed):
    boxes, kpg = cosine.shape
    rows = weights.shape[0]
    rim = spans[0][2] - spans[0][1]
    width = 256
    shape = (kpg // LANES * parents, 2 * LANES) if packed else (2, parents, kpg)

    def body(ins, outs, rest):
        sides = ins[: len(rims)]
        family_ref, cos_ref, sin_ref, y_ref, w_ref = ins[len(rims) :]
        (out_hbm,) = outs
        out_ref, e_ref, wr_ref, shift_ref, sems = rest
        eye = identity(boxes)
        wr_ref[:rim] = w_ref[:rim]
        wr_ref[rim:] = w_ref[rows - rim :]
        for r in range(2):
            for side, (n, low, high) in enumerate(spans):
                e_ref[r * boxes : (r + 1) * boxes, side * rim : (side + 1) * rim] = nt(
                    eye, sides[n][r, low:high, :]
                ).astype(bf16)
        for step in range(kpg // width):
            cols = slice(step * width, (step + 1) * width)
            y = y_ref[:, cols] + nn(e_ref[...], wr_ref[:, cols])
            yr, yi, c, s = y[:boxes], y[boxes:], cos_ref[:, cols], sin_ref[:, cols]
            for r, value in enumerate((yr * c - yi * s, yr * s + yi * c)):
                high = value.astype(bf16)
                shift_ref[r, :boxes, cols] = high
                shift_ref[r, boxes:, cols] = (value - high.astype(f32)).astype(bf16)
        for step in range(kpg // width):
            cols = slice(step * width, (step + 1) * width)
            for r in range(2):
                total = nn(family_ref[...], shift_ref[r, :, cols]).astype(bf16)
                if packed:
                    for part in range(width // LANES):
                        row = (step * (width // LANES) + part) * parents
                        out_ref[row : row + parents, r * LANES : (r + 1) * LANES] = total[
                            :, part * LANES : (part + 1) * LANES
                        ]
                else:
                    out_ref[r, :, cols] = total
        copy = pltpu.make_async_copy(out_ref, out_hbm, sems)
        copy.start()
        copy.wait()

    return call(
        body,
        [*rims, family, cosine, sine, inner, weights],
        [V] * (len(rims) + 5),
        [(shape, bf16, H)],
        "rise",
        scratch=[
            pltpu.VMEM(shape, bf16),
            pltpu.VMEM((2 * boxes, 2 * rim), bf16),
            pltpu.VMEM((2 * rim, kpg), bf16),
            pltpu.VMEM((2, 2 * boxes, kpg), bf16),
            pltpu.SemaphoreType.DMA,
        ],
        flops=2 * 2 * boxes * 2 * rim * kpg,
    )[0]


def operators_of_lists(offsets, counts, table):
    slots, boxes = offsets.shape
    operators, _, half = table.shape
    lanes = 2 * half

    def body(ins, outs, rest):
        off_in, cnt_in, tab_in = ins
        (coef_ref,) = outs
        off = jnp.where(iota((slots, boxes), 0) < cnt_in()[...], off_in()[...], -1).T
        size = slots * CHUNK
        tables = jnp.swapaxes(tab_in()[...], 0, 1)
        flat = jnp.concatenate([tables[0], tables[1]], axis=1)
        for chunk in range(boxes // CHUNK):
            rows = slice(chunk * CHUNK, (chunk + 1) * CHUNK)
            pick = jnp.concatenate(
                [ones_where(off[rows, m : m + 1] == iota((CHUNK, operators), 1)) for m in range(slots)], axis=0
            )
            coef_ref[chunk * size : (chunk + 1) * size] = nn(pick, flat).astype(bf16)

    return call(
        body,
        [offsets, counts, table],
        [H, H, H],
        [((slots * boxes, lanes), bf16, V)],
        "operators_of_lists",
        flops=2 * slots * boxes * operators * lanes,
    )[0]


def parent_sums(pattern, sources, coef):
    total, lanes = pattern.shape
    slots = sources.shape[0]
    half = lanes // 2
    size = slots * CHUNK
    chunks = total // CHUNK
    halves = 2

    def body(ins, outs, rest):
        pat_ref, src_ref, coef_ref = ins
        (out_hbm,) = outs
        pick_ref, out_ref, sems = rest
        src = src_ref[...].T
        for chunk in range(chunks):
            rows = slice(chunk * CHUNK, (chunk + 1) * CHUNK)
            hot = jnp.concatenate(
                [ones_where(src[rows, m : m + 1] == iota((CHUNK, total), 1)) for m in range(slots)], axis=0
            )
            pick_ref[chunk * size : (chunk + 1) * size] = nn(hot, pat_ref[...])
        copies = []
        for chunk in range(chunks):
            real = imag = 0.0
            for m in range(slots):
                part = slice(chunk * size + m * CHUNK, chunk * size + (m + 1) * CHUNK)
                pr, pi = pick_ref[part, :half], pick_ref[part, half:]
                c = coef_ref[part].astype(f32)
                cr, ci = c[:, :half], c[:, half:]
                real += cr * pr - ci * pi
                imag += cr * pi + ci * pr
            rows = slice(chunk * CHUNK, (chunk + 1) * CHUNK)
            out_ref[rows, :half] = real.astype(bf16)
            out_ref[rows, half:] = imag.astype(bf16)
            if (chunk + 1) % (chunks // halves) == 0:
                part = pl.ds(len(copies) * (total // halves), total // halves)
                copies.append(
                    pltpu.make_async_copy(out_ref.at[part], out_hbm.at[part], sems.at[len(copies)])
                )
                copies[-1].start()
        for copy in copies:
            copy.wait()

    return call(
        body,
        [pattern, sources, coef],
        [V, V, V],
        [((total, lanes), bf16, H)],
        "parent_sums",
        scratch=[
            pltpu.VMEM((slots * total, lanes), f32),
            pltpu.VMEM((total, lanes), bf16),
            pltpu.SemaphoreType.DMA((halves,)),
        ],
        flops=2 * slots * total * total * lanes,
        limit=24 << 20,
    )[0]


def lower(far, parent, octant, phases, weights, parents, rim, packed):
    boxes = parent.shape[1]
    rows, kpg = weights.shape
    width = LANES if packed else 256

    def body(ins, outs, rest):
        far_ref, par_ref, oct_ref, phase_ref, w_ref = ins
        low_ref, rim_ref = outs
        base = lax.axis_index("box") * parents
        hot = ones_where(iota((parents, boxes), 0) == par_ref[...] - base).T
        onehot = octant_rows(oct_ref[...], boxes).T
        for step in range(kpg // width):
            cols = slice(step * width, (step + 1) * width)
            if packed:
                spread = nn(hot, far_ref[step * parents : (step + 1) * parents])
                sr, si = spread[:, :LANES], spread[:, LANES:]
            else:
                sr, si = nn(hot, far_ref[0, :, cols]), nn(hot, far_ref[1, :, cols])
            both = nn(
                onehot,
                jnp.concatenate(
                    [phase_rows(phase_ref[:OCTANTS, cols]), phase_rows(phase_ref[OCTANTS:, cols])], axis=1
                ),
            )
            c, s = both[:, :width], both[:, width:]
            low_ref[:boxes, cols] = (sr * c + si * s).astype(bf16)
            low_ref[boxes:, cols] = (si * c - sr * s).astype(bf16)
        first = nt(w_ref[:rim], low_ref[...]).astype(bf16)
        last = nt(w_ref[rows - rim :], low_ref[...]).astype(bf16)
        for side, terms in enumerate((first, last)):
            for r in range(2):
                rim_ref[side, r] = terms[:, r * boxes : (r + 1) * boxes]

    return call(
        body,
        [far, parent, octant, phases, weights],
        [V, V, V, V, V],
        [((2 * boxes, kpg), bf16, V), ((2, 2, rim, boxes), bf16, V)],
        "lower",
        flops=2 * 2 * boxes * kpg * 2 * rim,
    )


def anterpolate(weights, lowered, nearby, rim):
    _, kcg, boxes = nearby.shape

    def body(ins, outs, rest):
        w_ref, low_ref, near_ref = ins
        (out_ref,) = outs
        terms = nt(w_ref[rim : rim + kcg], low_ref[...]).astype(bf16).astype(f32)
        for r in range(2):
            out_ref[r] = near_ref[r] + terms[:, r * boxes : (r + 1) * boxes]

    return call(
        body,
        [weights, lowered, nearby],
        [V, V, V],
        [(nearby.shape, f32, V)],
        "anterpolate",
        flops=2 * kcg * weights.shape[1] * 2 * boxes,
    )[0]


def finish(partial, start_terms, end_terms):
    _, kcg, boxes = partial.shape
    rim = start_terms[0].shape[-2]
    arrays = [start_terms[0]] if end_terms[0] is start_terms[0] else [start_terms[0], end_terms[0]]

    def body(ins, outs, rest):
        sum_ref, start_ref, end_ref = ins[0], ins[1], ins[-1]
        (out_ref,) = outs
        start = start_ref[...] if start_terms[1] is None else start_ref[start_terms[1]]
        end = end_ref[...] if end_terms[1] is None else end_ref[end_terms[1]]
        out_ref[:, rim : kcg - rim] = sum_ref[:, rim : kcg - rim].astype(bf16)
        out_ref[:, :rim] = (sum_ref[:, :rim] + start.astype(f32)).astype(bf16)
        out_ref[:, kcg - rim :] = (sum_ref[:, kcg - rim :] + end.astype(f32)).astype(bf16)

    return call(
        body, [partial, *arrays], [V] * (1 + len(arrays)), [(partial.shape, bf16, None)], "finish"
    )[0]


def near_sums(own, lead, trail, sources, offsets, counts, table):
    _, kcg, boxes = own.shape
    slots = sources.shape[0]
    operators = table.shape[0]
    depth = 2 * boxes
    pair = 2

    def body(ins, outs, rest):
        own_in, lead_in, trail_in, src_in, off_in, cnt_in, tab_in = ins
        (out_ref,) = outs
        ext_ref, tt_ref = rest
        eye = identity(boxes)
        own_ref = own_in()
        tables = jnp.swapaxes(tab_in()[...], 0, 1)
        for r in range(2):
            rows = slice(r * kcg, (r + 1) * kcg)
            ext_ref[rows, :boxes] = own_ref[r]
            for step in range(kcg // boxes):
                cols = slice(step * boxes, (step + 1) * boxes)
                part = slice(r * kcg + step * boxes, r * kcg + (step + 1) * boxes)
                tt_ref[part] = nt(eye, tables[r, :, cols]).astype(bf16)
        lead_ref, trail_ref = lead_in(), trail_in()
        for r in range(2):
            for step in range(kcg // boxes):
                cols = slice(step * boxes, (step + 1) * boxes)
                part = slice(r * kcg + step * boxes, r * kcg + (step + 1) * boxes)
                halo = jnp.concatenate(
                    [lead_ref[r, :, cols], trail_ref[r, :, cols], jnp.zeros((boxes - 2 * NEARB, boxes), bf16)],
                    axis=0,
                )
                ext_ref[part, boxes:] = nt(eye, halo).astype(bf16)
        me = lax.axis_index("box")
        odd = lax.rem(me, 2)
        rel = src_in()[...] - me * boxes
        below = rel + (boxes + NEARB) + (1 - odd) * NEARB
        above = rel + odd * NEARB
        rel = jnp.where(rel < 0, below, jnp.where(rel >= boxes, above, rel))
        off = jnp.where(iota((slots, boxes), 0) < cnt_in()[...], off_in()[...], -1)
        for m in range(0, slots, pair):
            src = jnp.concatenate([rel[m + j : m + j + 1] for j in range(pair)], axis=1)
            ops = jnp.concatenate([off[m + j : m + j + 1] for j in range(pair)], axis=1)
            hot = ones_where(iota((depth, pair * boxes), 0) == src)
            pick = ones_where(iota((operators, pair * boxes), 0) == ops)
            picked = nn(ext_ref[...], hot)
            coef = nn(tt_ref[...], pick)
            pr, pi, cr, ci = picked[:kcg], picked[kcg:], coef[:kcg], coef[kcg:]
            real, imag = cr * pr - ci * pi, cr * pi + ci * pr
            for r, value in enumerate((real, imag)):
                value = sum(value[:, j * boxes : (j + 1) * boxes] for j in range(pair))
                out_ref[r] = value if m == 0 else out_ref[r] + value

    return call(
        body,
        [own, lead, trail, sources, offsets, counts, table],
        [H] * 7,
        [(own.shape, f32, V)],
        "near_sums",
        scratch=[pltpu.VMEM((2 * kcg, depth), bf16), pltpu.VMEM((2 * kcg, operators), bf16)],
        flops=2 * slots * boxes * 2 * kcg * (depth + operators),
        limit=24 << 20,
    )[0]


def plain_translate(pattern, table, sources, offsets, counts):
    coef = jnp.transpose(table, (0, 2, 1))

    def advance(m, summed):
        src = lax.dynamic_index_in_dim(sources, m, 0, keepdims=False)
        off = lax.dynamic_index_in_dim(offsets, m, 0, keepdims=False)
        p = pattern[:, :, src].astype(f32)
        c = coef[:, :, off].astype(f32) * (m < counts).astype(f32)
        return summed + jnp.stack([c[0] * p[0] - c[1] * p[1], c[0] * p[1] + c[1] * p[0]])

    return lax.fori_loop(
        0, sources.shape[0], advance, jnp.zeros(pattern.shape[:2] + (sources.shape[1],), f32)
    )


def shift(value, axis, step):
    peers = lax.axis_size(axis)
    return lax.ppermute(value, axis, [(i, (i + step) % peers) for i in range(peers)])


def exchange(value, axis, first):
    peers = lax.axis_size(axis)
    pairs = [(i, i + 1) for i in range(first, peers - 1, 2)]
    return lax.ppermute(value, axis, pairs + [(j, i) for i, j in pairs])


def local(
    child_pattern,
    child_parent,
    child_octant,
    child_sources,
    child_offsets,
    child_counts,
    parent_sources,
    parent_offsets,
    parent_counts,
    interp_weights,
    shift_phase,
    child_table,
    parent_table,
):
    own = child_pattern[:, 0]
    _, kcg, boxes = own.shape
    rim = (interp_weights.shape[0] - kcg) // 2
    peers, groups = lax.axis_size("box"), lax.axis_size("samp")
    total = parent_sources.shape[0]
    parents = total // peers
    kpg = interp_weights.shape[1]
    mine = kpg // peers
    packed = mine == LANES and total % CHUNK == 0
    parent, octant = child_parent[None, :], child_octant[None, :]

    if groups == 2:
        rims = [shift(own, "samp", 1)]
        spans = ((0, kcg - rim, kcg), (0, 0, rim))
    else:
        rims = [shift(own[:, kcg - rim :], "samp", 1), shift(own[:, :rim], "samp", -1)]
        spans = ((0, 0, rim), (1, 0, rim))
    cosine, sine, inner, weights, family, phases, lead, trail = prepare(
        own, octant, parent, shift_phase, interp_weights, parents
    )
    pattern = rise(rims, spans, family, cosine, sine, inner, weights, parents, packed)
    lead, trail = exchange(lead, "box", 0), exchange(trail, "box", 1)

    table = parent_table[:, :, 0, :]
    if packed:
        regrouped = lax.all_to_all(pattern, "box", split_axis=0, concat_axis=0, tiled=True)
        coef = operators_of_lists(parent_offsets.T, parent_counts[None, :], jnp.swapaxes(table, 0, 1))
        far = parent_sums(regrouped, parent_sources.T, coef)
        far, lead, trail = lax.optimization_barrier((far, lead, trail))
        returned = lax.all_to_all(far, "box", split_axis=0, concat_axis=0, tiled=True)
    else:
        regrouped = lax.all_to_all(pattern, "box", split_axis=2, concat_axis=1, tiled=True)
        far = plain_translate(
            jnp.transpose(regrouped, (0, 2, 1)), table, parent_sources.T, parent_offsets.T, parent_counts
        ).astype(bf16)
        far = jnp.transpose(far, (0, 2, 1))
        returned = lax.all_to_all(far, "box", split_axis=1, concat_axis=2, tiled=True)

    nearby = near_sums(
        own,
        lead,
        trail,
        child_sources.T,
        child_offsets.T,
        child_counts[None, :],
        jnp.swapaxes(child_table[:, :, 0, :], 0, 1),
    )
    returned, nearby = lax.optimization_barrier((returned, nearby))
    lowered, terms = lower(returned, parent, octant, phases, interp_weights, parents, rim, packed)
    if groups == 2:
        got = shift(terms, "samp", 1)
        start_terms, end_terms = (got, 1), (got, 0)
    else:
        start_terms = (shift(terms[1], "samp", 1), None)
        end_terms = (shift(terms[0], "samp", -1), None)
    partial = anterpolate(interp_weights, lowered, nearby, rim)
    return finish(partial, start_terms, end_terms)[:, None]


def solution(mesh):
    return jax.shard_map(
        local,
        mesh=mesh,
        in_specs=(
            P(None, "samp", None, "box"),
            P("box"),
            P("box"),
            P("box", None),
            P("box", None),
            P("box"),
            P(),
            P(),
            P(),
            P(),
            P(None, "samp", None),
            P(None, None, "samp", None),
            P(None, None, "samp", "box"),
        ),
        out_specs=P(None, "samp", None, "box"),
        check_vma=False,
    )
```

```python
import jax
import jax.numpy as jnp
from jax import lax
from jax.experimental import pallas as pl
from jax.experimental.pallas import tpu as pltpu
from jax.sharding import PartitionSpec as P

NEARB = 32
OCTANTS = 8
LANES = 128
CHUNK = 128
f32, bf16, i32 = jnp.float32, jnp.bfloat16, jnp.int32
V, H = pltpu.VMEM, pltpu.HBM


class Fetched:
    def __init__(self, source, room, semaphore):
        self.copy = pltpu.make_async_copy(source, room, semaphore)
        self.room, self.waited = room, False
        self.copy.start()

    def __call__(self):
        if not self.waited:
            self.copy.wait()
            self.waited = True
        return self.room


def call(body, args, places, outs, name, rooms=(), scratch=(), flops=1 << 20, moved=1 << 20, limit=16 << 20):
    rooms = dict(rooms)
    fetched = [i for i, place in enumerate(places) if place is H and rooms.get(i, 0) is not None]
    spaces = [
        pltpu.VMEM(rooms.get(i, args[i].shape), args[i].dtype) for i in fetched
    ]

    def kernel(*refs):
        ins = list(refs[: len(args)])
        results = refs[len(args) : len(args) + len(outs)]
        rest = refs[len(args) + len(outs) :]
        held, rest = rest[: len(fetched)], rest[len(fetched) :]
        if fetched:
            semaphores, rest = rest[0], rest[1:]
            for n, i in enumerate(fetched):
                ins[i] = Fetched(ins[i], held[n], semaphores.at[n])
        body(ins, results, rest)

    semaphores = [pltpu.SemaphoreType.DMA((len(fetched),))] if fetched else []
    args = [
        pltpu.with_memory_space_constraint(arg, H) if place is H else arg for arg, place in zip(args, places)
    ]
    return pl.pallas_call(
        kernel,
        out_shape=[
            jax.ShapeDtypeStruct(shape, dtype) if place is None else place(shape, dtype)
            for shape, dtype, place in outs
        ],
        in_specs=[pl.BlockSpec(memory_space=place) for place in places],
        out_specs=[pl.BlockSpec(memory_space=place or V) for _, _, place in outs],
        scratch_shapes=spaces + semaphores + list(scratch),
        name=name,
        cost_estimate=pl.CostEstimate(flops=flops, bytes_accessed=moved, transcendentals=0),
        compiler_params=pltpu.CompilerParams(vmem_limit_bytes=limit),
    )(*args)


def nt(a, b):
    return lax.dot_general(a, b, (((1,), (1,)), ((), ())), preferred_element_type=f32)


def tn(a, b):
    return lax.dot_general(a, b, (((0,), (0,)), ((), ())), preferred_element_type=f32)


def nn(a, b):
    return lax.dot_general(a, b, (((1,), (0,)), ((), ())), preferred_element_type=f32)


def iota(shape, dim):
    return lax.broadcasted_iota(i32, shape, dim)


def ones_where(mask):
    return jnp.where(mask, 1.0, 0.0).astype(bf16)


def identity(n):
    return ones_where(iota((n, n), 0) == iota((n, n), 1))


def sincos(x):
    h = 0.5 * x
    q = h * h
    s = -2.50521083854417e-08 + q * 1.60590438368216e-10
    s = 2.75573192239859e-06 + q * s
    s = -1.98412698412698e-04 + q * s
    s = 8.33333333333333e-03 + q * s
    s = -1.66666666666667e-01 + q * s
    s = h + h * (q * s)
    c = 2.08767569878681e-09 + q * -1.14707455977297e-11
    c = -2.75573192239859e-07 + q * c
    c = 2.48015873015873e-05 + q * c
    c = -1.38888888888889e-03 + q * c
    c = 4.16666666666667e-02 + q * c
    c = -0.5 + q * c
    c = 1.0 + q * c
    return 2.0 * (s * c), 1.0 - 2.0 * (s * s)


def parts(x):
    high = x.astype(bf16)
    rest = x - high.astype(f32)
    middle = rest.astype(bf16)
    return [high, middle, (rest - middle.astype(f32)).astype(bf16)]


def phase_rows(x):
    return jnp.concatenate(parts(x) + [jnp.zeros(x.shape, bf16)], axis=0)


def octant_rows(octant, boxes):
    onehot = ones_where(iota((OCTANTS, boxes), 0) == octant)
    return jnp.concatenate([onehot] * 4, axis=0)


def prepare(own, octant, parent, phase, weights, parents):
    _, kcg, boxes = own.shape
    kpg = phase.shape[2]

    def body(ins, outs, rest):
        own_in, oct_in, par_in, ph_in, w_hbm = ins
        cos_ref, sin_ref, e_ref, family_ref, w_ref, lead_out, trail_out = outs
        phase_ref, sems = rest
        fill = pltpu.make_async_copy(w_hbm, w_ref, sems.at[4])
        fill.start()
        eye = identity(boxes)
        me = lax.axis_index("box")
        family = ones_where(iota((parents, boxes), 0) == par_in()[...] - me * parents)
        family_ref[...] = jnp.concatenate([family, family], axis=1)
        onehot = octant_rows(oct_in()[...], boxes)
        phases = ph_in()
        room = own_in()
        for r in range(2):
            e_ref[r * boxes : (r + 1) * boxes] = nt(eye, room[r]).astype(bf16)
        odd = lax.rem(me, 2)
        copies = []
        for n, out in enumerate((lead_out, trail_out)):
            begin = pl.multiple_of(jnp.where(odd == n, boxes - NEARB, 0), NEARB)
            for r in range(2):
                copies.append(
                    pltpu.make_async_copy(
                        e_ref.at[pl.ds(r * boxes + begin, NEARB)], out.at[r], sems.at[2 * n + r]
                    )
                )
        for copy in copies:
            copy.start()
        phase_ref[...] = phases[:, 0, :]
        sine, cosine = sincos(phase_ref[...])
        cos_ref[...] = tn(onehot, phase_rows(cosine))
        sin_ref[...] = tn(onehot, phase_rows(sine))
        for copy in copies + [fill]:
            copy.wait()

    wave = ((boxes, kpg), f32, V)
    edge = ((2, NEARB, kcg), bf16, H)
    return call(
        body,
        [own, octant, parent, phase, weights],
        [H] * 5,
        [
            wave,
            wave,
            ((2 * boxes, kcg), bf16, V),
            ((parents, 2 * boxes), bf16, V),
            (weights.shape, bf16, V),
            edge,
            edge,
        ],
        "prepare",
        rooms={4: None},
        scratch=[pltpu.VMEM((OCTANTS, kpg), f32), pltpu.SemaphoreType.DMA((5,))],
    )


def rise(rims, spans, family, cosine, sine, inner, weights, parents, packed):
    boxes, kpg = cosine.shape
    rows = weights.shape[0]
    rim = spans[0][2] - spans[0][1]
    width = 256
    shape = (kpg // LANES * parents, 2 * LANES) if packed else (2, parents, kpg)

    def body(ins, outs, rest):
        sides = ins[: len(rims)]
        family_ref, cos_ref, sin_ref, inner_ref, w_ref = ins[len(rims) :]
        (out_hbm,) = outs
        out_ref, e_ref, wr_ref, shift_ref, sems = rest
        eye = identity(boxes)
        wr_ref[:rim] = w_ref[:rim]
        wr_ref[rim:] = w_ref[rows - rim :]
        for r in range(2):
            for side, (n, low, high) in enumerate(spans):
                e_ref[r * boxes : (r + 1) * boxes, side * rim : (side + 1) * rim] = nt(
                    eye, sides[n][r, low:high, :]
                ).astype(bf16)
        for step in range(kpg // width):
            cols = slice(step * width, (step + 1) * width)
            y = nn(inner_ref[...], w_ref[rim : rows - rim, cols]) + nn(e_ref[...], wr_ref[:, cols])
            yr, yi, c, s = y[:boxes], y[boxes:], cos_ref[:, cols], sin_ref[:, cols]
            for r, value in enumerate((yr * c - yi * s, yr * s + yi * c)):
                high = value.astype(bf16)
                shift_ref[r, :boxes, cols] = high
                shift_ref[r, boxes:, cols] = (value - high.astype(f32)).astype(bf16)
        copies = []
        for step in range(kpg // width):
            cols = slice(step * width, (step + 1) * width)
            for r in range(2):
                total = nn(family_ref[...], shift_ref[r, :, cols]).astype(bf16)
                if packed:
                    for part in range(width // LANES):
                        row = (step * (width // LANES) + part) * parents
                        out_ref[row : row + parents, r * LANES : (r + 1) * LANES] = total[
                            :, part * LANES : (part + 1) * LANES
                        ]
                else:
                    out_ref[r, :, cols] = total
            if (step + 1) * width * 2 % kpg == 0:
                if packed:
                    part = pl.ds(len(copies) * (shape[0] // 2), shape[0] // 2)
                    pair = out_ref.at[part], out_hbm.at[part]
                else:
                    part = pl.ds(len(copies) * (kpg // 2), kpg // 2)
                    pair = out_ref.at[:, :, part], out_hbm.at[:, :, part]
                copies.append(pltpu.make_async_copy(*pair, sems.at[len(copies)]))
                copies[-1].start()
        for copy in copies:
            copy.wait()

    return call(
        body,
        [*rims, family, cosine, sine, inner, weights],
        [V] * (len(rims) + 5),
        [(shape, bf16, H)],
        "rise",
        scratch=[
            pltpu.VMEM(shape, bf16),
            pltpu.VMEM((2 * boxes, 2 * rim), bf16),
            pltpu.VMEM((2 * rim, kpg), bf16),
            pltpu.VMEM((2, 2 * boxes, kpg), bf16),
            pltpu.SemaphoreType.DMA((2,)),
        ],
        flops=2 * 2 * boxes * rows * kpg,
    )[0]


def operators_of_lists(sources, offsets, counts, table):
    slots, boxes = offsets.shape
    operators, _, half = table.shape
    lanes = 2 * half

    def body(ins, outs, rest):
        src_in, off_in, cnt_in, tab_in = ins
        coef_ref, lane_ref = outs
        src = src_in()[...].T
        off = jnp.where(iota((slots, boxes), 0) < cnt_in()[...], off_in()[...], -1).T
        size = slots * CHUNK
        tables = jnp.swapaxes(tab_in()[...], 0, 1)
        flat = jnp.concatenate([tables[0], tables[1]], axis=1)
        for chunk in range(boxes // CHUNK):
            rows = slice(chunk * CHUNK, (chunk + 1) * CHUNK)
            pick = jnp.concatenate(
                [ones_where(off[rows, m : m + 1] == iota((CHUNK, operators), 1)) for m in range(slots)], axis=0
            )
            coef_ref[chunk * size : (chunk + 1) * size] = nn(pick, flat).astype(bf16)
            for m in range(slots):
                at = chunk * size + m * CHUNK
                lane_ref[at : at + CHUNK] = jnp.broadcast_to(src[rows, m : m + 1], (CHUNK, LANES)).astype(jnp.int16)

    return call(
        body,
        [sources, offsets, counts, table],
        [H, H, H, H],
        [((slots * boxes, lanes), bf16, V), ((slots * boxes, LANES), jnp.int16, V)],
        "operators_of_lists",
        flops=2 * slots * boxes * operators * lanes,
    )


def parent_sums(pattern, sources, coef, slots):
    total, lanes = pattern.shape
    half = lanes // 2
    size = slots * CHUNK
    chunks = total // CHUNK
    halves = 2

    def body(ins, outs, rest):
        pat_ref, src_ref, coef_ref = ins
        (out_hbm,) = outs
        pick_ref, out_ref, sems = rest
        one, zero = jnp.ones((), bf16), jnp.zeros((), bf16)
        for chunk in range(chunks):
            part = slice(chunk * size, (chunk + 1) * size)
            src = src_ref[part]
            lane = lax.broadcasted_iota(jnp.int16, src.shape, 1)
            hot = jnp.concatenate(
                [jnp.where(src == lane + jnp.int16(at), one, zero) for at in range(0, total, LANES)], axis=1
            )
            pick_ref[part] = nn(hot, pat_ref[...])
        copies = []
        for chunk in range(chunks):
            real = imag = 0.0
            for m in range(slots):
                part = slice(chunk * size + m * CHUNK, chunk * size + (m + 1) * CHUNK)
                pr, pi = pick_ref[part, :half], pick_ref[part, half:]
                c = coef_ref[part].astype(f32)
                cr, ci = c[:, :half], c[:, half:]
                real += cr * pr - ci * pi
                imag += cr * pi + ci * pr
            rows = slice(chunk * CHUNK, (chunk + 1) * CHUNK)
            out_ref[rows, :half] = real.astype(bf16)
            out_ref[rows, half:] = imag.astype(bf16)
            if (chunk + 1) % (chunks // halves) == 0:
                part = pl.ds(len(copies) * (total // halves), total // halves)
                copies.append(
                    pltpu.make_async_copy(out_ref.at[part], out_hbm.at[part], sems.at[len(copies)])
                )
                copies[-1].start()
        for copy in copies:
            copy.wait()

    return call(
        body,
        [pattern, sources, coef],
        [V, V, V],
        [((total, lanes), bf16, H)],
        "parent_sums",
        scratch=[
            pltpu.VMEM((slots * total, lanes), f32),
            pltpu.VMEM((total, lanes), bf16),
            pltpu.SemaphoreType.DMA((halves,)),
        ],
        flops=2 * slots * total * total * lanes,
        limit=24 << 20,
    )[0]


def lower(far, parent, octant, phases, weights, parents, rim, packed):
    boxes = parent.shape[1]
    rows, kpg = weights.shape
    width = LANES if packed else 256

    def body(ins, outs, rest):
        far_ref, par_ref, oct_ref, phase_ref, w_ref = ins
        low_ref, rim_ref = outs
        base = lax.axis_index("box") * parents
        hot = ones_where(iota((parents, boxes), 0) == par_ref[...] - base).T
        onehot = octant_rows(oct_ref[...], boxes).T
        for step in range(kpg // width):
            cols = slice(step * width, (step + 1) * width)
            if packed:
                spread = nn(hot, far_ref[step * parents : (step + 1) * parents])
                sr, si = spread[:, :LANES], spread[:, LANES:]
            else:
                sr, si = nn(hot, far_ref[0, :, cols]), nn(hot, far_ref[1, :, cols])
            both = nn(
                onehot,
                jnp.concatenate(
                    [phase_rows(phase_ref[:OCTANTS, cols]), phase_rows(phase_ref[OCTANTS:, cols])], axis=1
                ),
            )
            c, s = both[:, :width], both[:, width:]
            low_ref[:boxes, cols] = (sr * c + si * s).astype(bf16)
            low_ref[boxes:, cols] = (si * c - sr * s).astype(bf16)
        ends = jnp.concatenate([w_ref[:rim], w_ref[rows - rim :]], axis=0)
        terms = nt(ends, low_ref[...]).astype(bf16)
        for side in range(2):
            for r in range(2):
                rim_ref[side, r] = terms[side * rim : (side + 1) * rim, r * boxes : (r + 1) * boxes]

    return call(
        body,
        [far, parent, octant, phases, weights],
        [V, V, V, V, V],
        [((2 * boxes, kpg), bf16, V), ((2, 2, rim, boxes), bf16, V)],
        "lower",
        flops=2 * 2 * boxes * kpg * 2 * rim,
    )


def anterpolate(weights, lowered, nearby, rim):
    _, kcg, boxes = nearby.shape

    def body(ins, outs, rest):
        w_ref, low_ref, near_ref = ins
        (out_ref,) = outs
        terms = nt(w_ref[rim : rim + kcg], low_ref[...]).astype(bf16).astype(f32)
        for r in range(2):
            out_ref[r] = near_ref[r] + terms[:, r * boxes : (r + 1) * boxes]

    return call(
        body,
        [weights, lowered, nearby],
        [V, V, V],
        [(nearby.shape, f32, V)],
        "anterpolate",
        flops=2 * kcg * weights.shape[1] * 2 * boxes,
    )[0]


def finish(partial, start_terms, end_terms):
    _, kcg, boxes = partial.shape
    rim = start_terms[0].shape[-2]
    arrays = [start_terms[0]] if end_terms[0] is start_terms[0] else [start_terms[0], end_terms[0]]

    def body(ins, outs, rest):
        sum_ref, start_ref, end_ref = ins[0], ins[1], ins[-1]
        (out_ref,) = outs
        start = start_ref[...] if start_terms[1] is None else start_ref[start_terms[1]]
        end = end_ref[...] if end_terms[1] is None else end_ref[end_terms[1]]
        out_ref[:, rim : kcg - rim] = sum_ref[:, rim : kcg - rim].astype(bf16)
        out_ref[:, :rim] = (sum_ref[:, :rim] + start.astype(f32)).astype(bf16)
        out_ref[:, kcg - rim :] = (sum_ref[:, kcg - rim :] + end.astype(f32)).astype(bf16)

    return call(
        body, [partial, *arrays], [V] * (1 + len(arrays)), [(partial.shape, bf16, None)], "finish"
    )[0]


def near_sums(own, lead, trail, sources, offsets, counts, table, phase):
    _, kcg, boxes = own.shape
    kpg = phase.shape[2]
    slots = sources.shape[0]
    operators = table.shape[0]
    depth = 2 * boxes
    pair = 2

    def body(ins, outs, rest):
        own_in, lead_in, trail_in, src_in, off_in, cnt_in, tab_in, ph_in = ins
        out_ref, phase_ref = outs
        ext_ref, tt_ref, dense_ref = rest
        dense_ref[...] = ph_in()[:, 0, :]
        sine, cosine = sincos(dense_ref[...])
        phase_ref[:OCTANTS] = cosine
        phase_ref[OCTANTS:] = sine
        eye = identity(boxes)
        own_ref = own_in()
        tables = jnp.swapaxes(tab_in()[...], 0, 1)
        for r in range(2):
            rows = slice(r * kcg, (r + 1) * kcg)
            ext_ref[rows, :boxes] = own_ref[r]
            for step in range(kcg // boxes):
                cols = slice(step * boxes, (step + 1) * boxes)
                part = slice(r * kcg + step * boxes, r * kcg + (step + 1) * boxes)
                tt_ref[part] = nt(eye, tables[r, :, cols]).astype(bf16)
        lead_ref, trail_ref = lead_in(), trail_in()
        for r in range(2):
            for step in range(kcg // boxes):
                cols = slice(step * boxes, (step + 1) * boxes)
                part = slice(r * kcg + step * boxes, r * kcg + (step + 1) * boxes)
                halo = jnp.concatenate(
                    [lead_ref[r, :, cols], trail_ref[r, :, cols], jnp.zeros((boxes - 2 * NEARB, boxes), bf16)],
                    axis=0,
                )
                ext_ref[part, boxes:] = nt(eye, halo).astype(bf16)
        me = lax.axis_index("box")
        odd = lax.rem(me, 2)
        rel = src_in()[...] - me * boxes
        below = rel + (boxes + NEARB) + (1 - odd) * NEARB
        above = rel + odd * NEARB
        rel = jnp.where(rel < 0, below, jnp.where(rel >= boxes, above, rel))
        off = jnp.where(iota((slots, boxes), 0) < cnt_in()[...], off_in()[...], -1)
        for m in range(0, slots, pair):
            src = jnp.concatenate([rel[m + j : m + j + 1] for j in range(pair)], axis=1)
            ops = jnp.concatenate([off[m + j : m + j + 1] for j in range(pair)], axis=1)
            hot = ones_where(iota((depth, pair * boxes), 0) == src)
            pick = ones_where(iota((operators, pair * boxes), 0) == ops)
            picked = nn(ext_ref[...], hot)
            coef = nn(tt_ref[...], pick)
            pr, pi, cr, ci = picked[:kcg], picked[kcg:], coef[:kcg], coef[kcg:]
            real, imag = cr * pr - ci * pi, cr * pi + ci * pr
            for r, value in enumerate((real, imag)):
                value = sum(value[:, j * boxes : (j + 1) * boxes] for j in range(pair))
                out_ref[r] = value if m == 0 else out_ref[r] + value

    return call(
        body,
        [own, lead, trail, sources, offsets, counts, table, phase],
        [H] * 8,
        [(own.shape, f32, V), ((2 * OCTANTS, kpg), f32, V)],
        "near_sums",
        scratch=[
            pltpu.VMEM((2 * kcg, depth), bf16),
            pltpu.VMEM((2 * kcg, operators), bf16),
            pltpu.VMEM((OCTANTS, kpg), f32),
        ],
        flops=2 * slots * boxes * 2 * kcg * (depth + operators),
        limit=24 << 20,
    )


def plain_translate(pattern, table, sources, offsets, counts):
    coef = jnp.transpose(table, (0, 2, 1))

    def advance(m, summed):
        src = lax.dynamic_index_in_dim(sources, m, 0, keepdims=False)
        off = lax.dynamic_index_in_dim(offsets, m, 0, keepdims=False)
        p = pattern[:, :, src].astype(f32)
        c = coef[:, :, off].astype(f32) * (m < counts).astype(f32)
        return summed + jnp.stack([c[0] * p[0] - c[1] * p[1], c[0] * p[1] + c[1] * p[0]])

    return lax.fori_loop(
        0, sources.shape[0], advance, jnp.zeros(pattern.shape[:2] + (sources.shape[1],), f32)
    )


def shift(value, axis, step):
    peers = lax.axis_size(axis)
    return lax.ppermute(value, axis, [(i, (i + step) % peers) for i in range(peers)])


def exchange(value, axis, first):
    peers = lax.axis_size(axis)
    pairs = [(i, i + 1) for i in range(first, peers - 1, 2)]
    return lax.ppermute(value, axis, pairs + [(j, i) for i, j in pairs])


def local(
    child_pattern,
    child_parent,
    child_octant,
    child_sources,
    child_offsets,
    child_counts,
    parent_sources,
    parent_offsets,
    parent_counts,
    interp_weights,
    shift_phase,
    child_table,
    parent_table,
):
    own = child_pattern[:, 0]
    _, kcg, boxes = own.shape
    rim = (interp_weights.shape[0] - kcg) // 2
    peers, groups = lax.axis_size("box"), lax.axis_size("samp")
    total = parent_sources.shape[0]
    parents = total // peers
    kpg = interp_weights.shape[1]
    mine = kpg // peers
    packed = mine == LANES and total % CHUNK == 0
    parent, octant = child_parent[None, :], child_octant[None, :]

    if groups == 2:
        rims = [shift(own, "samp", 1)]
        spans = ((0, kcg - rim, kcg), (0, 0, rim))
    else:
        rims = [shift(own[:, kcg - rim :], "samp", 1), shift(own[:, :rim], "samp", -1)]
        spans = ((0, 0, rim), (1, 0, rim))
    cosine, sine, inner, family, weights, lead, trail = prepare(
        own, octant, parent, shift_phase, interp_weights, parents
    )
    pattern = rise(rims, spans, family, cosine, sine, inner, weights, parents, packed)
    lead, trail = exchange(lead, "box", 0), exchange(trail, "box", 1)

    table = parent_table[:, :, 0, :]
    if packed:
        regrouped = lax.all_to_all(pattern, "box", split_axis=0, concat_axis=0, tiled=True)
        coef, sources = operators_of_lists(
            parent_sources.T, parent_offsets.T, parent_counts[None, :], jnp.swapaxes(table, 0, 1)
        )
        far = parent_sums(regrouped, sources, coef, parent_sources.shape[1])
        far, lead, trail = lax.optimization_barrier((far, lead, trail))
        returned = lax.all_to_all(far, "box", split_axis=0, concat_axis=0, tiled=True)
    else:
        regrouped = lax.all_to_all(pattern, "box", split_axis=2, concat_axis=1, tiled=True)
        far = plain_translate(
            jnp.transpose(regrouped, (0, 2, 1)), table, parent_sources.T, parent_offsets.T, parent_counts
        ).astype(bf16)
        far = jnp.transpose(far, (0, 2, 1))
        returned = lax.all_to_all(far, "box", split_axis=1, concat_axis=2, tiled=True)

    nearby, phases = near_sums(
        own,
        lead,
        trail,
        child_sources.T,
        child_offsets.T,
        child_counts[None, :],
        jnp.swapaxes(child_table[:, :, 0, :], 0, 1),
        shift_phase,
    )
    returned, nearby = lax.optimization_barrier((returned, nearby))
    lowered, terms = lower(returned, parent, octant, phases, interp_weights, parents, rim, packed)
    if groups == 2:
        got = shift(terms, "samp", 1)
        start_terms, end_terms = (got, 1), (got, 0)
    else:
        start_terms = (shift(terms[1], "samp", 1), None)
        end_terms = (shift(terms[0], "samp", -1), None)
    partial = anterpolate(interp_weights, lowered, nearby, rim)
    return finish(partial, start_terms, end_terms)[:, None]


def solution(mesh):
    return jax.shard_map(
        local,
        mesh=mesh,
        in_specs=(
            P(None, "samp", None, "box"),
            P("box"),
            P("box"),
            P("box", None),
            P("box", None),
            P("box"),
            P(),
            P(),
            P(),
            P(),
            P(None, "samp", None),
            P(None, None, "samp", None),
            P(None, None, "samp", "box"),
        ),
        out_specs=P(None, "samp", None, "box"),
        check_vma=False,
    )
```

```python
import jax
import jax.numpy as jnp
from jax import lax
from jax.experimental import pallas as pl
from jax.experimental.pallas import tpu as pltpu
from jax.sharding import PartitionSpec as P

NEARB = 32
OCTANTS = 8
LANES = 128
CHUNK = 128
f32, bf16, i32 = jnp.float32, jnp.bfloat16, jnp.int32
V, H = pltpu.VMEM, pltpu.HBM


class Fetched:
    def __init__(self, source, room, semaphore):
        self.copy = pltpu.make_async_copy(source, room, semaphore)
        self.room, self.waited = room, False
        self.copy.start()

    def __call__(self):
        if not self.waited:
            self.copy.wait()
            self.waited = True
        return self.room


def call(body, args, places, outs, name, rooms=(), scratch=(), flops=1 << 20, moved=1 << 20, limit=16 << 20):
    rooms = dict(rooms)
    fetched = [i for i, place in enumerate(places) if place is H and rooms.get(i, 0) is not None]
    spaces = [
        pltpu.VMEM(rooms.get(i, args[i].shape), args[i].dtype) for i in fetched
    ]

    def kernel(*refs):
        ins = list(refs[: len(args)])
        results = refs[len(args) : len(args) + len(outs)]
        rest = refs[len(args) + len(outs) :]
        held, rest = rest[: len(fetched)], rest[len(fetched) :]
        if fetched:
            semaphores, rest = rest[0], rest[1:]
            for n, i in enumerate(fetched):
                ins[i] = Fetched(ins[i], held[n], semaphores.at[n])
        body(ins, results, rest)

    semaphores = [pltpu.SemaphoreType.DMA((len(fetched),))] if fetched else []
    args = [
        pltpu.with_memory_space_constraint(arg, H) if place is H else arg for arg, place in zip(args, places)
    ]
    return pl.pallas_call(
        kernel,
        out_shape=[
            jax.ShapeDtypeStruct(shape, dtype) if place is None else place(shape, dtype)
            for shape, dtype, place in outs
        ],
        in_specs=[pl.BlockSpec(memory_space=place) for place in places],
        out_specs=[pl.BlockSpec(memory_space=place or V) for _, _, place in outs],
        scratch_shapes=spaces + semaphores + list(scratch),
        name=name,
        cost_estimate=pl.CostEstimate(flops=flops, bytes_accessed=moved, transcendentals=0),
        compiler_params=pltpu.CompilerParams(vmem_limit_bytes=limit),
    )(*args)


def nt(a, b):
    return lax.dot_general(a, b, (((1,), (1,)), ((), ())), preferred_element_type=f32)


def tn(a, b):
    return lax.dot_general(a, b, (((0,), (0,)), ((), ())), preferred_element_type=f32)


def nn(a, b):
    return lax.dot_general(a, b, (((1,), (0,)), ((), ())), preferred_element_type=f32)


def iota(shape, dim):
    return lax.broadcasted_iota(i32, shape, dim)


def ones_where(mask):
    return jnp.where(mask, 1.0, 0.0).astype(bf16)


def identity(n):
    return ones_where(iota((n, n), 0) == iota((n, n), 1))


def sincos(x):
    h = 0.5 * x
    q = h * h
    s = -2.50521083854417e-08 + q * 1.60590438368216e-10
    s = 2.75573192239859e-06 + q * s
    s = -1.98412698412698e-04 + q * s
    s = 8.33333333333333e-03 + q * s
    s = -1.66666666666667e-01 + q * s
    s = h + h * (q * s)
    c = 2.08767569878681e-09 + q * -1.14707455977297e-11
    c = -2.75573192239859e-07 + q * c
    c = 2.48015873015873e-05 + q * c
    c = -1.38888888888889e-03 + q * c
    c = 4.16666666666667e-02 + q * c
    c = -0.5 + q * c
    c = 1.0 + q * c
    return 2.0 * (s * c), 1.0 - 2.0 * (s * s)


def parts(x):
    high = x.astype(bf16)
    rest = x - high.astype(f32)
    middle = rest.astype(bf16)
    return [high, middle, (rest - middle.astype(f32)).astype(bf16)]


def phase_rows(x):
    return jnp.concatenate(parts(x) + [jnp.zeros(x.shape, bf16)], axis=0)


def octant_rows(octant, boxes):
    onehot = ones_where(iota((OCTANTS, boxes), 0) == octant)
    return jnp.concatenate([onehot] * 4, axis=0)


def prepare(own, octant, parent, phase, weights, parents):
    _, kcg, boxes = own.shape
    kpg = phase.shape[2]

    def body(ins, outs, rest):
        own_in, oct_in, par_in, ph_in, w_hbm = ins
        cos_ref, sin_ref, e_ref, family_ref, w_ref, lead_out, trail_out = outs
        phase_ref, sems = rest
        fill = pltpu.make_async_copy(w_hbm, w_ref, sems.at[4])
        fill.start()
        eye = identity(boxes)
        me = lax.axis_index("box")
        family = ones_where(iota((parents, boxes), 0) == par_in()[...] - me * parents)
        family_ref[...] = jnp.concatenate([family, family], axis=1)
        onehot = octant_rows(oct_in()[...], boxes)
        phases = ph_in()
        room = own_in()
        for r in range(2):
            e_ref[r * boxes : (r + 1) * boxes] = nt(eye, room[r]).astype(bf16)
        odd = lax.rem(me, 2)
        copies = []
        for n, out in enumerate((lead_out, trail_out)):
            begin = pl.multiple_of(jnp.where(odd == n, boxes - NEARB, 0), NEARB)
            for r in range(2):
                copies.append(
                    pltpu.make_async_copy(
                        e_ref.at[pl.ds(r * boxes + begin, NEARB)], out.at[r], sems.at[2 * n + r]
                    )
                )
        for copy in copies:
            copy.start()
        phase_ref[...] = phases[:, 0, :]
        sine, cosine = sincos(phase_ref[...])
        cos_ref[...] = tn(onehot, phase_rows(cosine))
        sin_ref[...] = tn(onehot, phase_rows(sine))
        for copy in copies + [fill]:
            copy.wait()

    wave = ((boxes, kpg), f32, V)
    edge = ((2, NEARB, kcg), bf16, H)
    return call(
        body,
        [own, octant, parent, phase, weights],
        [H] * 5,
        [
            wave,
            wave,
            ((2 * boxes, kcg), bf16, V),
            ((parents, 2 * boxes), bf16, V),
            (weights.shape, bf16, V),
            edge,
            edge,
        ],
        "prepare",
        rooms={4: None},
        scratch=[pltpu.VMEM((OCTANTS, kpg), f32), pltpu.SemaphoreType.DMA((5,))],
    )


def rise(rims, spans, family, cosine, sine, inner, weights, parents, order):
    boxes, kpg = cosine.shape
    rows = weights.shape[0]
    rim = spans[0][2] - spans[0][1]
    width = 256
    packed = order is not None
    shape = (kpg // LANES * parents, 2 * LANES) if packed else (2, parents, kpg)

    def body(ins, outs, rest):
        sides = ins[: len(rims)]
        family_ref, cos_ref, sin_ref, inner_ref, w_ref = ins[len(rims) :]
        (out_hbm,) = outs
        out_ref, e_ref, wr_ref, shift_ref, sems = rest
        eye = identity(boxes)
        wr_ref[:rim] = w_ref[:rim]
        wr_ref[rim:] = w_ref[rows - rim :]
        for r in range(2):
            for side, (n, low, high) in enumerate(spans):
                e_ref[r * boxes : (r + 1) * boxes, side * rim : (side + 1) * rim] = nt(
                    eye, sides[n][r, low:high, :]
                ).astype(bf16)
        for step in range(kpg // width):
            cols = slice(step * width, (step + 1) * width)
            y = nn(inner_ref[...], w_ref[rim : rows - rim, cols]) + nn(e_ref[...], wr_ref[:, cols])
            yr, yi, c, s = y[:boxes], y[boxes:], cos_ref[:, cols], sin_ref[:, cols]
            for r, value in enumerate((yr * c - yi * s, yr * s + yi * c)):
                high = value.astype(bf16)
                shift_ref[r, :boxes, cols] = high
                shift_ref[r, boxes:, cols] = (value - high.astype(f32)).astype(bf16)
        copies = []
        pieces = kpg // LANES
        for n in range(pieces):
            piece = order[n] if packed else n
            cols = slice(piece * LANES, (piece + 1) * LANES)
            both = nn(family_ref[...], jnp.concatenate([shift_ref[0, :, cols], shift_ref[1, :, cols]], axis=1))
            both = both.astype(bf16)
            if packed:
                out_ref[n * parents : (n + 1) * parents] = both
            else:
                out_ref[0, :, cols], out_ref[1, :, cols] = both[:, :LANES], both[:, LANES:]
            if (n + 1) * 2 % pieces == 0:
                if packed:
                    part = pl.ds(len(copies) * (shape[0] // 2), shape[0] // 2)
                    pair = out_ref.at[part], out_hbm.at[part]
                else:
                    part = pl.ds(len(copies) * (kpg // 2), kpg // 2)
                    pair = out_ref.at[:, :, part], out_hbm.at[:, :, part]
                copies.append(pltpu.make_async_copy(*pair, sems.at[len(copies)]))
                copies[-1].start()
        for copy in copies:
            copy.wait()

    return call(
        body,
        [*rims, family, cosine, sine, inner, weights],
        [V] * (len(rims) + 5),
        [(shape, bf16, H)],
        "rise",
        scratch=[
            pltpu.VMEM(shape, bf16),
            pltpu.VMEM((2 * boxes, 2 * rim), bf16),
            pltpu.VMEM((2 * rim, kpg), bf16),
            pltpu.VMEM((2, 2 * boxes, kpg), bf16),
            pltpu.SemaphoreType.DMA((2,)),
        ],
        flops=2 * 2 * boxes * rows * kpg,
    )[0]


def operators_of_lists(sources, offsets, counts, table, order):
    slots, boxes = offsets.shape
    operators, _, half = table.shape
    lanes = 2 * half

    def body(ins, outs, rest):
        src_in, off_in, cnt_in, tab_in = ins
        coef_ref, lane_ref = outs
        family = boxes // len(order)
        src = src_in()[...]
        home = src // family
        moved = src
        for n, index in enumerate(order):
            moved = jnp.where(home == index, src + (n - index) * family, moved)
        off = jnp.where(iota((slots, boxes), 0) < cnt_in()[...], off_in()[...], -1)
        src, off = (
            jnp.concatenate([x.T[index * family : (index + 1) * family] for index in order], axis=0)
            for x in (moved, off)
        )
        size = slots * CHUNK
        tables = jnp.swapaxes(tab_in()[...], 0, 1)
        flat = jnp.concatenate([tables[0], tables[1]], axis=1)
        for chunk in range(boxes // CHUNK):
            rows = slice(chunk * CHUNK, (chunk + 1) * CHUNK)
            pick = jnp.concatenate(
                [ones_where(off[rows, m : m + 1] == iota((CHUNK, operators), 1)) for m in range(slots)], axis=0
            )
            coef_ref[chunk * size : (chunk + 1) * size] = nn(pick, flat).astype(bf16)
            for m in range(slots):
                at = chunk * size + m * CHUNK
                lane_ref[at : at + CHUNK] = jnp.broadcast_to(src[rows, m : m + 1], (CHUNK, LANES)).astype(jnp.int16)

    return call(
        body,
        [sources, offsets, counts, table],
        [H, H, H, H],
        [((slots * boxes, lanes), bf16, V), ((slots * boxes, LANES), jnp.int16, V)],
        "operators_of_lists",
        flops=2 * slots * boxes * operators * lanes,
    )


def parent_sums(pattern, sources, coef, slots):
    total, lanes = pattern.shape
    half = lanes // 2
    size = slots * CHUNK
    chunks = total // CHUNK
    halves = 2

    def body(ins, outs, rest):
        pat_ref, src_ref, coef_ref = ins
        (out_hbm,) = outs
        pick_ref, out_ref, sems = rest
        one, zero = jnp.ones((), bf16), jnp.zeros((), bf16)
        for chunk in range(chunks):
            part = slice(chunk * size, (chunk + 1) * size)
            src = src_ref[part]
            lane = lax.broadcasted_iota(jnp.int16, src.shape, 1)
            hot = jnp.concatenate(
                [jnp.where(src == lane + jnp.int16(at), one, zero) for at in range(0, total, LANES)], axis=1
            )
            pick_ref[part] = nn(hot, pat_ref[...])
        copies = []
        for chunk in range(chunks):
            real = imag = 0.0
            for m in range(slots):
                part = slice(chunk * size + m * CHUNK, chunk * size + (m + 1) * CHUNK)
                pr, pi = pick_ref[part, :half], pick_ref[part, half:]
                c = coef_ref[part].astype(f32)
                cr, ci = c[:, :half], c[:, half:]
                real += cr * pr - ci * pi
                imag += cr * pi + ci * pr
            rows = slice(chunk * CHUNK, (chunk + 1) * CHUNK)
            out_ref[rows, :half] = real.astype(bf16)
            out_ref[rows, half:] = imag.astype(bf16)
            if (chunk + 1) % (chunks // halves) == 0:
                part = pl.ds(len(copies) * (total // halves), total // halves)
                copies.append(
                    pltpu.make_async_copy(out_ref.at[part], out_hbm.at[part], sems.at[len(copies)])
                )
                copies[-1].start()
        for copy in copies:
            copy.wait()

    return call(
        body,
        [pattern, sources, coef],
        [V, V, V],
        [((total, lanes), bf16, H)],
        "parent_sums",
        scratch=[
            pltpu.VMEM((slots * total, lanes), f32),
            pltpu.VMEM((total, lanes), bf16),
            pltpu.SemaphoreType.DMA((halves,)),
        ],
        flops=2 * slots * total * total * lanes,
        limit=24 << 20,
    )[0]


def lower(far, parent, octant, phases, weights, parents, rim, order):
    boxes = parent.shape[1]
    rows, kpg = weights.shape
    packed = order is not None
    width = LANES if packed else 256

    def body(ins, outs, rest):
        far_ref, par_ref, oct_ref, phase_ref, w_ref = ins
        low_ref, rim_ref = outs
        base = lax.axis_index("box") * parents
        hot = ones_where(iota((parents, boxes), 0) == par_ref[...] - base).T
        onehot = octant_rows(oct_ref[...], boxes).T
        for step in range(kpg // width):
            cols = slice(step * width, (step + 1) * width)
            if packed:
                at = order.index(step) * parents
                spread = nn(hot, far_ref[at : at + parents])
                sr, si = spread[:, :LANES], spread[:, LANES:]
            else:
                sr, si = nn(hot, far_ref[0, :, cols]), nn(hot, far_ref[1, :, cols])
            both = nn(
                onehot,
                jnp.concatenate(
                    [phase_rows(phase_ref[:OCTANTS, cols]), phase_rows(phase_ref[OCTANTS:, cols])], axis=1
                ),
            )
            c, s = both[:, :width], both[:, width:]
            low_ref[:boxes, cols] = (sr * c + si * s).astype(bf16)
            low_ref[boxes:, cols] = (si * c - sr * s).astype(bf16)
        ends = jnp.concatenate([w_ref[:rim], w_ref[rows - rim :]], axis=0)
        terms = nt(ends, low_ref[...]).astype(bf16)
        for side in range(2):
            for r in range(2):
                rim_ref[side, r] = terms[side * rim : (side + 1) * rim, r * boxes : (r + 1) * boxes]

    return call(
        body,
        [far, parent, octant, phases, weights],
        [V, V, V, V, V],
        [((2 * boxes, kpg), bf16, V), ((2, 2, rim, boxes), bf16, V)],
        "lower",
        flops=2 * 2 * boxes * kpg * 2 * rim,
    )


def anterpolate(weights, lowered, nearby, rim):
    _, kcg, boxes = nearby.shape

    def body(ins, outs, rest):
        w_ref, low_ref, near_ref = ins
        (out_ref,) = outs
        terms = nt(w_ref[rim : rim + kcg], low_ref[...]).astype(bf16).astype(f32)
        for r in range(2):
            out_ref[r] = near_ref[r] + terms[:, r * boxes : (r + 1) * boxes]

    return call(
        body,
        [weights, lowered, nearby],
        [V, V, V],
        [(nearby.shape, f32, V)],
        "anterpolate",
        flops=2 * kcg * weights.shape[1] * 2 * boxes,
    )[0]


def finish(partial, start_terms, end_terms):
    _, kcg, boxes = partial.shape
    rim = start_terms[0].shape[-2]
    arrays = [start_terms[0]] if end_terms[0] is start_terms[0] else [start_terms[0], end_terms[0]]

    def body(ins, outs, rest):
        sum_ref, start_ref, end_ref = ins[0], ins[1], ins[-1]
        (out_ref,) = outs
        start = start_ref[...] if start_terms[1] is None else start_ref[start_terms[1]]
        end = end_ref[...] if end_terms[1] is None else end_ref[end_terms[1]]
        out_ref[:, rim : kcg - rim] = sum_ref[:, rim : kcg - rim].astype(bf16)
        out_ref[:, :rim] = (sum_ref[:, :rim] + start.astype(f32)).astype(bf16)
        out_ref[:, kcg - rim :] = (sum_ref[:, kcg - rim :] + end.astype(f32)).astype(bf16)

    return call(
        body, [partial, *arrays], [V] * (1 + len(arrays)), [(partial.shape, bf16, None)], "finish"
    )[0]


def near_sums(own, lead, trail, sources, offsets, counts, table, phase):
    _, kcg, boxes = own.shape
    kpg = phase.shape[2]
    slots = sources.shape[0]
    operators = table.shape[0]
    depth = 2 * boxes
    pair = 2

    def body(ins, outs, rest):
        own_in, lead_in, trail_in, src_in, off_in, cnt_in, tab_in, ph_in = ins
        out_ref, phase_ref = outs
        ext_ref, tt_ref, dense_ref = rest
        dense_ref[...] = ph_in()[:, 0, :]
        sine, cosine = sincos(dense_ref[...])
        phase_ref[:OCTANTS] = cosine
        phase_ref[OCTANTS:] = sine
        eye = identity(boxes)
        own_ref = own_in()
        tables = jnp.swapaxes(tab_in()[...], 0, 1)
        for r in range(2):
            rows = slice(r * kcg, (r + 1) * kcg)
            ext_ref[rows, :boxes] = own_ref[r]
            for step in range(kcg // boxes):
                cols = slice(step * boxes, (step + 1) * boxes)
                part = slice(r * kcg + step * boxes, r * kcg + (step + 1) * boxes)
                tt_ref[part] = nt(eye, tables[r, :, cols]).astype(bf16)
        lead_ref, trail_ref = lead_in(), trail_in()
        for r in range(2):
            for step in range(kcg // boxes):
                cols = slice(step * boxes, (step + 1) * boxes)
                part = slice(r * kcg + step * boxes, r * kcg + (step + 1) * boxes)
                halo = jnp.concatenate(
                    [lead_ref[r, :, cols], trail_ref[r, :, cols], jnp.zeros((boxes - 2 * NEARB, boxes), bf16)],
                    axis=0,
                )
                ext_ref[part, boxes:] = nt(eye, halo).astype(bf16)
        me = lax.axis_index("box")
        odd = lax.rem(me, 2)
        rel = src_in()[...] - me * boxes
        below = rel + (boxes + NEARB) + (1 - odd) * NEARB
        above = rel + odd * NEARB
        rel = jnp.where(rel < 0, below, jnp.where(rel >= boxes, above, rel))
        off = jnp.where(iota((slots, boxes), 0) < cnt_in()[...], off_in()[...], -1)
        for m in range(0, slots, pair):
            src = jnp.concatenate([rel[m + j : m + j + 1] for j in range(pair)], axis=1)
            ops = jnp.concatenate([off[m + j : m + j + 1] for j in range(pair)], axis=1)
            hot = ones_where(iota((depth, pair * boxes), 0) == src)
            pick = ones_where(iota((operators, pair * boxes), 0) == ops)
            picked = nn(ext_ref[...], hot)
            coef = nn(tt_ref[...], pick)
            pr, pi, cr, ci = picked[:kcg], picked[kcg:], coef[:kcg], coef[kcg:]
            real, imag = cr * pr - ci * pi, cr * pi + ci * pr
            for r, value in enumerate((real, imag)):
                value = sum(value[:, j * boxes : (j + 1) * boxes] for j in range(pair))
                out_ref[r] = value if m == 0 else out_ref[r] + value

    return call(
        body,
        [own, lead, trail, sources, offsets, counts, table, phase],
        [H] * 8,
        [(own.shape, f32, V), ((2 * OCTANTS, kpg), f32, V)],
        "near_sums",
        scratch=[
            pltpu.VMEM((2 * kcg, depth), bf16),
            pltpu.VMEM((2 * kcg, operators), bf16),
            pltpu.VMEM((OCTANTS, kpg), f32),
        ],
        flops=2 * slots * boxes * 2 * kcg * (depth + operators),
        limit=24 << 20,
    )


def plain_translate(pattern, table, sources, offsets, counts):
    coef = jnp.transpose(table, (0, 2, 1))

    def advance(m, summed):
        src = lax.dynamic_index_in_dim(sources, m, 0, keepdims=False)
        off = lax.dynamic_index_in_dim(offsets, m, 0, keepdims=False)
        p = pattern[:, :, src].astype(f32)
        c = coef[:, :, off].astype(f32) * (m < counts).astype(f32)
        return summed + jnp.stack([c[0] * p[0] - c[1] * p[1], c[0] * p[1] + c[1] * p[0]])

    return lax.fori_loop(
        0, sources.shape[0], advance, jnp.zeros(pattern.shape[:2] + (sources.shape[1],), f32)
    )


def ring(peers):
    gray = [i ^ (i >> 1) for i in range(peers)]
    if sorted(gray) != list(range(peers)):
        return list(range(peers))
    middle = gray.index((peers // 2 + 1) % peers)
    return gray[middle:] + gray[:middle]


def regroup(value, order):
    return lax.all_to_all(
        value, "box", split_axis=0, concat_axis=0, tiled=True, axis_index_groups=[list(order)]
    )


def shift(value, axis, step):
    peers = lax.axis_size(axis)
    return lax.ppermute(value, axis, [(i, (i + step) % peers) for i in range(peers)])


def exchange(value, axis, first):
    peers = lax.axis_size(axis)
    pairs = [(i, i + 1) for i in range(first, peers - 1, 2)]
    return lax.ppermute(value, axis, pairs + [(j, i) for i, j in pairs])


def local(
    child_pattern,
    child_parent,
    child_octant,
    child_sources,
    child_offsets,
    child_counts,
    parent_sources,
    parent_offsets,
    parent_counts,
    interp_weights,
    shift_phase,
    child_table,
    parent_table,
):
    own = child_pattern[:, 0]
    _, kcg, boxes = own.shape
    rim = (interp_weights.shape[0] - kcg) // 2
    peers, groups = lax.axis_size("box"), lax.axis_size("samp")
    total = parent_sources.shape[0]
    parents = total // peers
    kpg = interp_weights.shape[1]
    mine = kpg // peers
    packed = mine == LANES and total % CHUNK == 0
    order = ring(peers) if packed else None
    parent, octant = child_parent[None, :], child_octant[None, :]

    if groups == 2:
        rims = [shift(own, "samp", 1)]
        spans = ((0, kcg - rim, kcg), (0, 0, rim))
    else:
        rims = [shift(own[:, kcg - rim :], "samp", 1), shift(own[:, :rim], "samp", -1)]
        spans = ((0, 0, rim), (1, 0, rim))
    cosine, sine, inner, family, weights, lead, trail = prepare(
        own, octant, parent, shift_phase, interp_weights, parents
    )
    pattern = rise(rims, spans, family, cosine, sine, inner, weights, parents, order)
    lead, trail = exchange(lead, "box", 0), exchange(trail, "box", 1)

    table = parent_table[:, :, 0, :]
    if packed:
        regrouped = regroup(pattern, order)
        coef, sources = operators_of_lists(
            parent_sources.T, parent_offsets.T, parent_counts[None, :], jnp.swapaxes(table, 0, 1), order
        )
        far = parent_sums(regrouped, sources, coef, parent_sources.shape[1])
        far, lead, trail = lax.optimization_barrier((far, lead, trail))
        returned = regroup(far, order)
    else:
        regrouped = lax.all_to_all(pattern, "box", split_axis=2, concat_axis=1, tiled=True)
        far = plain_translate(
            jnp.transpose(regrouped, (0, 2, 1)), table, parent_sources.T, parent_offsets.T, parent_counts
        ).astype(bf16)
        far = jnp.transpose(far, (0, 2, 1))
        returned = lax.all_to_all(far, "box", split_axis=1, concat_axis=2, tiled=True)

    nearby, phases = near_sums(
        own,
        lead,
        trail,
        child_sources.T,
        child_offsets.T,
        child_counts[None, :],
        jnp.swapaxes(child_table[:, :, 0, :], 0, 1),
        shift_phase,
    )
    returned, nearby = lax.optimization_barrier((returned, nearby))
    lowered, terms = lower(returned, parent, octant, phases, interp_weights, parents, rim, order)
    if groups == 2:
        got = shift(terms, "samp", 1)
        start_terms, end_terms = (got, 1), (got, 0)
    else:
        start_terms = (shift(terms[1], "samp", 1), None)
        end_terms = (shift(terms[0], "samp", -1), None)
    partial = anterpolate(interp_weights, lowered, nearby, rim)
    return finish(partial, start_terms, end_terms)[:, None]


def solution(mesh):
    return jax.shard_map(
        local,
        mesh=mesh,
        in_specs=(
            P(None, "samp", None, "box"),
            P("box"),
            P("box"),
            P("box", None),
            P("box", None),
            P("box"),
            P(),
            P(),
            P(),
            P(),
            P(None, "samp", None),
            P(None, None, "samp", None),
            P(None, None, "samp", "box"),
        ),
        out_specs=P(None, "samp", None, "box"),
        check_vma=False,
    )
```

```python
import jax
import jax.numpy as jnp
from jax import lax
from jax.experimental import pallas as pl
from jax.experimental.pallas import tpu as pltpu
from jax.sharding import PartitionSpec as P

NEARB = 32
OCTANTS = 8
LANES = 128
CHUNK = 128
f32, bf16, i32 = jnp.float32, jnp.bfloat16, jnp.int32
V, H = pltpu.VMEM, pltpu.HBM


class Fetched:
    def __init__(self, source, room, semaphore):
        self.copy = pltpu.make_async_copy(source, room, semaphore)
        self.room, self.waited = room, False
        self.copy.start()

    def __call__(self):
        if not self.waited:
            self.copy.wait()
            self.waited = True
        return self.room


def call(body, args, places, outs, name, rooms=(), scratch=(), flops=1 << 20, moved=1 << 20, limit=16 << 20):
    rooms = dict(rooms)
    fetched = [i for i, place in enumerate(places) if place is H and rooms.get(i, 0) is not None]
    spaces = [
        pltpu.VMEM(rooms.get(i, args[i].shape), args[i].dtype) for i in fetched
    ]

    def kernel(*refs):
        ins = list(refs[: len(args)])
        results = refs[len(args) : len(args) + len(outs)]
        rest = refs[len(args) + len(outs) :]
        held, rest = rest[: len(fetched)], rest[len(fetched) :]
        if fetched:
            semaphores, rest = rest[0], rest[1:]
            for n, i in enumerate(fetched):
                ins[i] = Fetched(ins[i], held[n], semaphores.at[n])
        body(ins, results, rest)

    semaphores = [pltpu.SemaphoreType.DMA((len(fetched),))] if fetched else []
    args = [
        pltpu.with_memory_space_constraint(arg, H) if place is H else arg for arg, place in zip(args, places)
    ]
    return pl.pallas_call(
        kernel,
        out_shape=[
            jax.ShapeDtypeStruct(shape, dtype) if place is None else place(shape, dtype)
            for shape, dtype, place in outs
        ],
        in_specs=[pl.BlockSpec(memory_space=place) for place in places],
        out_specs=[pl.BlockSpec(memory_space=place or V) for _, _, place in outs],
        scratch_shapes=spaces + semaphores + list(scratch),
        name=name,
        cost_estimate=pl.CostEstimate(flops=flops, bytes_accessed=moved, transcendentals=0),
        compiler_params=pltpu.CompilerParams(vmem_limit_bytes=limit),
    )(*args)


def nt(a, b):
    return lax.dot_general(a, b, (((1,), (1,)), ((), ())), preferred_element_type=f32)


def tn(a, b):
    return lax.dot_general(a, b, (((0,), (0,)), ((), ())), preferred_element_type=f32)


def nn(a, b):
    return lax.dot_general(a, b, (((1,), (0,)), ((), ())), preferred_element_type=f32)


def iota(shape, dim):
    return lax.broadcasted_iota(i32, shape, dim)


def ones_where(mask):
    return jnp.where(mask, 1.0, 0.0).astype(bf16)


def identity(n):
    return ones_where(iota((n, n), 0) == iota((n, n), 1))


def sincos(x):
    h = 0.5 * x
    q = h * h
    s = -2.50521083854417e-08 + q * 1.60590438368216e-10
    s = 2.75573192239859e-06 + q * s
    s = -1.98412698412698e-04 + q * s
    s = 8.33333333333333e-03 + q * s
    s = -1.66666666666667e-01 + q * s
    s = h + h * (q * s)
    c = 2.08767569878681e-09 + q * -1.14707455977297e-11
    c = -2.75573192239859e-07 + q * c
    c = 2.48015873015873e-05 + q * c
    c = -1.38888888888889e-03 + q * c
    c = 4.16666666666667e-02 + q * c
    c = -0.5 + q * c
    c = 1.0 + q * c
    return 2.0 * (s * c), 1.0 - 2.0 * (s * s)


def parts(x):
    high = x.astype(bf16)
    rest = x - high.astype(f32)
    middle = rest.astype(bf16)
    return [high, middle, (rest - middle.astype(f32)).astype(bf16)]


def phase_rows(x):
    return jnp.concatenate(parts(x) + [jnp.zeros(x.shape, bf16)], axis=0)


def octant_rows(octant, boxes):
    onehot = ones_where(iota((OCTANTS, boxes), 0) == octant)
    return jnp.concatenate([onehot] * 4, axis=0)


def prepare(own, octant, parent, phase, weights, parents):
    _, kcg, boxes = own.shape
    kpg = phase.shape[2]

    def body(ins, outs, rest):
        own_in, oct_in, par_in, ph_in, w_hbm = ins
        cos_ref, sin_ref, e_ref, family_ref, w_ref, lead_out, trail_out = outs
        phase_ref, sems = rest
        fill = pltpu.make_async_copy(w_hbm, w_ref, sems.at[4])
        fill.start()
        eye = identity(boxes)
        me = lax.axis_index("box")
        family = ones_where(iota((parents, boxes), 0) == par_in()[...] - me * parents)
        family_ref[...] = jnp.concatenate([family, family], axis=1)
        onehot = octant_rows(oct_in()[...], boxes)
        phases = ph_in()
        room = own_in()
        for r in range(2):
            e_ref[r * boxes : (r + 1) * boxes] = nt(eye, room[r]).astype(bf16)
        odd = lax.rem(me, 2)
        copies = []
        for n, out in enumerate((lead_out, trail_out)):
            begin = pl.multiple_of(jnp.where(odd == n, boxes - NEARB, 0), NEARB)
            for r in range(2):
                copies.append(
                    pltpu.make_async_copy(
                        e_ref.at[pl.ds(r * boxes + begin, NEARB)], out.at[r], sems.at[2 * n + r]
                    )
                )
        for copy in copies:
            copy.start()
        phase_ref[...] = phases[:, 0, :]
        sine, cosine = sincos(phase_ref[...])
        cos_ref[...] = tn(onehot, phase_rows(cosine))
        sin_ref[...] = tn(onehot, phase_rows(sine))
        for copy in copies + [fill]:
            copy.wait()

    wave = ((boxes, kpg), f32, V)
    edge = ((2, NEARB, kcg), bf16, H)
    return call(
        body,
        [own, octant, parent, phase, weights],
        [H] * 5,
        [
            wave,
            wave,
            ((2 * boxes, kcg), bf16, V),
            ((parents, 2 * boxes), bf16, V),
            (weights.shape, bf16, V),
            edge,
            edge,
        ],
        "prepare",
        rooms={4: None},
        scratch=[pltpu.VMEM((OCTANTS, kpg), f32), pltpu.SemaphoreType.DMA((5,))],
    )


def rise(rims, spans, family, cosine, sine, inner, weights, parents, order):
    boxes, kpg = cosine.shape
    rows = weights.shape[0]
    rim = spans[0][2] - spans[0][1]
    width = 256
    packed = order is not None
    shape = (kpg // LANES * parents, 2 * LANES) if packed else (2, parents, kpg)

    def body(ins, outs, rest):
        sides = ins[: len(rims)]
        family_ref, cos_ref, sin_ref, inner_ref, w_ref = ins[len(rims) :]
        (out_hbm,) = outs
        out_ref, e_ref, shift_ref, sems = rest
        eye = identity(boxes)
        for r in range(2):
            part = slice(r * boxes, (r + 1) * boxes)
            before, after = (nt(eye, sides[n][r, low:high, :]).astype(bf16) for n, low, high in spans)
            e_ref[part] = jnp.concatenate([before, inner_ref[part], after], axis=1)
        for step in range(kpg // width):
            cols = slice(step * width, (step + 1) * width)
            y = nn(e_ref[...], w_ref[:, cols])
            yr, yi, c, s = y[:boxes], y[boxes:], cos_ref[:, cols], sin_ref[:, cols]
            for r, value in enumerate((yr * c - yi * s, yr * s + yi * c)):
                high = value.astype(bf16)
                shift_ref[r, :boxes, cols] = high
                shift_ref[r, boxes:, cols] = (value - high.astype(f32)).astype(bf16)
        copies = []
        pieces = kpg // LANES
        for n in range(pieces):
            piece = order[n] if packed else n
            cols = slice(piece * LANES, (piece + 1) * LANES)
            both = nn(family_ref[...], jnp.concatenate([shift_ref[0, :, cols], shift_ref[1, :, cols]], axis=1))
            both = both.astype(bf16)
            if packed:
                out_ref[n * parents : (n + 1) * parents] = both
            else:
                out_ref[0, :, cols], out_ref[1, :, cols] = both[:, :LANES], both[:, LANES:]
            if (n + 1) * 2 % pieces == 0:
                if packed:
                    part = pl.ds(len(copies) * (shape[0] // 2), shape[0] // 2)
                    pair = out_ref.at[part], out_hbm.at[part]
                else:
                    part = pl.ds(len(copies) * (kpg // 2), kpg // 2)
                    pair = out_ref.at[:, :, part], out_hbm.at[:, :, part]
                copies.append(pltpu.make_async_copy(*pair, sems.at[len(copies)]))
                copies[-1].start()
        for copy in copies:
            copy.wait()

    return call(
        body,
        [*rims, family, cosine, sine, inner, weights],
        [V] * (len(rims) + 5),
        [(shape, bf16, H)],
        "rise",
        scratch=[
            pltpu.VMEM(shape, bf16),
            pltpu.VMEM((2 * boxes, rows), bf16),
            pltpu.VMEM((2, 2 * boxes, kpg), bf16),
            pltpu.SemaphoreType.DMA((2,)),
        ],
        flops=2 * 2 * boxes * rows * kpg,
    )[0]


def operators_of_lists(sources, offsets, counts, table, order, back):
    slots, boxes = offsets.shape
    operators, _, half = table.shape
    lanes = 2 * half

    def body(ins, outs, rest):
        src_in, off_in, cnt_in, tab_in = ins
        coef_ref, lane_ref = outs
        family = boxes // len(order)
        src = src_in()[...]
        home = src // family
        moved = src
        for n, index in enumerate(order):
            moved = jnp.where(home == index, src + (n - index) * family, moved)
        off = jnp.where(iota((slots, boxes), 0) < cnt_in()[...], off_in()[...], -1)
        src, off = (
            jnp.concatenate([x.T[index * family : (index + 1) * family] for index in back], axis=0)
            for x in (moved, off)
        )
        size = slots * CHUNK
        tables = jnp.swapaxes(tab_in()[...], 0, 1)
        flat = jnp.concatenate([tables[0], tables[1]], axis=1)
        for chunk in range(boxes // CHUNK):
            rows = slice(chunk * CHUNK, (chunk + 1) * CHUNK)
            pick = jnp.concatenate(
                [ones_where(off[rows, m : m + 1] == iota((CHUNK, operators), 1)) for m in range(slots)], axis=0
            )
            coef_ref[chunk * size : (chunk + 1) * size] = nn(pick, flat).astype(bf16)
            for m in range(slots):
                at = chunk * size + m * CHUNK
                lane_ref[at : at + CHUNK] = jnp.broadcast_to(src[rows, m : m + 1], (CHUNK, LANES)).astype(jnp.int16)

    return call(
        body,
        [sources, offsets, counts, table],
        [H, H, H, H],
        [((slots * boxes, lanes), bf16, V), ((slots * boxes, LANES), jnp.int16, V)],
        "operators_of_lists",
        flops=2 * slots * boxes * operators * lanes,
    )


def parent_sums(pattern, sources, coef, slots):
    total, lanes = pattern.shape
    half = lanes // 2
    size = slots * CHUNK
    chunks = total // CHUNK
    halves = 2

    def body(ins, outs, rest):
        pat_ref, src_ref, coef_ref = ins
        (out_hbm,) = outs
        pick_ref, out_ref, sems = rest
        one, zero = jnp.ones((), bf16), jnp.zeros((), bf16)
        for chunk in range(chunks):
            part = slice(chunk * size, (chunk + 1) * size)
            src = src_ref[part]
            lane = lax.broadcasted_iota(jnp.int16, src.shape, 1)
            hot = jnp.concatenate(
                [jnp.where(src == lane + jnp.int16(at), one, zero) for at in range(0, total, LANES)], axis=1
            )
            pick_ref[part] = nn(hot, pat_ref[...])
        copies = []
        for chunk in range(chunks):
            real = imag = 0.0
            for m in range(slots):
                part = slice(chunk * size + m * CHUNK, chunk * size + (m + 1) * CHUNK)
                pr, pi = pick_ref[part, :half], pick_ref[part, half:]
                c = coef_ref[part].astype(f32)
                cr, ci = c[:, :half], c[:, half:]
                real += cr * pr - ci * pi
                imag += cr * pi + ci * pr
            rows = slice(chunk * CHUNK, (chunk + 1) * CHUNK)
            out_ref[rows, :half] = real.astype(bf16)
            out_ref[rows, half:] = imag.astype(bf16)
            if (chunk + 1) % (chunks // halves) == 0:
                part = pl.ds(len(copies) * (total // halves), total // halves)
                copies.append(
                    pltpu.make_async_copy(out_ref.at[part], out_hbm.at[part], sems.at[len(copies)])
                )
                copies[-1].start()
        for copy in copies:
            copy.wait()

    return call(
        body,
        [pattern, sources, coef],
        [V, V, V],
        [((total, lanes), bf16, H)],
        "parent_sums",
        scratch=[
            pltpu.VMEM((slots * total, lanes), f32),
            pltpu.VMEM((total, lanes), bf16),
            pltpu.SemaphoreType.DMA((halves,)),
        ],
        flops=2 * slots * total * total * lanes,
        limit=24 << 20,
    )[0]


def lower(far, parent, octant, phases, weights, parents, rim, order):
    boxes = parent.shape[1]
    rows, kpg = weights.shape
    packed = order is not None
    width = LANES if packed else 256

    def body(ins, outs, rest):
        far_ref, par_ref, oct_ref, phase_ref, w_ref = ins
        low_ref, rim_ref = outs
        base = lax.axis_index("box") * parents
        hot = ones_where(iota((parents, boxes), 0) == par_ref[...] - base).T
        onehot = octant_rows(oct_ref[...], boxes).T
        for step in range(kpg // width):
            cols = slice(step * width, (step + 1) * width)
            if packed:
                at = order.index(step) * parents
                spread = nn(hot, far_ref[at : at + parents])
                sr, si = spread[:, :LANES], spread[:, LANES:]
            else:
                sr, si = nn(hot, far_ref[0, :, cols]), nn(hot, far_ref[1, :, cols])
            both = nn(
                onehot,
                jnp.concatenate(
                    [phase_rows(phase_ref[:OCTANTS, cols]), phase_rows(phase_ref[OCTANTS:, cols])], axis=1
                ),
            )
            c, s = both[:, :width], both[:, width:]
            low_ref[:boxes, cols] = (sr * c + si * s).astype(bf16)
            low_ref[boxes:, cols] = (si * c - sr * s).astype(bf16)
        ends = jnp.concatenate([w_ref[:rim], w_ref[rows - rim :]], axis=0)
        terms = nt(ends, low_ref[...]).astype(bf16)
        for side in range(2):
            for r in range(2):
                rim_ref[side, r] = terms[side * rim : (side + 1) * rim, r * boxes : (r + 1) * boxes]

    return call(
        body,
        [far, parent, octant, phases, weights],
        [V, V, V, V, V],
        [((2 * boxes, kpg), bf16, V), ((2, 2, rim, boxes), bf16, V)],
        "lower",
        flops=2 * 2 * boxes * kpg * 2 * rim,
    )


def anterpolate(weights, lowered, nearby, rim):
    _, kcg, boxes = nearby.shape

    def body(ins, outs, rest):
        w_ref, low_ref, near_ref = ins
        (out_ref,) = outs
        terms = nt(w_ref[rim : rim + kcg], low_ref[...]).astype(bf16).astype(f32)
        for r in range(2):
            out_ref[r] = near_ref[r] + terms[:, r * boxes : (r + 1) * boxes]

    return call(
        body,
        [weights, lowered, nearby],
        [V, V, V],
        [(nearby.shape, f32, V)],
        "anterpolate",
        flops=2 * kcg * weights.shape[1] * 2 * boxes,
    )[0]


def finish(partial, start_terms, end_terms):
    _, kcg, boxes = partial.shape
    rim = start_terms[0].shape[-2]
    arrays = [start_terms[0]] if end_terms[0] is start_terms[0] else [start_terms[0], end_terms[0]]

    def body(ins, outs, rest):
        sum_ref, start_ref, end_ref = ins[0], ins[1], ins[-1]
        (out_ref,) = outs
        start = start_ref[...] if start_terms[1] is None else start_ref[start_terms[1]]
        end = end_ref[...] if end_terms[1] is None else end_ref[end_terms[1]]
        out_ref[:, rim : kcg - rim] = sum_ref[:, rim : kcg - rim].astype(bf16)
        out_ref[:, :rim] = (sum_ref[:, :rim] + start.astype(f32)).astype(bf16)
        out_ref[:, kcg - rim :] = (sum_ref[:, kcg - rim :] + end.astype(f32)).astype(bf16)

    return call(
        body, [partial, *arrays], [V] * (1 + len(arrays)), [(partial.shape, bf16, None)], "finish"
    )[0]


def near_sums(own, lead, trail, sources, offsets, counts, table, phase):
    _, kcg, boxes = own.shape
    kpg = phase.shape[2]
    slots = sources.shape[0]
    operators = table.shape[0]
    depth = 2 * boxes
    pair = 2

    def body(ins, outs, rest):
        own_in, lead_in, trail_in, src_in, off_in, cnt_in, tab_in, ph_in = ins
        out_ref, phase_ref = outs
        ext_ref, tt_ref, dense_ref = rest
        dense_ref[...] = ph_in()[:, 0, :]
        sine, cosine = sincos(dense_ref[...])
        phase_ref[:OCTANTS] = cosine
        phase_ref[OCTANTS:] = sine
        eye = identity(boxes)
        own_ref = own_in()
        tables = jnp.swapaxes(tab_in()[...], 0, 1)
        for r in range(2):
            rows = slice(r * kcg, (r + 1) * kcg)
            ext_ref[rows, :boxes] = own_ref[r]
            for step in range(kcg // boxes):
                cols = slice(step * boxes, (step + 1) * boxes)
                part = slice(r * kcg + step * boxes, r * kcg + (step + 1) * boxes)
                tt_ref[part] = nt(eye, tables[r, :, cols]).astype(bf16)
        lead_ref, trail_ref = lead_in(), trail_in()
        for r in range(2):
            for step in range(kcg // boxes):
                cols = slice(step * boxes, (step + 1) * boxes)
                part = slice(r * kcg + step * boxes, r * kcg + (step + 1) * boxes)
                halo = jnp.concatenate(
                    [lead_ref[r, :, cols], trail_ref[r, :, cols], jnp.zeros((boxes - 2 * NEARB, boxes), bf16)],
                    axis=0,
                )
                ext_ref[part, boxes:] = nt(eye, halo).astype(bf16)
        me = lax.axis_index("box")
        odd = lax.rem(me, 2)
        rel = src_in()[...] - me * boxes
        below = rel + (boxes + NEARB) + (1 - odd) * NEARB
        above = rel + odd * NEARB
        rel = jnp.where(rel < 0, below, jnp.where(rel >= boxes, above, rel))
        off = jnp.where(iota((slots, boxes), 0) < cnt_in()[...], off_in()[...], -1)
        for m in range(0, slots, pair):
            src = jnp.concatenate([rel[m + j : m + j + 1] for j in range(pair)], axis=1)
            ops = jnp.concatenate([off[m + j : m + j + 1] for j in range(pair)], axis=1)
            hot = ones_where(iota((depth, pair * boxes), 0) == src)
            pick = ones_where(iota((operators, pair * boxes), 0) == ops)
            picked = nn(ext_ref[...], hot)
            coef = nn(tt_ref[...], pick)
            pr, pi, cr, ci = picked[:kcg], picked[kcg:], coef[:kcg], coef[kcg:]
            real, imag = cr * pr - ci * pi, cr * pi + ci * pr
            for r, value in enumerate((real, imag)):
                value = sum(value[:, j * boxes : (j + 1) * boxes] for j in range(pair))
                out_ref[r] = value if m == 0 else out_ref[r] + value

    return call(
        body,
        [own, lead, trail, sources, offsets, counts, table, phase],
        [H] * 8,
        [(own.shape, f32, V), ((2 * OCTANTS, kpg), f32, V)],
        "near_sums",
        scratch=[
            pltpu.VMEM((2 * kcg, depth), bf16),
            pltpu.VMEM((2 * kcg, operators), bf16),
            pltpu.VMEM((OCTANTS, kpg), f32),
        ],
        flops=2 * slots * boxes * 2 * kcg * (depth + operators),
        limit=24 << 20,
    )


def plain_translate(pattern, table, sources, offsets, counts):
    coef = jnp.transpose(table, (0, 2, 1))

    def advance(m, summed):
        src = lax.dynamic_index_in_dim(sources, m, 0, keepdims=False)
        off = lax.dynamic_index_in_dim(offsets, m, 0, keepdims=False)
        p = pattern[:, :, src].astype(f32)
        c = coef[:, :, off].astype(f32) * (m < counts).astype(f32)
        return summed + jnp.stack([c[0] * p[0] - c[1] * p[1], c[0] * p[1] + c[1] * p[0]])

    return lax.fori_loop(
        0, sources.shape[0], advance, jnp.zeros(pattern.shape[:2] + (sources.shape[1],), f32)
    )


def ring(peers):
    gray = [i ^ (i >> 1) for i in range(peers)]
    if sorted(gray) != list(range(peers)):
        return list(range(peers))
    middle = gray.index((peers // 2 + 1) % peers)
    return gray[middle:] + gray[:middle]


def regroup(value, order):
    return lax.all_to_all(
        value, "box", split_axis=0, concat_axis=0, tiled=True, axis_index_groups=[list(order)]
    )


def shift(value, axis, step):
    peers = lax.axis_size(axis)
    return lax.ppermute(value, axis, [(i, (i + step) % peers) for i in range(peers)])


def exchange(value, axis, first):
    peers = lax.axis_size(axis)
    pairs = [(i, i + 1) for i in range(first, peers - 1, 2)]
    return lax.ppermute(value, axis, pairs + [(j, i) for i, j in pairs])


def local(
    child_pattern,
    child_parent,
    child_octant,
    child_sources,
    child_offsets,
    child_counts,
    parent_sources,
    parent_offsets,
    parent_counts,
    interp_weights,
    shift_phase,
    child_table,
    parent_table,
):
    own = child_pattern[:, 0]
    _, kcg, boxes = own.shape
    rim = (interp_weights.shape[0] - kcg) // 2
    peers, groups = lax.axis_size("box"), lax.axis_size("samp")
    total = parent_sources.shape[0]
    parents = total // peers
    kpg = interp_weights.shape[1]
    mine = kpg // peers
    packed = mine == LANES and total % CHUNK == 0
    order, back = (ring(peers), ring(peers)) if packed else (None, None)
    parent, octant = child_parent[None, :], child_octant[None, :]

    if groups == 2:
        rims = [shift(own, "samp", 1)]
        spans = ((0, kcg - rim, kcg), (0, 0, rim))
    else:
        rims = [shift(own[:, kcg - rim :], "samp", 1), shift(own[:, :rim], "samp", -1)]
        spans = ((0, 0, rim), (1, 0, rim))
    cosine, sine, inner, family, weights, lead, trail = prepare(
        own, octant, parent, shift_phase, interp_weights, parents
    )
    pattern = rise(rims, spans, family, cosine, sine, inner, weights, parents, order)
    lead, trail = exchange(lead, "box", 0), exchange(trail, "box", 1)

    table = parent_table[:, :, 0, :]
    if packed:
        regrouped = regroup(pattern, order)
        coef, sources = operators_of_lists(
            parent_sources.T, parent_offsets.T, parent_counts[None, :], jnp.swapaxes(table, 0, 1), order, back
        )
        far = parent_sums(regrouped, sources, coef, parent_sources.shape[1])
        far, lead, trail = lax.optimization_barrier((far, lead, trail))
        returned = regroup(far, back)
    else:
        regrouped = lax.all_to_all(pattern, "box", split_axis=2, concat_axis=1, tiled=True)
        far = plain_translate(
            jnp.transpose(regrouped, (0, 2, 1)), table, parent_sources.T, parent_offsets.T, parent_counts
        ).astype(bf16)
        far = jnp.transpose(far, (0, 2, 1))
        returned = lax.all_to_all(far, "box", split_axis=1, concat_axis=2, tiled=True)

    nearby, phases = near_sums(
        own,
        lead,
        trail,
        child_sources.T,
        child_offsets.T,
        child_counts[None, :],
        jnp.swapaxes(child_table[:, :, 0, :], 0, 1),
        shift_phase,
    )
    returned, nearby = lax.optimization_barrier((returned, nearby))
    lowered, terms = lower(returned, parent, octant, phases, interp_weights, parents, rim, back)
    if groups == 2:
        got = shift(terms, "samp", 1)
        start_terms, end_terms = (got, 1), (got, 0)
    else:
        start_terms = (shift(terms[1], "samp", 1), None)
        end_terms = (shift(terms[0], "samp", -1), None)
    partial = anterpolate(interp_weights, lowered, nearby, rim)
    return finish(partial, start_terms, end_terms)[:, None]


def solution(mesh):
    return jax.shard_map(
        local,
        mesh=mesh,
        in_specs=(
            P(None, "samp", None, "box"),
            P("box"),
            P("box"),
            P("box", None),
            P("box", None),
            P("box"),
            P(),
            P(),
            P(),
            P(),
            P(None, "samp", None),
            P(None, None, "samp", None),
            P(None, None, "samp", "box"),
        ),
        out_specs=P(None, "samp", None, "box"),
        check_vma=False,
    )
```

```python
import jax
import jax.numpy as jnp
from jax import lax
from jax.experimental import pallas as pl
from jax.experimental.pallas import tpu as pltpu
from jax.sharding import PartitionSpec as P

NEARB = 32
OCTANTS = 8
LANES = 128
CHUNK = 128
f32, bf16, i32 = jnp.float32, jnp.bfloat16, jnp.int32
V, H = pltpu.VMEM, pltpu.HBM


class Fetched:
    def __init__(self, source, room, semaphore):
        self.copy = pltpu.make_async_copy(source, room, semaphore)
        self.room, self.waited = room, False
        self.copy.start()

    def __call__(self):
        if not self.waited:
            self.copy.wait()
            self.waited = True
        return self.room


def call(body, args, places, outs, name, rooms=(), scratch=(), flops=1 << 20, moved=1 << 20, limit=16 << 20):
    rooms = dict(rooms)
    fetched = [i for i, place in enumerate(places) if place is H and rooms.get(i, 0) is not None]
    spaces = [
        pltpu.VMEM(rooms.get(i, args[i].shape), args[i].dtype) for i in fetched
    ]

    def kernel(*refs):
        ins = list(refs[: len(args)])
        results = refs[len(args) : len(args) + len(outs)]
        rest = refs[len(args) + len(outs) :]
        held, rest = rest[: len(fetched)], rest[len(fetched) :]
        if fetched:
            semaphores, rest = rest[0], rest[1:]
            for n, i in enumerate(fetched):
                ins[i] = Fetched(ins[i], held[n], semaphores.at[n])
        body(ins, results, rest)

    semaphores = [pltpu.SemaphoreType.DMA((len(fetched),))] if fetched else []
    args = [
        pltpu.with_memory_space_constraint(arg, H) if place is H else arg for arg, place in zip(args, places)
    ]
    return pl.pallas_call(
        kernel,
        out_shape=[
            jax.ShapeDtypeStruct(shape, dtype) if place is None else place(shape, dtype)
            for shape, dtype, place in outs
        ],
        in_specs=[pl.BlockSpec(memory_space=place) for place in places],
        out_specs=[pl.BlockSpec(memory_space=place or V) for _, _, place in outs],
        scratch_shapes=spaces + semaphores + list(scratch),
        name=name,
        cost_estimate=pl.CostEstimate(flops=flops, bytes_accessed=moved, transcendentals=0),
        compiler_params=pltpu.CompilerParams(vmem_limit_bytes=limit),
    )(*args)


def nt(a, b):
    return lax.dot_general(a, b, (((1,), (1,)), ((), ())), preferred_element_type=f32)


def tn(a, b):
    return lax.dot_general(a, b, (((0,), (0,)), ((), ())), preferred_element_type=f32)


def nn(a, b):
    return lax.dot_general(a, b, (((1,), (0,)), ((), ())), preferred_element_type=f32)


def iota(shape, dim):
    return lax.broadcasted_iota(i32, shape, dim)


def ones_where(mask):
    return jnp.where(mask, 1.0, 0.0).astype(bf16)


def identity(n):
    return ones_where(iota((n, n), 0) == iota((n, n), 1))


def sincos(x):
    h = 0.5 * x
    q = h * h
    s = -2.50521083854417e-08 + q * 1.60590438368216e-10
    s = 2.75573192239859e-06 + q * s
    s = -1.98412698412698e-04 + q * s
    s = 8.33333333333333e-03 + q * s
    s = -1.66666666666667e-01 + q * s
    s = h + h * (q * s)
    c = 2.08767569878681e-09 + q * -1.14707455977297e-11
    c = -2.75573192239859e-07 + q * c
    c = 2.48015873015873e-05 + q * c
    c = -1.38888888888889e-03 + q * c
    c = 4.16666666666667e-02 + q * c
    c = -0.5 + q * c
    c = 1.0 + q * c
    return 2.0 * (s * c), 1.0 - 2.0 * (s * s)


def parts(x):
    high = x.astype(bf16)
    rest = x - high.astype(f32)
    middle = rest.astype(bf16)
    return [high, middle, (rest - middle.astype(f32)).astype(bf16)]


def phase_rows(x):
    return jnp.concatenate(parts(x) + [jnp.zeros(x.shape, bf16)], axis=0)


def octant_rows(octant, boxes):
    onehot = ones_where(iota((OCTANTS, boxes), 0) == octant)
    return jnp.concatenate([onehot] * 4, axis=0)


def prepare(own, octant, parent, phase, weights, parents):
    _, kcg, boxes = own.shape
    kpg = phase.shape[2]

    def body(ins, outs, rest):
        own_in, oct_in, par_in, ph_in, w_hbm = ins
        cos_ref, sin_ref, e_ref, family_ref, w_ref, lead_out, trail_out = outs
        phase_ref, sems = rest
        fill = pltpu.make_async_copy(w_hbm, w_ref, sems.at[4])
        fill.start()
        eye = identity(boxes)
        me = lax.axis_index("box")
        family = ones_where(iota((parents, boxes), 0) == par_in()[...] - me * parents)
        family_ref[...] = jnp.concatenate([family, family], axis=1)
        onehot = octant_rows(oct_in()[...], boxes)
        phases = ph_in()
        room = own_in()
        for r in range(2):
            e_ref[r * boxes : (r + 1) * boxes] = nt(eye, room[r]).astype(bf16)
        odd = lax.rem(me, 2)
        copies = []
        for n, out in enumerate((lead_out, trail_out)):
            begin = pl.multiple_of(jnp.where(odd == n, boxes - NEARB, 0), NEARB)
            for r in range(2):
                copies.append(
                    pltpu.make_async_copy(
                        e_ref.at[pl.ds(r * boxes + begin, NEARB)], out.at[r], sems.at[2 * n + r]
                    )
                )
        for copy in copies:
            copy.start()
        phase_ref[...] = phases[:, 0, :]
        sine, cosine = sincos(phase_ref[...])
        cos_ref[...] = tn(onehot, phase_rows(cosine))
        sin_ref[...] = tn(onehot, phase_rows(sine))
        for copy in copies + [fill]:
            copy.wait()

    wave = ((boxes, kpg), f32, V)
    edge = ((2, NEARB, kcg), bf16, H)
    return call(
        body,
        [own, octant, parent, phase, weights],
        [H] * 5,
        [
            wave,
            wave,
            ((2 * boxes, kcg), bf16, V),
            ((parents, 2 * boxes), bf16, V),
            (weights.shape, bf16, V),
            edge,
            edge,
        ],
        "prepare",
        rooms={4: None},
        scratch=[pltpu.VMEM((OCTANTS, kpg), f32), pltpu.SemaphoreType.DMA((5,))],
    )


def rise(rims, spans, family, cosine, sine, inner, weights, parents, order):
    boxes, kpg = cosine.shape
    rows = weights.shape[0]
    rim = spans[0][2] - spans[0][1]
    width = 512
    packed = order is not None
    shape = (kpg // LANES * parents, 2 * LANES) if packed else (2, parents, kpg)

    def body(ins, outs, rest):
        sides = ins[: len(rims)]
        family_ref, cos_ref, sin_ref, inner_ref, w_ref = ins[len(rims) :]
        (out_hbm,) = outs
        out_ref, e_ref, shift_ref, sems = rest
        eye = identity(boxes)
        for r in range(2):
            part = slice(r * boxes, (r + 1) * boxes)
            before, after = (nt(eye, sides[n][r, low:high, :]).astype(bf16) for n, low, high in spans)
            e_ref[part] = jnp.concatenate([before, inner_ref[part], after], axis=1)
        for step in range(kpg // width):
            cols = slice(step * width, (step + 1) * width)
            y = nn(e_ref[...], w_ref[:, cols])
            yr, yi, c, s = y[:boxes], y[boxes:], cos_ref[:, cols], sin_ref[:, cols]
            for r, value in enumerate((yr * c - yi * s, yr * s + yi * c)):
                high = value.astype(bf16)
                shift_ref[r, :boxes, cols] = high
                shift_ref[r, boxes:, cols] = (value - high.astype(f32)).astype(bf16)
        copies = []
        pieces = kpg // LANES
        for n in range(pieces):
            piece = order[n] if packed else n
            cols = slice(piece * LANES, (piece + 1) * LANES)
            both = nn(family_ref[...], jnp.concatenate([shift_ref[0, :, cols], shift_ref[1, :, cols]], axis=1))
            both = both.astype(bf16)
            if packed:
                out_ref[n * parents : (n + 1) * parents] = both
            else:
                out_ref[0, :, cols], out_ref[1, :, cols] = both[:, :LANES], both[:, LANES:]
            if (n + 1) * 2 % pieces == 0:
                if packed:
                    part = pl.ds(len(copies) * (shape[0] // 2), shape[0] // 2)
                    pair = out_ref.at[part], out_hbm.at[part]
                else:
                    part = pl.ds(len(copies) * (kpg // 2), kpg // 2)
                    pair = out_ref.at[:, :, part], out_hbm.at[:, :, part]
                copies.append(pltpu.make_async_copy(*pair, sems.at[len(copies)]))
                copies[-1].start()
        for copy in copies:
            copy.wait()

    return call(
        body,
        [*rims, family, cosine, sine, inner, weights],
        [V] * (len(rims) + 5),
        [(shape, bf16, H)],
        "rise",
        scratch=[
            pltpu.VMEM(shape, bf16),
            pltpu.VMEM((2 * boxes, rows), bf16),
            pltpu.VMEM((2, 2 * boxes, kpg), bf16),
            pltpu.SemaphoreType.DMA((2,)),
        ],
        flops=2 * 2 * boxes * rows * kpg,
    )[0]


def operators_of_lists(sources, offsets, counts, table, order, back):
    slots, boxes = offsets.shape
    operators, _, half = table.shape
    lanes = 2 * half

    def body(ins, outs, rest):
        src_in, off_in, cnt_in, tab_in = ins
        coef_ref, lane_ref = outs
        family = boxes // len(order)
        src = src_in()[...]
        home = src // family
        moved = src
        for n, index in enumerate(order):
            moved = jnp.where(home == index, src + (n - index) * family, moved)
        off = jnp.where(iota((slots, boxes), 0) < cnt_in()[...], off_in()[...], -1)
        src, off = (
            jnp.concatenate([x.T[index * family : (index + 1) * family] for index in back], axis=0)
            for x in (moved, off)
        )
        size = slots * CHUNK
        tables = jnp.swapaxes(tab_in()[...], 0, 1)
        flat = jnp.concatenate([tables[0], tables[1]], axis=1)
        for chunk in range(boxes // CHUNK):
            rows = slice(chunk * CHUNK, (chunk + 1) * CHUNK)
            pick = jnp.concatenate(
                [ones_where(off[rows, m : m + 1] == iota((CHUNK, operators), 1)) for m in range(slots)], axis=0
            )
            coef_ref[chunk * size : (chunk + 1) * size] = nn(pick, flat).astype(bf16)
            for m in range(slots):
                at = chunk * size + m * CHUNK
                lane_ref[at : at + CHUNK] = jnp.broadcast_to(src[rows, m : m + 1], (CHUNK, LANES)).astype(jnp.int16)

    return call(
        body,
        [sources, offsets, counts, table],
        [H, H, H, H],
        [((slots * boxes, lanes), bf16, V), ((slots * boxes, LANES), jnp.int16, V)],
        "operators_of_lists",
        flops=2 * slots * boxes * operators * lanes,
    )


def parent_sums(pattern, sources, coef, slots):
    total, lanes = pattern.shape
    half = lanes // 2
    size = slots * CHUNK
    chunks = total // CHUNK
    halves = 2

    def body(ins, outs, rest):
        pat_ref, src_ref, coef_ref = ins
        (out_hbm,) = outs
        pick_ref, out_ref, sems = rest
        one, zero = jnp.ones((), bf16), jnp.zeros((), bf16)
        for chunk in range(chunks):
            part = slice(chunk * size, (chunk + 1) * size)
            src = src_ref[part]
            lane = lax.broadcasted_iota(jnp.int16, src.shape, 1)
            hot = jnp.concatenate(
                [jnp.where(src == lane + jnp.int16(at), one, zero) for at in range(0, total, LANES)], axis=1
            )
            pick_ref[part] = nn(hot, pat_ref[...])
        copies = []
        for chunk in range(chunks):
            real = imag = 0.0
            for m in range(slots):
                part = slice(chunk * size + m * CHUNK, chunk * size + (m + 1) * CHUNK)
                pr, pi = pick_ref[part, :half], pick_ref[part, half:]
                c = coef_ref[part].astype(f32)
                cr, ci = c[:, :half], c[:, half:]
                real += cr * pr - ci * pi
                imag += cr * pi + ci * pr
            rows = slice(chunk * CHUNK, (chunk + 1) * CHUNK)
            out_ref[rows, :half] = real.astype(bf16)
            out_ref[rows, half:] = imag.astype(bf16)
            if (chunk + 1) % (chunks // halves) == 0:
                part = pl.ds(len(copies) * (total // halves), total // halves)
                copies.append(
                    pltpu.make_async_copy(out_ref.at[part], out_hbm.at[part], sems.at[len(copies)])
                )
                copies[-1].start()
        for copy in copies:
            copy.wait()

    return call(
        body,
        [pattern, sources, coef],
        [V, V, V],
        [((total, lanes), bf16, H)],
        "parent_sums",
        scratch=[
            pltpu.VMEM((slots * total, lanes), f32),
            pltpu.VMEM((total, lanes), bf16),
            pltpu.SemaphoreType.DMA((halves,)),
        ],
        flops=2 * slots * total * total * lanes,
        limit=24 << 20,
    )[0]


def lower(far, parent, octant, phases, weights, parents, rim, order):
    boxes = parent.shape[1]
    rows, kpg = weights.shape
    packed = order is not None
    width = LANES if packed else 256

    def body(ins, outs, rest):
        far_ref, par_ref, oct_ref, phase_ref, w_ref = ins
        low_ref, rim_ref = outs
        base = lax.axis_index("box") * parents
        hot = ones_where(iota((parents, boxes), 0) == par_ref[...] - base).T
        onehot = octant_rows(oct_ref[...], boxes).T
        for step in range(kpg // width):
            cols = slice(step * width, (step + 1) * width)
            if packed:
                at = order.index(step) * parents
                spread = nn(hot, far_ref[at : at + parents])
                sr, si = spread[:, :LANES], spread[:, LANES:]
            else:
                sr, si = nn(hot, far_ref[0, :, cols]), nn(hot, far_ref[1, :, cols])
            both = nn(
                onehot,
                jnp.concatenate(
                    [phase_rows(phase_ref[:OCTANTS, cols]), phase_rows(phase_ref[OCTANTS:, cols])], axis=1
                ),
            )
            c, s = both[:, :width], both[:, width:]
            low_ref[:boxes, cols] = (sr * c + si * s).astype(bf16)
            low_ref[boxes:, cols] = (si * c - sr * s).astype(bf16)
        ends = jnp.concatenate([w_ref[:rim], w_ref[rows - rim :]], axis=0)
        terms = nt(ends, low_ref[...]).astype(bf16)
        for side in range(2):
            for r in range(2):
                rim_ref[side, r] = terms[side * rim : (side + 1) * rim, r * boxes : (r + 1) * boxes]

    return call(
        body,
        [far, parent, octant, phases, weights],
        [V, V, V, V, V],
        [((2 * boxes, kpg), bf16, V), ((2, 2, rim, boxes), bf16, V)],
        "lower",
        flops=2 * 2 * boxes * kpg * 2 * rim,
    )


def anterpolate(weights, lowered, nearby, rim):
    _, kcg, boxes = nearby.shape

    def body(ins, outs, rest):
        w_ref, low_ref, near_ref = ins
        (out_ref,) = outs
        terms = nt(w_ref[rim : rim + kcg], low_ref[...]).astype(bf16).astype(f32)
        for r in range(2):
            out_ref[r] = near_ref[r] + terms[:, r * boxes : (r + 1) * boxes]

    return call(
        body,
        [weights, lowered, nearby],
        [V, V, V],
        [(nearby.shape, f32, V)],
        "anterpolate",
        flops=2 * kcg * weights.shape[1] * 2 * boxes,
    )[0]


def finish(partial, start_terms, end_terms):
    _, kcg, boxes = partial.shape
    rim = start_terms[0].shape[-2]
    arrays = [start_terms[0]] if end_terms[0] is start_terms[0] else [start_terms[0], end_terms[0]]

    def body(ins, outs, rest):
        sum_ref, start_ref, end_ref = ins[0], ins[1], ins[-1]
        (out_ref,) = outs
        start = start_ref[...] if start_terms[1] is None else start_ref[start_terms[1]]
        end = end_ref[...] if end_terms[1] is None else end_ref[end_terms[1]]
        out_ref[:, rim : kcg - rim] = sum_ref[:, rim : kcg - rim].astype(bf16)
        out_ref[:, :rim] = (sum_ref[:, :rim] + start.astype(f32)).astype(bf16)
        out_ref[:, kcg - rim :] = (sum_ref[:, kcg - rim :] + end.astype(f32)).astype(bf16)

    return call(
        body, [partial, *arrays], [V] * (1 + len(arrays)), [(partial.shape, bf16, None)], "finish"
    )[0]


def near_sums(own, lead, trail, sources, offsets, counts, table, phase):
    _, kcg, boxes = own.shape
    kpg = phase.shape[2]
    slots = sources.shape[0]
    operators = table.shape[0]
    depth = 2 * boxes
    pair = 2

    def body(ins, outs, rest):
        own_in, lead_in, trail_in, src_in, off_in, cnt_in, tab_in, ph_in = ins
        out_ref, phase_ref = outs
        ext_ref, tt_ref, dense_ref = rest
        dense_ref[...] = ph_in()[:, 0, :]
        sine, cosine = sincos(dense_ref[...])
        phase_ref[:OCTANTS] = cosine
        phase_ref[OCTANTS:] = sine
        eye = identity(boxes)
        own_ref = own_in()
        tables = jnp.swapaxes(tab_in()[...], 0, 1)
        for r in range(2):
            rows = slice(r * kcg, (r + 1) * kcg)
            ext_ref[rows, :boxes] = own_ref[r]
            for step in range(kcg // boxes):
                cols = slice(step * boxes, (step + 1) * boxes)
                part = slice(r * kcg + step * boxes, r * kcg + (step + 1) * boxes)
                tt_ref[part] = nt(eye, tables[r, :, cols]).astype(bf16)
        lead_ref, trail_ref = lead_in(), trail_in()
        for r in range(2):
            for step in range(kcg // boxes):
                cols = slice(step * boxes, (step + 1) * boxes)
                part = slice(r * kcg + step * boxes, r * kcg + (step + 1) * boxes)
                halo = jnp.concatenate(
                    [lead_ref[r, :, cols], trail_ref[r, :, cols], jnp.zeros((boxes - 2 * NEARB, boxes), bf16)],
                    axis=0,
                )
                ext_ref[part, boxes:] = nt(eye, halo).astype(bf16)
        me = lax.axis_index("box")
        odd = lax.rem(me, 2)
        rel = src_in()[...] - me * boxes
        below = rel + (boxes + NEARB) + (1 - odd) * NEARB
        above = rel + odd * NEARB
        rel = jnp.where(rel < 0, below, jnp.where(rel >= boxes, above, rel))
        off = jnp.where(iota((slots, boxes), 0) < cnt_in()[...], off_in()[...], -1)
        for m in range(0, slots, pair):
            src = jnp.concatenate([rel[m + j : m + j + 1] for j in range(pair)], axis=1)
            ops = jnp.concatenate([off[m + j : m + j + 1] for j in range(pair)], axis=1)
            hot = ones_where(iota((depth, pair * boxes), 0) == src)
            pick = ones_where(iota((operators, pair * boxes), 0) == ops)
            picked = nn(ext_ref[...], hot)
            coef = nn(tt_ref[...], pick)
            pr, pi, cr, ci = picked[:kcg], picked[kcg:], coef[:kcg], coef[kcg:]
            real, imag = cr * pr - ci * pi, cr * pi + ci * pr
            for r, value in enumerate((real, imag)):
                value = sum(value[:, j * boxes : (j + 1) * boxes] for j in range(pair))
                out_ref[r] = value if m == 0 else out_ref[r] + value

    return call(
        body,
        [own, lead, trail, sources, offsets, counts, table, phase],
        [H] * 8,
        [(own.shape, f32, V), ((2 * OCTANTS, kpg), f32, V)],
        "near_sums",
        scratch=[
            pltpu.VMEM((2 * kcg, depth), bf16),
            pltpu.VMEM((2 * kcg, operators), bf16),
            pltpu.VMEM((OCTANTS, kpg), f32),
        ],
        flops=2 * slots * boxes * 2 * kcg * (depth + operators),
        limit=24 << 20,
    )


def plain_translate(pattern, table, sources, offsets, counts):
    coef = jnp.transpose(table, (0, 2, 1))

    def advance(m, summed):
        src = lax.dynamic_index_in_dim(sources, m, 0, keepdims=False)
        off = lax.dynamic_index_in_dim(offsets, m, 0, keepdims=False)
        p = pattern[:, :, src].astype(f32)
        c = coef[:, :, off].astype(f32) * (m < counts).astype(f32)
        return summed + jnp.stack([c[0] * p[0] - c[1] * p[1], c[0] * p[1] + c[1] * p[0]])

    return lax.fori_loop(
        0, sources.shape[0], advance, jnp.zeros(pattern.shape[:2] + (sources.shape[1],), f32)
    )


def ring(peers):
    gray = [i ^ (i >> 1) for i in range(peers)]
    if sorted(gray) != list(range(peers)):
        return list(range(peers))
    middle = gray.index((peers // 2 + 1) % peers)
    return gray[middle:] + gray[:middle]


def regroup(value, order):
    return lax.all_to_all(
        value, "box", split_axis=0, concat_axis=0, tiled=True, axis_index_groups=[list(order)]
    )


def shift(value, axis, step):
    peers = lax.axis_size(axis)
    return lax.ppermute(value, axis, [(i, (i + step) % peers) for i in range(peers)])


def exchange(value, axis, first):
    peers = lax.axis_size(axis)
    pairs = [(i, i + 1) for i in range(first, peers - 1, 2)]
    return lax.ppermute(value, axis, pairs + [(j, i) for i, j in pairs])


def local(
    child_pattern,
    child_parent,
    child_octant,
    child_sources,
    child_offsets,
    child_counts,
    parent_sources,
    parent_offsets,
    parent_counts,
    interp_weights,
    shift_phase,
    child_table,
    parent_table,
):
    own = child_pattern[:, 0]
    _, kcg, boxes = own.shape
    rim = (interp_weights.shape[0] - kcg) // 2
    peers, groups = lax.axis_size("box"), lax.axis_size("samp")
    total = parent_sources.shape[0]
    parents = total // peers
    kpg = interp_weights.shape[1]
    mine = kpg // peers
    packed = mine == LANES and total % CHUNK == 0
    order, back = (ring(peers), ring(peers)) if packed else (None, None)
    parent, octant = child_parent[None, :], child_octant[None, :]

    if groups == 2:
        rims = [shift(own, "samp", 1)]
        spans = ((0, kcg - rim, kcg), (0, 0, rim))
    else:
        rims = [shift(own[:, kcg - rim :], "samp", 1), shift(own[:, :rim], "samp", -1)]
        spans = ((0, 0, rim), (1, 0, rim))
    cosine, sine, inner, family, weights, lead, trail = prepare(
        own, octant, parent, shift_phase, interp_weights, parents
    )
    pattern = rise(rims, spans, family, cosine, sine, inner, weights, parents, order)
    lead, trail = exchange(lead, "box", 0), exchange(trail, "box", 1)

    table = parent_table[:, :, 0, :]
    if packed:
        regrouped = regroup(pattern, order)
        coef, sources = operators_of_lists(
            parent_sources.T, parent_offsets.T, parent_counts[None, :], jnp.swapaxes(table, 0, 1), order, back
        )
        far = parent_sums(regrouped, sources, coef, parent_sources.shape[1])
        far, lead, trail = lax.optimization_barrier((far, lead, trail))
        returned = regroup(far, back)
    else:
        regrouped = lax.all_to_all(pattern, "box", split_axis=2, concat_axis=1, tiled=True)
        far = plain_translate(
            jnp.transpose(regrouped, (0, 2, 1)), table, parent_sources.T, parent_offsets.T, parent_counts
        ).astype(bf16)
        far = jnp.transpose(far, (0, 2, 1))
        returned = lax.all_to_all(far, "box", split_axis=1, concat_axis=2, tiled=True)

    nearby, phases = near_sums(
        own,
        lead,
        trail,
        child_sources.T,
        child_offsets.T,
        child_counts[None, :],
        jnp.swapaxes(child_table[:, :, 0, :], 0, 1),
        shift_phase,
    )
    returned, nearby = lax.optimization_barrier((returned, nearby))
    lowered, terms = lower(returned, parent, octant, phases, interp_weights, parents, rim, back)
    if groups == 2:
        got = shift(terms, "samp", 1)
        start_terms, end_terms = (got, 1), (got, 0)
    else:
        start_terms = (shift(terms[1], "samp", 1), None)
        end_terms = (shift(terms[0], "samp", -1), None)
    partial = anterpolate(interp_weights, lowered, nearby, rim)
    return finish(partial, start_terms, end_terms)[:, None]


def solution(mesh):
    return jax.shard_map(
        local,
        mesh=mesh,
        in_specs=(
            P(None, "samp", None, "box"),
            P("box"),
            P("box"),
            P("box", None),
            P("box", None),
            P("box"),
            P(),
            P(),
            P(),
            P(),
            P(None, "samp", None),
            P(None, None, "samp", None),
            P(None, None, "samp", "box"),
        ),
        out_specs=P(None, "samp", None, "box"),
        check_vma=False,
    )
```

```python
import jax
import jax.numpy as jnp
from jax import lax
from jax.experimental import pallas as pl
from jax.experimental.pallas import tpu as pltpu
from jax.sharding import PartitionSpec as P

NEARB = 32
OCTANTS = 8
LANES = 128
CHUNK = 128
f32, bf16, i32 = jnp.float32, jnp.bfloat16, jnp.int32
V, H = pltpu.VMEM, pltpu.HBM


class Fetched:
    def __init__(self, source, room, semaphore):
        self.copy = pltpu.make_async_copy(source, room, semaphore)
        self.room, self.waited = room, False
        self.copy.start()

    def __call__(self):
        if not self.waited:
            self.copy.wait()
            self.waited = True
        return self.room


def call(body, args, places, outs, name, rooms=(), scratch=(), flops=1 << 20, moved=1 << 20, limit=16 << 20):
    rooms = dict(rooms)
    fetched = [i for i, place in enumerate(places) if place is H and rooms.get(i, 0) is not None]
    spaces = [
        pltpu.VMEM(rooms.get(i, args[i].shape), args[i].dtype) for i in fetched
    ]

    def kernel(*refs):
        ins = list(refs[: len(args)])
        results = refs[len(args) : len(args) + len(outs)]
        rest = refs[len(args) + len(outs) :]
        held, rest = rest[: len(fetched)], rest[len(fetched) :]
        if fetched:
            semaphores, rest = rest[0], rest[1:]
            for n, i in enumerate(fetched):
                ins[i] = Fetched(ins[i], held[n], semaphores.at[n])
        body(ins, results, rest)

    semaphores = [pltpu.SemaphoreType.DMA((len(fetched),))] if fetched else []
    args = [
        pltpu.with_memory_space_constraint(arg, H) if place is H else arg for arg, place in zip(args, places)
    ]
    return pl.pallas_call(
        kernel,
        out_shape=[
            jax.ShapeDtypeStruct(shape, dtype) if place is None else place(shape, dtype)
            for shape, dtype, place in outs
        ],
        in_specs=[pl.BlockSpec(memory_space=place) for place in places],
        out_specs=[pl.BlockSpec(memory_space=place or V) for _, _, place in outs],
        scratch_shapes=spaces + semaphores + list(scratch),
        name=name,
        cost_estimate=pl.CostEstimate(flops=flops, bytes_accessed=moved, transcendentals=0),
        compiler_params=pltpu.CompilerParams(vmem_limit_bytes=limit),
    )(*args)


def nt(a, b):
    return lax.dot_general(a, b, (((1,), (1,)), ((), ())), preferred_element_type=f32)


def tn(a, b):
    return lax.dot_general(a, b, (((0,), (0,)), ((), ())), preferred_element_type=f32)


def nn(a, b):
    return lax.dot_general(a, b, (((1,), (0,)), ((), ())), preferred_element_type=f32)


def iota(shape, dim):
    return lax.broadcasted_iota(i32, shape, dim)


def ones_where(mask):
    return jnp.where(mask, 1.0, 0.0).astype(bf16)


def identity(n):
    return ones_where(iota((n, n), 0) == iota((n, n), 1))


def sincos(x):
    h = 0.5 * x
    q = h * h
    s = -2.50521083854417e-08 + q * 1.60590438368216e-10
    s = 2.75573192239859e-06 + q * s
    s = -1.98412698412698e-04 + q * s
    s = 8.33333333333333e-03 + q * s
    s = -1.66666666666667e-01 + q * s
    s = h + h * (q * s)
    c = 2.08767569878681e-09 + q * -1.14707455977297e-11
    c = -2.75573192239859e-07 + q * c
    c = 2.48015873015873e-05 + q * c
    c = -1.38888888888889e-03 + q * c
    c = 4.16666666666667e-02 + q * c
    c = -0.5 + q * c
    c = 1.0 + q * c
    return 2.0 * (s * c), 1.0 - 2.0 * (s * s)


def parts(x):
    high = x.astype(bf16)
    rest = x - high.astype(f32)
    middle = rest.astype(bf16)
    return [high, middle, (rest - middle.astype(f32)).astype(bf16)]


def phase_rows(x):
    return jnp.concatenate(parts(x) + [jnp.zeros(x.shape, bf16)], axis=0)


def octant_rows(octant, boxes):
    onehot = ones_where(iota((OCTANTS, boxes), 0) == octant)
    return jnp.concatenate([onehot] * 4, axis=0)


def prepare(own, octant, parent, phase, weights, parents):
    _, kcg, boxes = own.shape
    kpg = phase.shape[2]

    def body(ins, outs, rest):
        own_in, oct_in, par_in, ph_in, w_hbm = ins
        cos_ref, sin_ref, e_ref, family_ref, w_ref, lead_out, trail_out = outs
        phase_ref, sems = rest
        fill = pltpu.make_async_copy(w_hbm, w_ref, sems.at[4])
        fill.start()
        eye = identity(boxes)
        me = lax.axis_index("box")
        family = ones_where(iota((parents, boxes), 0) == par_in()[...] - me * parents)
        family_ref[...] = jnp.concatenate([family, family], axis=1)
        onehot = octant_rows(oct_in()[...], boxes)
        phases = ph_in()
        room = own_in()
        for r in range(2):
            e_ref[r * boxes : (r + 1) * boxes] = nt(eye, room[r]).astype(bf16)
        odd = lax.rem(me, 2)
        copies = []
        for n, out in enumerate((lead_out, trail_out)):
            begin = pl.multiple_of(jnp.where(odd == n, boxes - NEARB, 0), NEARB)
            for r in range(2):
                copies.append(
                    pltpu.make_async_copy(
                        e_ref.at[pl.ds(r * boxes + begin, NEARB)], out.at[r], sems.at[2 * n + r]
                    )
                )
        for copy in copies:
            copy.start()
        phase_ref[...] = phases[:, 0, :]
        sine, cosine = sincos(phase_ref[...])
        cos_ref[...] = tn(onehot, phase_rows(cosine))
        sin_ref[...] = tn(onehot, phase_rows(sine))
        for copy in copies + [fill]:
            copy.wait()

    wave = ((boxes, kpg), f32, V)
    edge = ((2, NEARB, kcg), bf16, H)
    return call(
        body,
        [own, octant, parent, phase, weights],
        [H] * 5,
        [
            wave,
            wave,
            ((2 * boxes, kcg), bf16, V),
            ((parents, 2 * boxes), bf16, V),
            (weights.shape, bf16, V),
            edge,
            edge,
        ],
        "prepare",
        rooms={4: None},
        scratch=[pltpu.VMEM((OCTANTS, kpg), f32), pltpu.SemaphoreType.DMA((5,))],
    )


def rise(rims, spans, family, cosine, sine, inner, weights, parents, order):
    boxes, kpg = cosine.shape
    rows = weights.shape[0]
    rim = spans[0][2] - spans[0][1]
    width = 256
    packed = order is not None
    shape = (kpg // LANES * parents, 2 * LANES) if packed else (2, parents, kpg)

    def body(ins, outs, rest):
        sides = ins[: len(rims)]
        family_ref, cos_ref, sin_ref, inner_ref, w_ref = ins[len(rims) :]
        (out_hbm,) = outs
        out_ref, e_ref, shift_ref, sems = rest
        eye = identity(boxes)
        for r in range(2):
            part = slice(r * boxes, (r + 1) * boxes)
            before, after = (nt(eye, sides[n][r, low:high, :]).astype(bf16) for n, low, high in spans)
            e_ref[part] = jnp.concatenate([before, inner_ref[part], after], axis=1)
        for step in range(kpg // width):
            cols = slice(step * width, (step + 1) * width)
            y = nn(e_ref[...], w_ref[:, cols])
            yr, yi, c, s = y[:boxes], y[boxes:], cos_ref[:, cols], sin_ref[:, cols]
            for r, value in enumerate((yr * c - yi * s, yr * s + yi * c)):
                high = value.astype(bf16)
                shift_ref[r, :boxes, cols] = high
                shift_ref[r, boxes:, cols] = (value - high.astype(f32)).astype(bf16)
        copies = []
        pieces = kpg // LANES
        for n in range(pieces):
            piece = order[n] if packed else n
            cols = slice(piece * LANES, (piece + 1) * LANES)
            both = nn(family_ref[...], jnp.concatenate([shift_ref[0, :, cols], shift_ref[1, :, cols]], axis=1))
            both = both.astype(bf16)
            if packed:
                out_ref[n * parents : (n + 1) * parents] = both
            else:
                out_ref[0, :, cols], out_ref[1, :, cols] = both[:, :LANES], both[:, LANES:]
            if (n + 1) * 2 % pieces == 0:
                if packed:
                    part = pl.ds(len(copies) * (shape[0] // 2), shape[0] // 2)
                    pair = out_ref.at[part], out_hbm.at[part]
                else:
                    part = pl.ds(len(copies) * (kpg // 2), kpg // 2)
                    pair = out_ref.at[:, :, part], out_hbm.at[:, :, part]
                copies.append(pltpu.make_async_copy(*pair, sems.at[len(copies)]))
                copies[-1].start()
        for copy in copies:
            copy.wait()

    return call(
        body,
        [*rims, family, cosine, sine, inner, weights],
        [V] * (len(rims) + 5),
        [(shape, bf16, H)],
        "rise",
        scratch=[
            pltpu.VMEM(shape, bf16),
            pltpu.VMEM((2 * boxes, rows), bf16),
            pltpu.VMEM((2, 2 * boxes, kpg), bf16),
            pltpu.SemaphoreType.DMA((2,)),
        ],
        flops=2 * 2 * boxes * rows * kpg,
    )[0]


def operators_of_lists(sources, offsets, counts, table, order, back):
    slots, boxes = offsets.shape
    operators, _, half = table.shape
    lanes = 2 * half

    def body(ins, outs, rest):
        src_in, off_in, cnt_in, tab_in = ins
        coef_ref, lane_ref = outs
        family = boxes // len(order)
        src = src_in()[...]
        home = src // family
        moved = src
        for n, index in enumerate(order):
            moved = jnp.where(home == index, src + (n - index) * family, moved)
        off = jnp.where(iota((slots, boxes), 0) < cnt_in()[...], off_in()[...], -1)
        src, off = (
            jnp.concatenate([x.T[index * family : (index + 1) * family] for index in back], axis=0)
            for x in (moved, off)
        )
        size = slots * CHUNK
        tables = jnp.swapaxes(tab_in()[...], 0, 1)
        flat = jnp.concatenate([tables[0], tables[1]], axis=1)
        for chunk in range(boxes // CHUNK):
            rows = slice(chunk * CHUNK, (chunk + 1) * CHUNK)
            pick = jnp.concatenate(
                [ones_where(off[rows, m : m + 1] == iota((CHUNK, operators), 1)) for m in range(slots)], axis=0
            )
            coef_ref[chunk * size : (chunk + 1) * size] = nn(pick, flat).astype(bf16)
            for m in range(slots):
                at = chunk * size + m * CHUNK
                lane_ref[at : at + CHUNK] = jnp.broadcast_to(src[rows, m : m + 1], (CHUNK, LANES)).astype(jnp.int16)

    return call(
        body,
        [sources, offsets, counts, table],
        [H, H, H, H],
        [((slots * boxes, lanes), bf16, V), ((slots * boxes, LANES), jnp.int16, V)],
        "operators_of_lists",
        flops=2 * slots * boxes * operators * lanes,
    )


def parent_sums(pattern, sources, coef, slots):
    total, lanes = pattern.shape
    half = lanes // 2
    size = slots * CHUNK
    chunks = total // CHUNK
    halves = 2

    def body(ins, outs, rest):
        pat_ref, src_ref, coef_ref = ins
        (out_hbm,) = outs
        pick_ref, out_ref, sems = rest
        one, zero = jnp.ones((), bf16), jnp.zeros((), bf16)
        for chunk in range(chunks):
            part = slice(chunk * size, (chunk + 1) * size)
            src = src_ref[part]
            lane = lax.broadcasted_iota(jnp.int16, src.shape, 1)
            hot = jnp.concatenate(
                [jnp.where(src == lane + jnp.int16(at), one, zero) for at in range(0, total, LANES)], axis=1
            )
            pick_ref[part] = nn(hot, pat_ref[...])
        copies = []
        for chunk in range(chunks):
            real = imag = 0.0
            for m in range(slots):
                part = slice(chunk * size + m * CHUNK, chunk * size + (m + 1) * CHUNK)
                pr, pi = pick_ref[part, :half], pick_ref[part, half:]
                c = coef_ref[part].astype(f32)
                cr, ci = c[:, :half], c[:, half:]
                real += cr * pr - ci * pi
                imag += cr * pi + ci * pr
            rows = slice(chunk * CHUNK, (chunk + 1) * CHUNK)
            out_ref[rows, :half] = real.astype(bf16)
            out_ref[rows, half:] = imag.astype(bf16)
            if (chunk + 1) % (chunks // halves) == 0:
                part = pl.ds(len(copies) * (total // halves), total // halves)
                copies.append(
                    pltpu.make_async_copy(out_ref.at[part], out_hbm.at[part], sems.at[len(copies)])
                )
                copies[-1].start()
        for copy in copies:
            copy.wait()

    return call(
        body,
        [pattern, sources, coef],
        [V, V, V],
        [((total, lanes), bf16, H)],
        "parent_sums",
        scratch=[
            pltpu.VMEM((slots * total, lanes), f32),
            pltpu.VMEM((total, lanes), bf16),
            pltpu.SemaphoreType.DMA((halves,)),
        ],
        flops=2 * slots * total * total * lanes,
        limit=24 << 20,
    )[0]


def lower(far, parent, octant, phases, weights, parents, rim, order):
    boxes = parent.shape[1]
    rows, kpg = weights.shape
    packed = order is not None
    width = LANES if packed else 256

    def body(ins, outs, rest):
        far_ref, par_ref, oct_ref, phase_ref, w_ref = ins
        low_ref, rim_ref = outs
        base = lax.axis_index("box") * parents
        hot = ones_where(iota((parents, boxes), 0) == par_ref[...] - base).T
        onehot = octant_rows(oct_ref[...], boxes).T
        for step in range(kpg // width):
            cols = slice(step * width, (step + 1) * width)
            if packed:
                at = order.index(step) * parents
                spread = nn(hot, far_ref[at : at + parents])
                sr, si = spread[:, :LANES], spread[:, LANES:]
            else:
                sr, si = nn(hot, far_ref[0, :, cols]), nn(hot, far_ref[1, :, cols])
            both = nn(
                onehot,
                jnp.concatenate(
                    [phase_rows(phase_ref[:OCTANTS, cols]), phase_rows(phase_ref[OCTANTS:, cols])], axis=1
                ),
            )
            c, s = both[:, :width], both[:, width:]
            low_ref[:boxes, cols] = (sr * c + si * s).astype(bf16)
            low_ref[boxes:, cols] = (si * c - sr * s).astype(bf16)
        ends = jnp.concatenate([w_ref[:rim], w_ref[rows - rim :]], axis=0)
        terms = nt(ends, low_ref[...]).astype(bf16)
        for side in range(2):
            for r in range(2):
                rim_ref[side, r] = terms[side * rim : (side + 1) * rim, r * boxes : (r + 1) * boxes]

    return call(
        body,
        [far, parent, octant, phases, weights],
        [V, V, V, V, V],
        [((2 * boxes, kpg), bf16, V), ((2, 2, rim, boxes), bf16, V)],
        "lower",
        flops=2 * 2 * boxes * kpg * 2 * rim,
    )


def anterpolate(weights, lowered, nearby, rim):
    _, kcg, boxes = nearby.shape

    def body(ins, outs, rest):
        w_ref, low_ref, near_ref = ins
        (out_ref,) = outs
        terms = nt(w_ref[rim : rim + kcg], low_ref[...]).astype(bf16).astype(f32)
        for r in range(2):
            out_ref[r] = near_ref[r] + terms[:, r * boxes : (r + 1) * boxes]

    return call(
        body,
        [weights, lowered, nearby],
        [V, V, V],
        [(nearby.shape, f32, V)],
        "anterpolate",
        flops=2 * kcg * weights.shape[1] * 2 * boxes,
    )[0]


def finish(partial, start_terms, end_terms):
    _, kcg, boxes = partial.shape
    rim = start_terms[0].shape[-2]
    arrays = [start_terms[0]] if end_terms[0] is start_terms[0] else [start_terms[0], end_terms[0]]

    spans = ((rim, kcg - 2 * rim), (0, rim), (kcg - rim, rim))

    def body(ins, outs, rest):
        sum_ref, start_ref, end_ref = ins[0], ins[1], ins[-1]
        (out_hbm,) = outs
        out_ref, sems = rest
        start = start_ref[...] if start_terms[1] is None else start_ref[start_terms[1]]
        end = end_ref[...] if end_terms[1] is None else end_ref[end_terms[1]]
        copies = []
        for n, ((at, size), terms) in enumerate(zip(spans, (None, start, end))):
            value = sum_ref[:, at : at + size]
            value = value if terms is None else value + terms.astype(f32)
            out_ref[:, at : at + size] = value.astype(bf16)
            part = pl.ds(at, size)
            copies.append(pltpu.make_async_copy(out_ref.at[:, part], out_hbm.at[:, part], sems.at[n]))
            copies[-1].start()
        for copy in copies:
            copy.wait()

    return call(
        body,
        [partial, *arrays],
        [V] * (1 + len(arrays)),
        [(partial.shape, bf16, H)],
        "finish",
        scratch=[pltpu.VMEM(partial.shape, bf16), pltpu.SemaphoreType.DMA((3,))],
    )[0]


def near_sums(own, lead, trail, sources, offsets, counts, table, phase):
    _, kcg, boxes = own.shape
    kpg = phase.shape[2]
    slots = sources.shape[0]
    operators = table.shape[0]
    depth = 2 * boxes
    pair = 2

    def body(ins, outs, rest):
        own_in, lead_in, trail_in, src_in, off_in, cnt_in, tab_in, ph_in = ins
        out_ref, phase_ref = outs
        ext_ref, tt_ref, dense_ref = rest
        dense_ref[...] = ph_in()[:, 0, :]
        sine, cosine = sincos(dense_ref[...])
        phase_ref[:OCTANTS] = cosine
        phase_ref[OCTANTS:] = sine
        eye = identity(boxes)
        own_ref = own_in()
        tables = jnp.swapaxes(tab_in()[...], 0, 1)
        for r in range(2):
            rows = slice(r * kcg, (r + 1) * kcg)
            ext_ref[rows, :boxes] = own_ref[r]
            for step in range(kcg // boxes):
                cols = slice(step * boxes, (step + 1) * boxes)
                part = slice(r * kcg + step * boxes, r * kcg + (step + 1) * boxes)
                tt_ref[part] = nt(eye, tables[r, :, cols]).astype(bf16)
        lead_ref, trail_ref = lead_in(), trail_in()
        for r in range(2):
            for step in range(kcg // boxes):
                cols = slice(step * boxes, (step + 1) * boxes)
                part = slice(r * kcg + step * boxes, r * kcg + (step + 1) * boxes)
                halo = jnp.concatenate(
                    [lead_ref[r, :, cols], trail_ref[r, :, cols], jnp.zeros((boxes - 2 * NEARB, boxes), bf16)],
                    axis=0,
                )
                ext_ref[part, boxes:] = nt(eye, halo).astype(bf16)
        me = lax.axis_index("box")
        odd = lax.rem(me, 2)
        rel = src_in()[...] - me * boxes
        below = rel + (boxes + NEARB) + (1 - odd) * NEARB
        above = rel + odd * NEARB
        rel = jnp.where(rel < 0, below, jnp.where(rel >= boxes, above, rel))
        off = jnp.where(iota((slots, boxes), 0) < cnt_in()[...], off_in()[...], -1)
        for m in range(0, slots, pair):
            src = jnp.concatenate([rel[m + j : m + j + 1] for j in range(pair)], axis=1)
            ops = jnp.concatenate([off[m + j : m + j + 1] for j in range(pair)], axis=1)
            hot = ones_where(iota((depth, pair * boxes), 0) == src)
            pick = ones_where(iota((operators, pair * boxes), 0) == ops)
            picked = nn(ext_ref[...], hot)
            coef = nn(tt_ref[...], pick)
            pr, pi, cr, ci = picked[:kcg], picked[kcg:], coef[:kcg], coef[kcg:]
            real, imag = cr * pr - ci * pi, cr * pi + ci * pr
            for r, value in enumerate((real, imag)):
                value = sum(value[:, j * boxes : (j + 1) * boxes] for j in range(pair))
                out_ref[r] = value if m == 0 else out_ref[r] + value

    return call(
        body,
        [own, lead, trail, sources, offsets, counts, table, phase],
        [H] * 8,
        [(own.shape, f32, V), ((2 * OCTANTS, kpg), f32, V)],
        "near_sums",
        scratch=[
            pltpu.VMEM((2 * kcg, depth), bf16),
            pltpu.VMEM((2 * kcg, operators), bf16),
            pltpu.VMEM((OCTANTS, kpg), f32),
        ],
        flops=2 * slots * boxes * 2 * kcg * (depth + operators),
        limit=24 << 20,
    )


def plain_translate(pattern, table, sources, offsets, counts):
    coef = jnp.transpose(table, (0, 2, 1))

    def advance(m, summed):
        src = lax.dynamic_index_in_dim(sources, m, 0, keepdims=False)
        off = lax.dynamic_index_in_dim(offsets, m, 0, keepdims=False)
        p = pattern[:, :, src].astype(f32)
        c = coef[:, :, off].astype(f32) * (m < counts).astype(f32)
        return summed + jnp.stack([c[0] * p[0] - c[1] * p[1], c[0] * p[1] + c[1] * p[0]])

    return lax.fori_loop(
        0, sources.shape[0], advance, jnp.zeros(pattern.shape[:2] + (sources.shape[1],), f32)
    )


def ring(peers):
    gray = [i ^ (i >> 1) for i in range(peers)]
    if sorted(gray) != list(range(peers)):
        return list(range(peers))
    middle = gray.index((peers // 2 + 1) % peers)
    return gray[middle:] + gray[:middle]


def regroup(value, order):
    return lax.all_to_all(
        value, "box", split_axis=0, concat_axis=0, tiled=True, axis_index_groups=[list(order)]
    )


def shift(value, axis, step):
    peers = lax.axis_size(axis)
    return lax.ppermute(value, axis, [(i, (i + step) % peers) for i in range(peers)])


def exchange(value, axis, first):
    peers = lax.axis_size(axis)
    pairs = [(i, i + 1) for i in range(first, peers - 1, 2)]
    return lax.ppermute(value, axis, pairs + [(j, i) for i, j in pairs])


def local(
    child_pattern,
    child_parent,
    child_octant,
    child_sources,
    child_offsets,
    child_counts,
    parent_sources,
    parent_offsets,
    parent_counts,
    interp_weights,
    shift_phase,
    child_table,
    parent_table,
):
    own = child_pattern[:, 0]
    _, kcg, boxes = own.shape
    rim = (interp_weights.shape[0] - kcg) // 2
    peers, groups = lax.axis_size("box"), lax.axis_size("samp")
    total = parent_sources.shape[0]
    parents = total // peers
    kpg = interp_weights.shape[1]
    mine = kpg // peers
    packed = mine == LANES and total % CHUNK == 0
    order, back = (ring(peers), ring(peers)) if packed else (None, None)
    parent, octant = child_parent[None, :], child_octant[None, :]

    if groups == 2:
        rims = [shift(own, "samp", 1)]
        spans = ((0, kcg - rim, kcg), (0, 0, rim))
    else:
        rims = [shift(own[:, kcg - rim :], "samp", 1), shift(own[:, :rim], "samp", -1)]
        spans = ((0, 0, rim), (1, 0, rim))
    cosine, sine, inner, family, weights, lead, trail = prepare(
        own, octant, parent, shift_phase, interp_weights, parents
    )
    pattern = rise(rims, spans, family, cosine, sine, inner, weights, parents, order)
    lead, trail = exchange(lead, "box", 0), exchange(trail, "box", 1)

    table = parent_table[:, :, 0, :]
    if packed:
        regrouped = regroup(pattern, order)
        coef, sources = operators_of_lists(
            parent_sources.T, parent_offsets.T, parent_counts[None, :], jnp.swapaxes(table, 0, 1), order, back
        )
        far = parent_sums(regrouped, sources, coef, parent_sources.shape[1])
        far, lead, trail = lax.optimization_barrier((far, lead, trail))
        returned = regroup(far, back)
    else:
        regrouped = lax.all_to_all(pattern, "box", split_axis=2, concat_axis=1, tiled=True)
        far = plain_translate(
            jnp.transpose(regrouped, (0, 2, 1)), table, parent_sources.T, parent_offsets.T, parent_counts
        ).astype(bf16)
        far = jnp.transpose(far, (0, 2, 1))
        returned = lax.all_to_all(far, "box", split_axis=1, concat_axis=2, tiled=True)

    nearby, phases = near_sums(
        own,
        lead,
        trail,
        child_sources.T,
        child_offsets.T,
        child_counts[None, :],
        jnp.swapaxes(child_table[:, :, 0, :], 0, 1),
        shift_phase,
    )
    returned, nearby = lax.optimization_barrier((returned, nearby))
    lowered, terms = lower(returned, parent, octant, phases, interp_weights, parents, rim, back)
    if groups == 2:
        got = shift(terms, "samp", 1)
        start_terms, end_terms = (got, 1), (got, 0)
    else:
        start_terms = (shift(terms[1], "samp", 1), None)
        end_terms = (shift(terms[0], "samp", -1), None)
    partial = anterpolate(interp_weights, lowered, nearby, rim)
    return finish(partial, start_terms, end_terms)[:, None]


def solution(mesh):
    return jax.shard_map(
        local,
        mesh=mesh,
        in_specs=(
            P(None, "samp", None, "box"),
            P("box"),
            P("box"),
            P("box", None),
            P("box", None),
            P("box"),
            P(),
            P(),
            P(),
            P(),
            P(None, "samp", None),
            P(None, None, "samp", None),
            P(None, None, "samp", "box"),
        ),
        out_specs=P(None, "samp", None, "box"),
        check_vma=False,
    )
```
